32 devices in a mesh: grp: 2 (over y), row: 16 (over z, x, core), col: 1.
Axes of the slice: x: 2, y: 2, z: 4, core: 2. Of those that a mesh axis runs over, the one named last changes fastest.
Arguments:
- alignment_state: bfloat16 [64, 128, 64], P(('grp', 'row'), 'col'), parts along dimension 0, may hold values from -6 to 6
- pair_state: bfloat16 [256, 128, 128], P(('grp', 'row'), 'col'), parts along dimension 0, may hold values from -6 to 6
- cotangent: bfloat16 [256, 128, 128], P(('grp', 'row'), 'col'), parts along dimension 0, may hold values from -0.046875 to 0.046875
- sequence_row_mask: int32 [64], P('grp'), parts along dimension 0, may hold values 0 or 1
- residue_mask: int32 [256], P('grp'), parts along dimension 0, may hold values 0 or 1
- norm_gain_vector: float32 [64], replicated, may hold values from 0.1 to 1.9
- left_matrix_weight: bfloat16 [64, 32], replicated, may hold values from -3 to 3
- right_matrix_weight: bfloat16 [64, 32], replicated, may hold values from -3 to 3
- output_weight: bfloat16 [1024, 128], replicated, may hold values from -0.1875 to 0.1875
- output_bias: float32 [128], replicated, may hold values from -4 to 4
- gate_matrix: bfloat16 [128, 128], replicated, may hold values from -0.5 to 0.5
Outputs:
- pair_update: bfloat16 [256, 128, 128], P(('grp', 'row'), 'col'), parts along dimension 0
- grad_left: float32 [128, 32], P('grp'), parts along dimension 0
- grad_right: float32 [128, 32], P('grp'), parts along dimension 0
- grad_out: float32 [2048, 128], P('grp'), parts along dimension 0
- grad_gate: float32 [256, 128], P('grp'), parts along dimension 0
The draws below stay inside these ranges and needn't reach their ends.
There are 2 independent parts, one for each index of `grp`. The reference program is written for one: setup_inputs(seed, part) draws one part's arguments, and reference() takes and returns one part's arrays. A program takes and returns all parts, laid end to end along the dimension named above; an argument that names none is the same for every part. Nothing has to cross between parts.
All inputs are finite; a program needn't handle non-finite values.
Results may differ from the reference program's by a relative error of at most 0.0076.
Values may be sent and summed in bfloat16 or wider, within the bound.
No kernel may reach another device: no remote copies, remote signals or barrier semaphores. Data moves between devices by JAX's collectives and lax.ppermute only.
A program may use at most 64 MiB of HBM per device.

```python
import jax
import jax.numpy as jnp
from jax import lax

ALIGN_CHANNELS = 64
PROJECT_WIDTH = 32
PAIR_CH = 128
ALIGN_ROWS = 32
CROP_RESIDUES = 128


def place_ends(array, own_key, smallest, largest):
    longest = array.shape.index(max(array.shape))
    spots = []
    for shift in (0, 1):
        where = [jax.random.randint(jax.random.fold_in(own_key, axis), (), 0, length) for axis, length in enumerate(array.shape)]
        where[longest] = (where[longest] + shift) % array.shape[longest]
        spots.append(tuple(where))
    return array.at[spots[0]].set(smallest).at[spots[1]].set(largest)


def block_scale(rng, extent, cuts, low, high):
    def one(axis_at, blocks):
        steps = jax.random.uniform(jax.random.fold_in(jax.random.fold_in(rng, 6), axis_at), (blocks,), jnp.float32, low / len(cuts), high / len(cuts))
        return jnp.repeat(jnp.exp(steps), extent[axis_at] // blocks).reshape((-1,) + (1,) * (len(extent) - axis_at - 1))

    loudness = one(*cuts[0])
    for cut in cuts[1:]:
        loudness = loudness * one(*cut)
    return loudness


def scatter_about(own_key, shape, spread, bound, cuts=(), kind=jnp.bfloat16):
    values = jax.random.normal(own_key, shape, jnp.float32) * spread
    if len(cuts) > 0:
        values = block_scale(own_key, shape, cuts, -0.22, 0.18) * values
    return jnp.clip(values, min=-bound, max=bound).astype(kind)


def setup_inputs(seed: int = 0, part: int = 0) -> dict:
    seeds = jax.random.split(jax.random.key(seed), 12)
    part_keys = jax.random.split(jax.random.fold_in(seeds[11], part), 12)
    alignment_state = scatter_about(part_keys[0], (ALIGN_ROWS, CROP_RESIDUES, ALIGN_CHANNELS), 1.0, 6.0, ((0, 16),))
    pair_state = scatter_about(part_keys[1], (CROP_RESIDUES, CROP_RESIDUES, PAIR_CH), 1.0, 6.0, ((0, 16),))
    cotangent = scatter_about(part_keys[2], (CROP_RESIDUES, CROP_RESIDUES, PAIR_CH), (1.0 / CROP_RESIDUES), 0.046875, ((0, 16),))
    sequence_row_mask = place_ends((jax.random.randint(part_keys[3], (ALIGN_ROWS,), 0, 8) < 7).astype(jnp.int32), jax.random.fold_in(part_keys[3], 1), 0, 1)
    residue_mask = place_ends((jax.random.randint(part_keys[4], (CROP_RESIDUES,), 0, 16) < 15).astype(jnp.int32), jax.random.fold_in(part_keys[4], 1), 0, 1)
    norm_gain_vector = jnp.clip(1.0 + 0.18 * jax.random.normal(seeds[5], (ALIGN_CHANNELS,), jnp.float32), 0.1, 1.9)
    left_matrix_weight = scatter_about(seeds[6], (ALIGN_CHANNELS, PROJECT_WIDTH), 0.5, 3.0)
    right_matrix_weight = scatter_about(seeds[7], (ALIGN_CHANNELS, PROJECT_WIDTH), 0.5, 3.0)
    output_weight = scatter_about(seeds[8], (PROJECT_WIDTH * PROJECT_WIDTH, PAIR_CH), (PROJECT_WIDTH * PROJECT_WIDTH) ** -0.5, 0.1875)
    output_bias = scatter_about(seeds[9], (PAIR_CH,), 1.0, 4.0, (), jnp.float32)
    gate_matrix = scatter_about(seeds[10], (PAIR_CH, PAIR_CH), PAIR_CH ** -0.5, 0.5)
    return dict(alignment_state=alignment_state, pair_state=pair_state, cotangent=cotangent, sequence_row_mask=sequence_row_mask, residue_mask=residue_mask, norm_gain_vector=norm_gain_vector, left_matrix_weight=left_matrix_weight, right_matrix_weight=right_matrix_weight, output_weight=output_weight, output_bias=output_bias, gate_matrix=gate_matrix)


def layer_normalize(alignment_state, norm_gain_vector):
    value_entries = alignment_state.astype(jnp.float32)
    average = lax.optimization_barrier(jnp.mean(value_entries, axis=-1, keepdims=True))
    centred = value_entries - average
    variance = lax.optimization_barrier(jnp.mean(centred * centred, axis=-1, keepdims=True))
    return (centred * lax.rsqrt(variance + 1e-05) * norm_gain_vector).astype(jnp.bfloat16)

def reference(alignment_state, pair_state, cotangent, sequence_row_mask, residue_mask, norm_gain_vector, left_matrix_weight, right_matrix_weight, output_weight, output_bias, gate_matrix):
    feature_values = layer_normalize(alignment_state, norm_gain_vector)
    seq_flags = sequence_row_mask.astype(jnp.float32)
    res_flags = residue_mask.astype(jnp.float32)
    both_mask = seq_flags[:, None] * res_flags[None, :]
    flattened_features = feature_values.reshape(ALIGN_ROWS * CROP_RESIDUES, ALIGN_CHANNELS)
    left_proj = (jnp.dot(flattened_features, left_matrix_weight, preferred_element_type=jnp.float32).reshape(ALIGN_ROWS, CROP_RESIDUES, PROJECT_WIDTH) * both_mask[:, :, None]).astype(jnp.bfloat16)
    right_proj = (jnp.dot(flattened_features, right_matrix_weight, preferred_element_type=jnp.float32).reshape(ALIGN_ROWS, CROP_RESIDUES, PROJECT_WIDTH) * both_mask[:, :, None]).astype(jnp.bfloat16)
    left_rows = left_proj.transpose(1, 2, 0)
    right_flat = right_proj.reshape(ALIGN_ROWS, CROP_RESIDUES * PROJECT_WIDTH)
    row_total = jnp.sum(seq_flags)
    row_block = 32 if CROP_RESIDUES % 32 == 0 else CROP_RESIDUES
    n_blocks = CROP_RESIDUES // row_block
    contract_first = (((0,), (0,)), ((), ()))
    contract_second = (((1,), (1,)), ((), ()))

    def one_block(carry, block_idx):
        grad_out, grad_gate, grad_right_acc = carry
        first_row = block_idx * row_block
        left_blk = lax.dynamic_slice_in_dim(left_rows, first_row, row_block, 0).reshape(row_block * PROJECT_WIDTH, ALIGN_ROWS)
        outer_prod = jnp.dot(left_blk, right_flat, preferred_element_type=jnp.float32)
        outer_prod = outer_prod.reshape(row_block, PROJECT_WIDTH, CROP_RESIDUES, PROJECT_WIDTH).transpose(0, 2, 1, 3)
        outer_prod = outer_prod.reshape(row_block * CROP_RESIDUES, PROJECT_WIDTH * PROJECT_WIDTH).astype(jnp.bfloat16)
        linear = jnp.dot(outer_prod, output_weight, preferred_element_type=jnp.float32) + output_bias
        pair_blk = lax.dynamic_slice_in_dim(pair_state, first_row, row_block, 0).reshape(row_block * CROP_RESIDUES, PAIR_CH)
        gate_val = jax.nn.sigmoid(jnp.dot(pair_blk, gate_matrix, preferred_element_type=jnp.float32))
        blk_flags = lax.dynamic_slice_in_dim(res_flags, first_row, row_block, 0)
        divisor = jnp.maximum(row_total * blk_flags[:, None] * res_flags[None, :], 1.0).reshape(row_block * CROP_RESIDUES, 1)
        cot_blk = lax.dynamic_slice_in_dim(cotangent, first_row, row_block, 0).reshape(row_block * CROP_RESIDUES, PAIR_CH).astype(jnp.float32)
        new_pair = (gate_val * linear / divisor).astype(jnp.bfloat16)
        grad_lin = (cot_blk * gate_val / divisor).astype(jnp.bfloat16)
        grad_pre = (cot_blk * linear / divisor * gate_val * (1.0 - gate_val)).astype(jnp.bfloat16)
        grad_out = grad_out + lax.dot_general(outer_prod, grad_lin, contract_first, preferred_element_type=jnp.float32)
        grad_gate = grad_gate + lax.dot_general(pair_blk, grad_pre, contract_first, preferred_element_type=jnp.float32)
        grad_outer = lax.dot_general(grad_lin, output_weight, contract_second, preferred_element_type=jnp.float32).astype(jnp.bfloat16)
        outer_turned = grad_outer.reshape(row_block, CROP_RESIDUES, PROJECT_WIDTH, PROJECT_WIDTH).transpose(0, 2, 1, 3).reshape(row_block * PROJECT_WIDTH, CROP_RESIDUES * PROJECT_WIDTH)
        left_part = lax.dot_general(outer_turned, right_flat, contract_second, preferred_element_type=jnp.float32)
        grad_right_acc = grad_right_acc + lax.dot_general(left_blk, outer_turned, contract_first, preferred_element_type=jnp.float32)
        return ((grad_out, grad_gate, grad_right_acc), (new_pair.reshape(row_block, CROP_RESIDUES, PAIR_CH), left_part))
    start_carry = (jnp.zeros((PROJECT_WIDTH * PROJECT_WIDTH, PAIR_CH), jnp.float32), jnp.zeros((PAIR_CH, PAIR_CH), jnp.float32), jnp.zeros((ALIGN_ROWS, CROP_RESIDUES * PROJECT_WIDTH), jnp.float32))
    final_carry, stacked = lax.scan(one_block, start_carry, jnp.arange(n_blocks, dtype=jnp.int32))
    grad_out, grad_gate, grad_right_acc = final_carry
    pair_blocks, left_blocks = stacked
    pair_update = pair_blocks.reshape(CROP_RESIDUES, CROP_RESIDUES, PAIR_CH)
    grad_left_act = left_blocks.reshape(CROP_RESIDUES, PROJECT_WIDTH, ALIGN_ROWS).transpose(2, 0, 1) * both_mask[:, :, None]
    grad_right_act = grad_right_acc.reshape(ALIGN_ROWS, CROP_RESIDUES, PROJECT_WIDTH) * both_mask[:, :, None]
    feats_wide = flattened_features.astype(jnp.float32)
    grad_left = jnp.dot(feats_wide.T, grad_left_act.reshape(ALIGN_ROWS * CROP_RESIDUES, PROJECT_WIDTH), precision=lax.Precision.HIGHEST)
    grad_right = jnp.dot(feats_wide.T, grad_right_act.reshape(ALIGN_ROWS * CROP_RESIDUES, PROJECT_WIDTH), precision=lax.Precision.HIGHEST)
    return (pair_update, grad_left, grad_right, grad_out, grad_gate)
```

```python
import functools

import jax
import jax.numpy as jnp
from jax import lax
from jax.experimental import pallas as pl
from jax.experimental.pallas import tpu as pltpu
from jax.sharding import PartitionSpec as P

F32 = jnp.float32
BF16 = jnp.bfloat16
VMEM = pl.BlockSpec(memory_space=pltpu.VMEM)
SMEM = pl.BlockSpec(memory_space=pltpu.SMEM)
LHS_T = (((0,), (0,)), ((), ()))
RHS_T = (((1,), (1,)), ((), ()))
QUAD = 4
CHANS = 32
GROUP = 16


def iota(shape, dim):
    return lax.broadcasted_iota(jnp.int32, shape, dim)


def dot(a, b, dims=(((1,), (0,)), ((), ())), **kw):
    return lax.dot_general(a, b, dims, preferred_element_type=F32, **kw)


def norm_kernel(seq_ref, state_ref, res_ref, gain_ref, out_ref):
    first = lax.axis_index("row") * 2
    res = res_ref[...].astype(F32)
    halves = []
    for s in range(2):
        value = state_ref[s].astype(F32)
        centred = value - jnp.mean(value, axis=0, keepdims=True)
        variance = jnp.mean(centred * centred, axis=0, keepdims=True)
        seq = seq_ref[first + s].astype(F32)
        halves.append(centred * (lax.rsqrt(variance + 1e-05) * (res * seq)))
    turned = jnp.concatenate(halves, axis=0).T
    gain = gain_ref[...]
    out_ref[...] = (turned * jnp.concatenate([gain, gain], axis=1)).astype(BF16)


def gate_kernel(
    res_s_ref, seq_ref, res_ref, pair_ref, cot_ref, gate_ref,
    scale_ref, slope_ref, full_ref, own_ref, core_ref, across_ref, both_ref,
):
    row = lax.axis_index("row")
    quad_at = lax.rem(row, QUAD)
    rows = pair_ref.shape[0]
    n = res_ref.shape[1]
    total = jnp.sum(seq_ref[...].astype(F32), axis=1, keepdims=True)
    eye = iota((n, n), 0) == iota((n, n), 1)
    res_col = jnp.sum(jnp.where(eye, res_ref[...].astype(F32), 0.0), axis=1, keepdims=True)
    wide = QUAD * n
    src = iota((wide, wide), 0)
    dst = iota((wide, wide), 1)
    slot = dst // n
    chan = (quad_at ^ slot) * CHANS + dst % CHANS
    place = jnp.where(
        (src // n == (dst % n) // CHANS) & (src % n == chan), 1.0, 0.0
    ).astype(BF16)
    outs = (own_ref, core_ref, across_ref, both_ref)
    for half in range(rows // QUAD):
        for k in range(QUAD):
            i = half * QUAD + k
            gate = jax.nn.sigmoid(dot(pair_ref[i], gate_ref[...]))
            res_row = res_s_ref[row * rows + i].astype(F32)
            scale = gate / jnp.maximum(total * res_row * res_col, 1.0)
            lin = cot_ref[i].astype(F32) * scale
            scale_ref[i] = scale
            slope_ref[i] = lin * (1.0 - gate)
            full_ref[:, i * n : (i + 1) * n] = lin.astype(BF16)
        packed = dot(full_ref[:, half * wide : (half + 1) * wide], place).astype(BF16)
        for m in range(QUAD):
            outs[m][:, half * n : (half + 1) * n] = packed[:, m * n : (m + 1) * n]


def weight_kernel(
    right_ref, left_ref, out_w_ref,
    kron_ref, block_ref, wide_ref, part_ref, wf_ref,
):
    quad_at = lax.rem(lax.axis_index("row"), QUAD)
    width, chans = right_ref.shape
    n = out_w_ref.shape[1]
    cols = width * GROUP
    spread = jnp.where(iota((width, cols), 0) == iota((width, cols), 1) // GROUP, 1.0, 0.0)
    repeated = dot(right_ref[...], spread.astype(BF16), LHS_T)
    lane = iota((chans, cols), 1) % GROUP
    for s in range(GROUP):
        kron_ref[s * chans : (s + 1) * chans, :] = jnp.where(lane == s, repeated, 0.0).astype(BF16)
    spread = jnp.where(iota((width, n), 0) == iota((width, n), 1) % width, 1.0, 0.0)
    repeated = dot(left_ref[...], spread.astype(BF16), LHS_T)
    lane = iota((chans, n), 1) // width
    for k in range(QUAD):
        block_ref[k * chans : (k + 1) * chans, :] = jnp.where(lane == k, repeated, 0.0).astype(BF16)
    wf_ref[...] = out_w_ref[...].astype(F32)
    for e in range(width):
        wide_ref[:, e * n : (e + 1) * n] = wf_ref[pl.ds(e, width, stride=width), :].astype(BF16)
    pick = jnp.where(
        iota((n, n), 0) == quad_at * CHANS + iota((n, n), 1) % CHANS, 1.0, 0.0
    ).astype(BF16)
    wf_ref[...] = dot(out_w_ref[...], pick)
    lane = iota((width, n), 1) // CHANS
    for e in range(width):
        tile = wf_ref[pl.ds(e, width, stride=width), :]
        part_ref[:, e * n : (e + 1) * n] = jnp.concatenate(
            [jnp.where(lane == k, tile, 0.0) for k in range(QUAD)], axis=0
        ).astype(BF16)


def main_kernel(
    y0_ref, y1_ref, y2_ref, y3_ref, g0_ref, g1_ref, g2_ref, g3_ref,
    full_ref, scale_ref, slope_ref, pair_ref, bias_ref,
    kron_ref, block_ref, wide_ref, part_ref,
    update_ref, sums_ref,
    r_ref, m_ref, n_ref, turn_ref, own_ref, slope_s_ref,
):
    row = lax.axis_index("row")
    quad_at = lax.rem(row, QUAD)
    first = (row - quad_at) * 8
    rows, n, _ = pair_ref.shape
    chans = 64
    width = 32
    cols = width * GROUP
    seqs = 2 * GROUP
    ys = (y0_ref, y1_ref, y2_ref, y3_ref)
    slots = [y[t * n : (t + 1) * n, :] for y in ys for t in range(4)]
    feats = [jnp.concatenate(slots[g * 8 : (g + 1) * 8], axis=1) for g in range(2)]
    for g in range(2):
        r_ref[:, g * cols : (g + 1) * cols] = dot(feats[g], kron_ref[...]).astype(BF16)
    at = iota((32, n), 0)
    four = at % 8
    here = first + (quad_at ^ (four // 2)) * 8 + (four % 2) * QUAD + at // 8
    pick = jnp.where(iota((32, n), 1) == here, 1.0, 0.0).astype(BF16)
    for t, slot in enumerate(slots):
        picked = dot(pick, slot)
        for s in range(2):
            at = (2 * t + s) * 8
            for half in range(2):
                turn_ref[half, at : at + 8, :] = jnp.concatenate(
                    [
                        picked[k * 8 : (k + 1) * 8, s * chans : (s + 1) * chans]
                        for k in (2 * half, 2 * half + 1)
                    ],
                    axis=1,
                )
    for f in range(8):
        for half in range(2):
            own_ref[f * seqs : (f + 1) * seqs, half * n : (half + 1) * n] = turn_ref[
                half, pl.ds(f, seqs, stride=8), :
            ].astype(BF16)
    left = dot(own_ref[...], block_ref[...])
    left_b = left.astype(BF16)
    mine = jnp.concatenate(
        [
            left[f * seqs : (f + 1) * seqs, k * width : (k + 1) * width]
            for f in range(2)
            for k in range(QUAD)
        ],
        axis=0,
    ).astype(BF16)
    for e4 in range(width // 4):
        part = dot(mine, wide_ref[:, e4 * 4 * n : (e4 + 1) * 4 * n]).astype(BF16)
        for el in range(4):
            e = e4 * 4 + el
            for i in range(rows):
                for g in range(2):
                    m_ref[g * cols + e * GROUP : g * cols + (e + 1) * GROUP, i * n : (i + 1) * n] = (
                        part[i * seqs + g * GROUP : i * seqs + (g + 1) * GROUP, el * n : (el + 1) * n]
                    )
    for f2, g_ref in enumerate((g0_ref, g1_ref, g2_ref, g3_ref)):
        part = dot(r_ref[...], g_ref[...], LHS_T).astype(BF16)
        for fl in range(2):
            f = f2 * 2 + fl
            for g in range(2):
                for e in range(width):
                    n_ref[f * seqs + g * GROUP : f * seqs + (g + 1) * GROUP, e * n : (e + 1) * n] = (
                        part[g * cols + e * GROUP : g * cols + (e + 1) * GROUP, fl * n : (fl + 1) * n]
                    )
    lane = iota((width, n), 1) // CHANS
    for h in range(width // 4):
        whole = dot(left_b, n_ref[:, h * 4 * n : (h + 1) * 4 * n], LHS_T)
        packed = None
        for el in range(4):
            tile = None
            for k in range(QUAD):
                block = whole[k * width : (k + 1) * width, el * n : (el + 1) * n]
                tile = block if tile is None else jnp.where(lane == k, block, tile)
            tile = tile + pltpu.roll(tile, 2 * CHANS, 1)
            tile = tile + pltpu.roll(tile, CHANS, 1)
            packed = tile if packed is None else jnp.where(lane == el, tile, packed)
        sums_ref[h * width : (h + 1) * width, :] = packed.astype(BF16)
    linear = dot(r_ref[...], m_ref[...])
    for i in range(rows):
        value = linear[:, i * n : (i + 1) * n] + bias_ref[...]
        update_ref[i] = (scale_ref[i] * value).astype(BF16)
        slope_s_ref[i * n : (i + 1) * n, :] = (slope_ref[i] * value).astype(BF16)
    grad_gate = dot(pair_ref[...].reshape(rows * n, n), slope_s_ref[...], LHS_T)
    sums_ref[256:384, :] = grad_gate.astype(BF16)
    left_act = dot(n_ref[...], part_ref[...], RHS_T).astype(BF16)
    whole = dot(left_act, own_ref[...], LHS_T)
    grad_left = whole[0:width, 0:chans]
    for k in range(1, QUAD):
        grad_left = grad_left + whole[k * width : (k + 1) * width, k * chans : (k + 1) * chans]
    right_act = dot(full_ref[...], m_ref[...], RHS_T).astype(BF16)
    whole = dot(feats[0], right_act[:, :cols], LHS_T) + dot(feats[1], right_act[:, cols:], LHS_T)
    lane = iota((chans, cols), 1) % GROUP
    tile = whole[0:chans, :]
    for s in range(1, GROUP):
        tile = jnp.where(lane == s, whole[s * chans : (s + 1) * chans, :], tile)
    spread = jnp.where(iota((width, cols), 0) == iota((width, cols), 1) // GROUP, 1.0, 0.0)
    grad_right = dot(spread, tile, RHS_T, precision=lax.Precision.HIGHEST)
    sums_ref[384:416, :] = jnp.concatenate([grad_left, grad_right], axis=1).astype(BF16)


def last_kernel(t0_ref, t1_ref, t2_ref, t3_ref, out_ref, gate_ref, left_ref, right_ref):
    quad_at = lax.rem(lax.axis_index("row"), QUAD)
    n = t0_ref.shape[1]
    ts = (t0_ref, t1_ref, t2_ref, t3_ref)
    wide = QUAD * n
    src = iota((wide, wide), 0)
    dst = iota((wide, wide), 1)
    chan = (quad_at ^ (src // n)) * CHANS + src % CHANS
    place = jnp.where(
        (dst // n == (src % n) // CHANS) & (dst % n == chan), 1.0, 0.0
    ).astype(BF16)
    packed = jnp.concatenate([t[0:256, :] for t in ts], axis=1)
    whole = dot(packed, place)
    for h in range(8):
        for el in range(4):
            out_ref[pl.ds(h * 4 + el, 32, stride=32), :] = whole[
                h * 32 : (h + 1) * 32, el * n : (el + 1) * n
            ]

    def total(lo, hi):
        a, b, c, d = (t[lo:hi, :].astype(F32) for t in ts)
        return (a + b) + (c + d)

    gate_ref[...] = total(256, 384)
    both = total(384, 416)
    left_ref[...] = both[:, 0:64]
    right_ref[...] = both[:, 64:128]


def call(kernel, shapes, scratch=(), smem=0, ins=0, flops=1 << 20):
    return pl.pallas_call(
        kernel,
        out_shape=[jax.ShapeDtypeStruct(s, d) for s, d in shapes],
        in_specs=[SMEM] * smem + [VMEM] * (ins - smem),
        out_specs=[VMEM] * len(shapes),
        scratch_shapes=[pltpu.VMEM(s, d) for s, d in scratch],
        compiler_params=pltpu.CompilerParams(vmem_limit_bytes=48 << 20),
        cost_estimate=pl.CostEstimate(flops=flops, bytes_accessed=1 << 20, transcendentals=0),
    )


def swap(x, bit, size):
    return lax.ppermute(x, "row", [(i, i ^ bit) for i in range(size)])


def one_column(
    alignment_state, pair_state, cotangent, sequence_row_mask, residue_mask, norm_gain_vector,
    left_matrix_weight, right_matrix_weight, output_weight, output_bias, gate_matrix,
):
    size = lax.axis_size("row")
    rows, n, _ = pair_state.shape
    res = residue_mask.reshape(1, n)
    seq = sequence_row_mask.reshape(1, -1)
    (feat,) = call(norm_kernel, [((n, n), BF16)], smem=1, ins=4)(
        sequence_row_mask, alignment_state.transpose(0, 2, 1), res, norm_gain_vector.reshape(1, -1)
    )
    near = swap(feat, 4, size)
    scale, slope, full, g0, g1, g2, g3 = call(
        gate_kernel,
        [((rows, n, n), F32), ((rows, n, n), F32), ((n, rows * n), BF16)] + [((n, 2 * n), BF16)] * 4,
        smem=1, ins=6, flops=300 << 20,
    )(residue_mask, seq, res, pair_state, cotangent, gate_matrix)
    g1 = swap(g1, 1, size)
    g2 = swap(g2, 2, size)
    g3 = swap(g3, 3, size)
    kron, block, wide, part = call(
        weight_kernel,
        [((1024, 512), BF16), ((256, n), BF16), ((32, 32 * n), BF16), ((n, 32 * n), BF16)],
        scratch=[((1024, n), F32)], ins=3, flops=300 << 20,
    )(right_matrix_weight.T, left_matrix_weight.T, output_weight)
    y0 = jnp.concatenate([feat, near], axis=0)
    y0 = jnp.concatenate([y0, swap(y0, 8, size)], axis=0)
    y1 = swap(y0, 2, size)
    y2 = swap(y0, 1, size)
    y3 = swap(y1, 1, size)
    update, sums = call(
        main_kernel,
        [((rows, n, n), BF16), ((416, n), BF16)],
        scratch=[
            ((n, 1024), BF16), ((1024, rows * n), BF16), ((256, 32 * n), BF16),
            ((2, 256, n), F32), ((256, 256), BF16), ((rows * n, n), BF16),
        ],
        ins=17, flops=2000 << 20,
    )(
        y0, y1, y2, y3, g0, g1, g2, g3, full, scale, slope, pair_state,
        output_bias.reshape(1, n), kron, block, wide, part,
    )
    sums = sums + swap(sums, 4, size)
    sums = sums + swap(sums, 8, size)
    across = swap(sums, 2, size)
    core = swap(sums, 1, size)
    both = swap(across, 1, size)
    grad_out, grad_gate, left, right = call(
        last_kernel,
        [((1024, n), F32), ((n, n), F32), ((32, 64), F32), ((32, 64), F32)],
        ins=4,
    )(sums, core, across, both)
    return update, left.T, right.T, grad_out, grad_gate


def layer_normalize(alignment_state, norm_gain_vector):
    value_entries = alignment_state.astype(jnp.float32)
    average = jnp.mean(value_entries, axis=-1, keepdims=True)
    centred = value_entries - average
    variance = jnp.mean(centred * centred, axis=-1, keepdims=True)
    return (centred * lax.rsqrt(variance + 1e-05) * norm_gain_vector).astype(jnp.bfloat16)


def any_mesh(
    alignment_state,
    pair_state,
    cotangent,
    sequence_row_mask,
    residue_mask,
    norm_gain_vector,
    left_matrix_weight,
    right_matrix_weight,
    output_weight,
    output_bias,
    gate_matrix,
):
    sequence_resident, column_count, alignment_channel_count = alignment_state.shape
    count_of_rows = pair_state.shape[0]
    pair_chans = pair_state.shape[2]
    projection_width = left_matrix_weight.shape[1]
    every_sequence = sequence_row_mask.shape[0]
    row_at = lax.axis_index("row")
    col_at = lax.axis_index("col")
    number_of_rows = lax.axis_size("row")
    contract_first = (((0,), (0,)), ((), ()))
    contract_second = (((1,), (1,)), ((), ()))
    resident_features = layer_normalize(alignment_state, norm_gain_vector)
    seq_flags = sequence_row_mask.astype(jnp.float32)
    res_flags = residue_mask.astype(jnp.float32)
    my_cols = lax.dynamic_slice_in_dim(res_flags, col_at * column_count, column_count, 0)
    my_rows = lax.dynamic_slice_in_dim(res_flags, row_at * count_of_rows, count_of_rows, 0)
    panel_mask = seq_flags[:, None] * my_rows[None, :]
    column_mask = seq_flags[:, None] * my_cols[None, :]
    broadcast_features = lax.all_gather(
        resident_features.reshape(sequence_resident, column_count * alignment_channel_count),
        "col",
        axis=1,
        tiled=True,
    )
    row_portions = broadcast_features.reshape(
        sequence_resident, number_of_rows, count_of_rows * alignment_channel_count
    )
    row_feats = lax.all_to_all(
        row_portions, "row", split_axis=1, concat_axis=0, tiled=True
    ).reshape(every_sequence * count_of_rows, alignment_channel_count)
    left_panel = (
        jnp.dot(row_feats, left_matrix_weight, preferred_element_type=jnp.float32).reshape(
            every_sequence, count_of_rows, projection_width
        )
        * panel_mask[:, :, None]
    ).astype(jnp.bfloat16)
    left_matrix = left_panel.transpose(1, 2, 0).reshape(
        count_of_rows * projection_width, every_sequence
    )
    column_features = lax.all_gather(
        resident_features.reshape(sequence_resident, column_count * alignment_channel_count),
        "row",
        axis=0,
        tiled=True,
    ).reshape(every_sequence, column_count, alignment_channel_count)
    right_panel = (
        jnp.dot(
            column_features.reshape(every_sequence * column_count, alignment_channel_count),
            right_matrix_weight,
            preferred_element_type=jnp.float32,
        ).reshape(every_sequence, column_count, projection_width)
        * column_mask[:, :, None]
    ).astype(jnp.bfloat16)
    surplus_offset = jnp.zeros((alignment_channel_count, projection_width), jnp.float32)

    def absorb(extra, first_col, width_columns, right_part):
        feat_blk = (
            lax.dynamic_slice_in_dim(column_features, first_col, width_columns, 1)
            .reshape(every_sequence * width_columns, alignment_channel_count)
            .astype(jnp.float32)
        )
        mask_blk = lax.dynamic_slice_in_dim(column_mask, first_col, width_columns, 1)
        masked_part = (
            right_part.reshape(every_sequence, width_columns, projection_width)
            * mask_blk[:, :, None]
        ).reshape(every_sequence * width_columns, projection_width)
        return extra + jnp.dot(feat_blk.T, masked_part, precision=lax.Precision.HIGHEST)

    right_flat = right_panel.reshape(every_sequence, column_count * projection_width)
    row_total = jnp.sum(seq_flags)
    col_block = 128
    n_blocks = column_count // col_block

    def one_block(block_idx, carry):
        new_update, grad_out, grad_gate, left_acc, extra = carry
        first_col = block_idx * col_block
        right_blk = lax.dynamic_slice_in_dim(
            right_flat, first_col * projection_width, col_block * projection_width, 1
        )
        outer_prod = jnp.dot(left_matrix, right_blk, preferred_element_type=jnp.float32)
        outer_prod = outer_prod.reshape(
            count_of_rows, projection_width, col_block, projection_width
        ).transpose(0, 2, 1, 3)
        outer_prod = outer_prod.reshape(
            count_of_rows * col_block, projection_width * projection_width
        ).astype(jnp.bfloat16)
        linear = (
            jnp.dot(outer_prod, output_weight, preferred_element_type=jnp.float32) + output_bias
        )
        pair_blk = lax.dynamic_slice_in_dim(pair_state, first_col, col_block, 1).reshape(
            count_of_rows * col_block, pair_chans
        )
        gate_val = jax.nn.sigmoid(
            jnp.dot(pair_blk, gate_matrix, preferred_element_type=jnp.float32)
        )
        blk_flags = lax.dynamic_slice_in_dim(my_cols, first_col, col_block, 0)
        divisor = jnp.maximum(row_total * my_rows[:, None] * blk_flags[None, :], 1.0).reshape(
            count_of_rows * col_block, 1
        )
        cot_blk = (
            lax.dynamic_slice_in_dim(cotangent, first_col, col_block, 1)
            .reshape(count_of_rows * col_block, pair_chans)
            .astype(jnp.float32)
        )
        new_pair = (gate_val * linear / divisor).astype(jnp.bfloat16)
        new_update = lax.dynamic_update_slice_in_dim(
            new_update, new_pair.reshape(count_of_rows, col_block, pair_chans), first_col, 1
        )
        grad_lin = (cot_blk * gate_val / divisor).astype(jnp.bfloat16)
        grad_pre = (cot_blk * linear / divisor * gate_val * (1.0 - gate_val)).astype(jnp.bfloat16)
        grad_out = grad_out + lax.dot_general(
            outer_prod, grad_lin, contract_first, preferred_element_type=jnp.float32
        )
        grad_gate = grad_gate + lax.dot_general(
            pair_blk, grad_pre, contract_first, preferred_element_type=jnp.float32
        )
        grad_outer = lax.dot_general(
            grad_lin, output_weight, contract_second, preferred_element_type=jnp.float32
        ).astype(jnp.bfloat16)
        outer_turned = (
            grad_outer.reshape(count_of_rows, col_block, projection_width, projection_width)
            .transpose(0, 2, 1, 3)
            .reshape(count_of_rows * projection_width, col_block * projection_width)
        )
        left_acc = left_acc + lax.dot_general(
            outer_turned, right_blk, contract_second, preferred_element_type=jnp.float32
        )
        right_part = lax.dot_general(
            left_matrix, outer_turned, contract_first, preferred_element_type=jnp.float32
        )
        extra = absorb(extra, first_col, col_block, right_part)
        return (new_update, grad_out, grad_gate, left_acc, extra)

    start_carry = (
        jnp.zeros((count_of_rows, column_count, pair_chans), jnp.bfloat16),
        jnp.zeros((projection_width * projection_width, pair_chans), jnp.float32),
        jnp.zeros((pair_chans, pair_chans), jnp.float32),
        jnp.zeros((count_of_rows * projection_width, every_sequence), jnp.float32),
        surplus_offset,
    )
    new_update, grad_out, grad_gate, left_acc, extra = lax.fori_loop(
        0, n_blocks, one_block, start_carry
    )
    grad_left_act = (
        left_acc.reshape(count_of_rows, projection_width, every_sequence).transpose(2, 0, 1)
        * panel_mask[:, :, None]
    )
    grad_left = jnp.dot(
        row_feats.astype(jnp.float32).T,
        grad_left_act.reshape(every_sequence * count_of_rows, projection_width),
        precision=lax.Precision.HIGHEST,
    )
    summed_left, summed_right, summed_out, summed_gate = lax.psum(
        (grad_left, extra, grad_out, grad_gate), ("row", "col")
    )
    return (new_update, summed_left, summed_right, summed_out, summed_gate)


def per_device(*args):
    alignment_state, pair_state = args[0], args[1]
    fits = (
        lax.axis_size("col") == 1
        and lax.axis_size("row") == 16
        and alignment_state.shape == (2, 128, 64)
        and pair_state.shape == (8, 128, 128)
    )
    return one_column(*args) if fits else any_mesh(*args)


def solution(mesh):
    return jax.shard_map(
        per_device,
        mesh=mesh,
        in_specs=(
            P(("grp", "row"), "col", None),
            P(("grp", "row"), "col", None),
            P(("grp", "row"), "col", None),
            P("grp"),
            P("grp"),
            P(),
            P(),
            P(),
            P(),
            P(),
            P(),
        ),
        out_specs=(
            P(("grp", "row"), "col", None),
            P("grp", None),
            P("grp", None),
            P("grp", None),
            P("grp", None),
        ),
        check_vma=False,
    )
```

```python
import functools

import jax
import jax.numpy as jnp
from jax import lax
from jax.experimental import pallas as pl
from jax.experimental.pallas import tpu as pltpu
from jax.sharding import PartitionSpec as P

F32 = jnp.float32
BF16 = jnp.bfloat16
VMEM = pl.BlockSpec(memory_space=pltpu.VMEM)
SMEM = pl.BlockSpec(memory_space=pltpu.SMEM)
LHS_T = (((0,), (0,)), ((), ()))
RHS_T = (((1,), (1,)), ((), ()))
QUAD = 4
CHANS = 32
GROUP = 16


def iota(shape, dim):
    return lax.broadcasted_iota(jnp.int32, shape, dim)


def dot(a, b, dims=(((1,), (0,)), ((), ())), **kw):
    return lax.dot_general(a, b, dims, preferred_element_type=F32, **kw)


def first_kernel(out_ref):
    out_ref[...] = jnp.zeros_like(out_ref)


def norm_kernel(seq_ref, res_ref, gain_ref, own_ref, near_ref, out_ref):
    row = lax.axis_index("row")
    n = res_ref.shape[1]
    res = res_ref[...].astype(F32)
    gain = gain_ref[...]
    gain = jnp.concatenate([gain, gain], axis=1)
    for at, (state_ref, first) in enumerate(((own_ref, row * 2), (near_ref, (row ^ 4) * 2))):
        halves = []
        for s in range(2):
            value = state_ref[s].astype(F32)
            centred = value - jnp.mean(value, axis=0, keepdims=True)
            variance = jnp.mean(centred * centred, axis=0, keepdims=True)
            seq = seq_ref[first + s].astype(F32)
            halves.append(centred * (lax.rsqrt(variance + 1e-05) * (res * seq)))
        turned = jnp.concatenate(halves, axis=0).T
        out_ref[at * n : (at + 1) * n, :] = (turned * gain).astype(BF16)


def gate_kernel(
    res_s_ref, seq_ref, res_ref, pair_ref, cot_ref, gate_ref, gain_ref, bias_ref, after_ref,
    scale_ref, slope_ref, turned_ref, own_ref, core_ref, across_ref, both_ref, gain_out_ref, bias_out_ref,
    full_ref,
):
    gain_out_ref[...] = gain_ref[...]
    bias_out_ref[...] = bias_ref[...]
    row = lax.axis_index("row")
    quad_at = lax.rem(row, QUAD)
    rows = pair_ref.shape[0]
    n = res_ref.shape[1]
    total = jnp.sum(seq_ref[...].astype(F32), axis=1, keepdims=True)
    eye = iota((n, n), 0) == iota((n, n), 1)
    res_col = jnp.sum(jnp.where(eye, res_ref[...].astype(F32), 0.0), axis=1, keepdims=True)
    wide = QUAD * n
    src = iota((wide, wide), 0)
    dst = iota((wide, wide), 1)
    slot = dst // n
    chan = (quad_at ^ slot) * CHANS + dst % CHANS
    place = jnp.where(
        (src // n == (dst % n) // CHANS) & (src % n == chan), 1.0, 0.0
    ).astype(BF16)
    outs = (own_ref, core_ref, across_ref, both_ref)
    for half in range(rows // QUAD):
        for k in range(QUAD):
            i = half * QUAD + k
            gate = jax.nn.sigmoid(dot(pair_ref[i], gate_ref[...]))
            res_row = res_s_ref[row * rows + i].astype(F32)
            scale = gate / jnp.maximum(total * res_row * res_col, 1.0)
            lin = cot_ref[i].astype(F32) * scale
            scale_ref[i] = scale
            slope_ref[i] = lin * (1.0 - gate)
            full_ref[:, i * n : (i + 1) * n] = lin.astype(BF16)
            turned_ref[i * n : (i + 1) * n, :] = lin.T.astype(BF16)
        packed = dot(full_ref[:, half * wide : (half + 1) * wide], place).astype(BF16)
        for m in range(QUAD):
            outs[m][:, half * n : (half + 1) * n] = packed[:, m * n : (m + 1) * n]


def weight_kernel(
    right_ref, left_ref, out_w_ref, after_ref,
    kron_ref, block_ref, wide_ref, part_ref, wf_ref,
):
    quad_at = lax.rem(lax.axis_index("row"), QUAD)
    width, chans = right_ref.shape
    n = out_w_ref.shape[1]
    cols = width * GROUP
    spread = jnp.where(iota((width, cols), 0) == iota((width, cols), 1) // GROUP, 1.0, 0.0)
    repeated = dot(right_ref[...], spread.astype(BF16), LHS_T)
    lane = iota((chans, cols), 1) % GROUP
    for s in range(GROUP):
        kron_ref[s * chans : (s + 1) * chans, :] = jnp.where(lane == s, repeated, 0.0).astype(BF16)
    spread = jnp.where(iota((width, n), 0) == iota((width, n), 1) % width, 1.0, 0.0)
    repeated = dot(left_ref[...], spread.astype(BF16), LHS_T)
    lane = iota((chans, n), 1) // width
    for k in range(QUAD):
        block_ref[k * chans : (k + 1) * chans, :] = jnp.where(lane == k, repeated, 0.0).astype(BF16)
    wf_ref[...] = out_w_ref[...].astype(F32)
    for e in range(width):
        wide_ref[:, e * n : (e + 1) * n] = wf_ref[pl.ds(e, width, stride=width), :].astype(BF16)
    pick = jnp.where(
        iota((n, n), 0) == quad_at * CHANS + iota((n, n), 1) % CHANS, 1.0, 0.0
    ).astype(BF16)
    wf_ref[...] = dot(out_w_ref[...], pick)
    lane = iota((width, n), 1) // CHANS
    for h in range(width // QUAD):
        tile = None
        for k in range(QUAD):
            rows = wf_ref[pl.ds(h * QUAD + k, width, stride=width), :]
            tile = rows if tile is None else jnp.where(lane == k, rows, tile)
        part_ref[:, h * n : (h + 1) * n] = tile.astype(BF16)


def fold(tiles, lane):
    high, low = lane // 2 == 0, lane % 2 == 0
    pairs = [
        jnp.where(high, tiles[k], tiles[k + 2])
        + pltpu.roll(jnp.where(high, tiles[k + 2], tiles[k]), 2 * CHANS, 1)
        for k in range(2)
    ]
    other = jnp.where(low, pairs[1], pairs[0])
    size = lane.shape[1]
    other = jnp.where(low, pltpu.roll(other, size - CHANS, 1), pltpu.roll(other, CHANS, 1))
    return jnp.where(low, pairs[0], pairs[1]) + other


def half_of_rows(ys, gs, turned, kron_ref, block_ref, wide_ref, scratch):
    m_ref, n_ref, turn_ref, own_ref, right_ref, flat_ref = scratch
    row = lax.axis_index("row")
    quad_at = lax.rem(row, QUAD)
    first = (row - quad_at) * 8
    n = ys[0].shape[1]
    chans, width = 64, 32
    slots = [y[t * n : (t + 1) * n, :] for y in ys for t in range(4)]
    right = dot(jnp.concatenate(slots, axis=1), kron_ref[...]).astype(BF16)
    right_t = right.T
    at = iota((32, n), 0)
    four = at % 8
    here = first + (quad_at ^ (four // 2)) * 8 + (four % 2) * QUAD + at // 8
    pick = jnp.where(iota((32, n), 1) == here, 1.0, 0.0).astype(BF16)
    for t, slot in enumerate(slots):
        picked = dot(pick, slot)
        for s in range(2):
            at = (2 * t + s) * 8
            for half in range(2):
                turn_ref[half, at : at + 8, :] = jnp.concatenate(
                    [
                        picked[k * 8 : (k + 1) * 8, s * chans : (s + 1) * chans]
                        for k in (2 * half, 2 * half + 1)
                    ],
                    axis=1,
                )
    for f in range(8):
        for half in range(2):
            own_ref[f * GROUP : (f + 1) * GROUP, half * n : (half + 1) * n] = turn_ref[
                half, pl.ds(f, GROUP, stride=8), :
            ].astype(BF16)
    left = dot(own_ref[0 : 2 * GROUP, :], block_ref[...])
    mine = jnp.concatenate(
        [
            left[f * GROUP : (f + 1) * GROUP, k * width : (k + 1) * width]
            for f in range(2)
            for k in range(QUAD)
        ],
        axis=0,
    ).astype(BF16)
    for e4 in range(width // 4):
        part = dot(mine, wide_ref[:, e4 * 4 * n : (e4 + 1) * 4 * n]).astype(BF16)
        for el in range(4):
            e = e4 * 4 + el
            for i in range(8):
                m_ref[e * GROUP : (e + 1) * GROUP, i * n : (i + 1) * n] = part[
                    i * GROUP : (i + 1) * GROUP, el * n : (el + 1) * n
                ]
    for f2, g_ref in enumerate(gs):
        part = dot(right_t, g_ref[...]).astype(BF16)
        for fl in range(2):
            f = f2 * 2 + fl
            for e in range(width):
                n_ref[f * GROUP : (f + 1) * GROUP, e * n : (e + 1) * n] = part[
                    e * GROUP : (e + 1) * GROUP, fl * n : (fl + 1) * n
                ]
    linear = dot(right, m_ref[...])
    right_ref[...] = dot(m_ref[...], turned[...])
    for t in range(8):
        for s in range(2):
            flat_ref[s * width : (s + 1) * width, t * n : (t + 1) * n] = right_ref[
                pl.ds(2 * t + s, width, stride=GROUP), :
            ].astype(BF16)
    half = 4 * n
    act = dot(flat_ref[:, :half], ys[0][...]) + dot(flat_ref[:, half:], ys[1][...])
    own_t = own_ref[...].T
    lane = iota((chans, n), 1) // CHANS
    packed = []
    for h in range(width // QUAD):
        whole = dot(own_t, n_ref[:, h * 4 * n : (h + 1) * 4 * n])
        tiles = []
        for el in range(QUAD):
            tile = whole[0:chans, el * n : (el + 1) * n]
            for k in range(1, QUAD):
                tile = jnp.where(
                    lane == k, whole[k * chans : (k + 1) * chans, el * n : (el + 1) * n], tile
                )
            tiles.append(tile)
        packed.append(fold(tiles, lane))
    return linear, act, jnp.concatenate(packed, axis=1)


def half_kernel(
    y0_ref, y1_ref, g0_ref, g1_ref, g2_ref, g3_ref, turned_ref, kron_ref, block_ref, wide_ref, bias_ref,
    linear_ref, act_ref, feat_ref, *scratch
):
    linear, act, feat = half_of_rows(
        (y0_ref, y1_ref), (g0_ref, g1_ref, g2_ref, g3_ref), turned_ref, kron_ref, block_ref, wide_ref, scratch
    )
    bias = bias_ref[...]
    linear_ref[...] = linear + jnp.concatenate([bias] * 8, axis=1)
    act_ref[...] = act
    feat_ref[...] = feat


def main_kernel(
    y0_ref, y1_ref, g0_ref, g1_ref, g2_ref, g3_ref, turned_ref, kron_ref, block_ref, wide_ref,
    linear_ref, act_ref, feat_ref, scale_ref, slope_ref, pair_ref, part_ref, left_ref,
    update_ref, sums_ref,
    slope_s_ref, *scratch
):
    rows, n, _ = pair_ref.shape
    chans, width = 64, 32
    linear, act, feat = half_of_rows(
        (y0_ref, y1_ref), (g0_ref, g1_ref, g2_ref, g3_ref), turned_ref, kron_ref, block_ref, wide_ref, scratch
    )
    for i in range(rows):
        value = linear[:, i * n : (i + 1) * n] + linear_ref[:, i * n : (i + 1) * n]
        update_ref[i] = (scale_ref[i] * value).astype(BF16)
        slope_s_ref[i * n : (i + 1) * n, :] = (slope_ref[i] * value).astype(BF16)
    grad_gate = dot(pair_ref[...].reshape(rows * n, n), slope_s_ref[...], LHS_T)
    sums_ref[256:384, :] = grad_gate.astype(BF16)
    feat = feat + feat_ref[...]
    coarse = feat.astype(BF16)
    fine = (feat - coarse.astype(F32)).astype(BF16)
    grad_out = dot(left_ref[...], coarse) + dot(left_ref[...], fine)
    for h in range(width // QUAD):
        sums_ref[h * width : (h + 1) * width, :] = grad_out[:, h * n : (h + 1) * n].astype(BF16)
    grad_left = dot(part_ref[...], coarse, RHS_T) + dot(part_ref[...], fine, RHS_T)
    act = act + act_ref[...]
    grad_right = act[:width, :chans] + act[width:, chans:]
    sums_ref[384:416, :] = jnp.concatenate([grad_left, grad_right], axis=1).astype(BF16)


def last_kernel(t0_ref, t1_ref, t2_ref, t3_ref, out_ref, gate_ref, left_ref, right_ref):
    quad_at = lax.rem(lax.axis_index("row"), QUAD)
    n = t0_ref.shape[1]
    ts = (t0_ref, t1_ref, t2_ref, t3_ref)
    wide = QUAD * n
    src = iota((wide, wide), 0)
    dst = iota((wide, wide), 1)
    chan = (quad_at ^ (src // n)) * CHANS + src % CHANS
    place = jnp.where(
        (dst // n == (src % n) // CHANS) & (dst % n == chan), 1.0, 0.0
    ).astype(BF16)
    packed = jnp.concatenate([t[0:256, :] for t in ts], axis=1)
    whole = dot(packed, place)
    for h in range(8):
        for el in range(4):
            out_ref[pl.ds(h * 4 + el, 32, stride=32), :] = whole[
                h * 32 : (h + 1) * 32, el * n : (el + 1) * n
            ]

    def total(lo, hi):
        a, b, c, d = (t[lo:hi, :].astype(F32) for t in ts)
        return (a + b) + (c + d)

    gate_ref[...] = total(256, 384)
    both = total(384, 416)
    left_ref[...] = both[:, 0:64]
    right_ref[...] = both[:, 64:128]


def tie_kernel(*refs):
    out_ref, at = refs[-1], 0
    for ref in refs:
        if at < out_ref.shape[0]:
            out_ref[at : at + ref.shape[0], :] = ref[...]
            at += ref.shape[0]


def call(kernel, shapes, scratch=(), smem=0, ins=0, flops=1 << 20, vmem=4):
    return pl.pallas_call(
        kernel,
        out_shape=[jax.ShapeDtypeStruct(s, d) for s, d in shapes],
        in_specs=[SMEM] * smem + [VMEM] * (ins - smem),
        out_specs=[VMEM] * len(shapes),
        scratch_shapes=[pltpu.VMEM(s, d) for s, d in scratch],
        compiler_params=pltpu.CompilerParams(vmem_limit_bytes=vmem << 20),
        cost_estimate=pl.CostEstimate(flops=flops, bytes_accessed=1 << 20, transcendentals=0),
    )


def swap(x, bit, size):
    return lax.ppermute(x, "row", [(i, i ^ bit) for i in range(size)])


def one_column(
    alignment_state, pair_state, cotangent, sequence_row_mask, residue_mask, norm_gain_vector,
    left_matrix_weight, right_matrix_weight, output_weight, output_bias, gate_matrix,
):
    size = lax.axis_size("row")
    rows, n, _ = pair_state.shape
    res = residue_mask.reshape(1, n)
    seq = sequence_row_mask.reshape(1, -1)
    state = alignment_state.transpose(0, 2, 1)
    near = swap(state, 4, size)
    (token,) = call(first_kernel, [((8, n), F32)], flops=20 << 30)()
    gain = norm_gain_vector.reshape(1, -1)
    bias = output_bias.reshape(1, n)
    scale, slope, turned, g0, g1, g2, g3, gain, bias = call(
        gate_kernel,
        [((rows, n, n), F32), ((rows, n, n), F32), ((rows * n, n), BF16)] + [((n, 2 * n), BF16)] * 4
        + [(gain.shape, F32), (bias.shape, F32)],
        scratch=[((n, rows * n), BF16)], smem=1, ins=9, flops=1 << 30, vmem=12,
    )(residue_mask, seq, res, pair_state, cotangent, gate_matrix, gain, bias, token)
    (pair,) = call(norm_kernel, [((2 * n, n), BF16)], smem=1, ins=5)(
        sequence_row_mask, res, gain, state, near
    )
    g1 = swap(g1, 1, size)
    g2 = swap(g2, 2, size)
    g3 = swap(g3, 3, size)
    far = swap(pair, 8, size)
    left_t = left_matrix_weight.T
    kron, block, wide, part = call(
        weight_kernel,
        [((1024, 512), BF16), ((256, n), BF16), ((32, 32 * n), BF16), ((32, 8 * n), BF16)],
        scratch=[((1024, n), F32)], ins=4, flops=1 << 30, vmem=12,
    )(right_matrix_weight.T, left_t, output_weight, pair)
    (y0,) = call(tie_kernel, [((4 * n, n), BF16)], ins=6)(pair, far, g1, g2, g3, block)
    y1 = swap(y0, 2, size)
    y2 = swap(y0, 1, size)
    scratch = [
        ((512, rows * n), BF16), ((n, 32 * n), BF16), ((2, n, n), F32), ((n, 256), BF16),
        ((512, n), F32), ((64, 8 * n), BF16),
    ]
    shared = (turned, kron, block, wide)
    linear, act, gathered = call(
        half_kernel,
        [((n, rows * n), F32), ((64, n), F32), ((64, 8 * n), F32)],
        scratch=scratch, ins=11, flops=2 << 30, vmem=24,
    )(y0, y2, g0, g1, g2, g3, *shared, bias)
    (y1,) = call(tie_kernel, [((4 * n, n), BF16)], ins=2)(y1, act)
    y3 = swap(y1, 1, size)
    update, sums = call(
        main_kernel,
        [((rows, n, n), BF16), ((416, n), BF16)],
        scratch=[((rows * n, n), BF16), *scratch], ins=18, flops=3 << 30, vmem=24,
    )(
        y1, y3, g0, g1, g2, g3, *shared, linear, act, gathered, scale, slope, pair_state, part, left_t
    )
    sums = sums + swap(sums, 4, size)
    sums = sums + swap(sums, 8, size)
    across = swap(sums, 2, size)
    core = swap(sums, 1, size)
    both = swap(across, 1, size)
    grad_out, grad_gate, left, right = call(
        last_kernel,
        [((1024, n), F32), ((n, n), F32), ((32, 64), F32), ((32, 64), F32)],
        ins=4,
    )(sums, core, across, both)
    return update, left.T, right.T, grad_out, grad_gate


def layer_normalize(alignment_state, norm_gain_vector):
    value_entries = alignment_state.astype(jnp.float32)
    average = jnp.mean(value_entries, axis=-1, keepdims=True)
    centred = value_entries - average
    variance = jnp.mean(centred * centred, axis=-1, keepdims=True)
    return (centred * lax.rsqrt(variance + 1e-05) * norm_gain_vector).astype(jnp.bfloat16)


def any_mesh(
    alignment_state,
    pair_state,
    cotangent,
    sequence_row_mask,
    residue_mask,
    norm_gain_vector,
    left_matrix_weight,
    right_matrix_weight,
    output_weight,
    output_bias,
    gate_matrix,
):
    sequence_resident, column_count, alignment_channel_count = alignment_state.shape
    count_of_rows = pair_state.shape[0]
    pair_chans = pair_state.shape[2]
    projection_width = left_matrix_weight.shape[1]
    every_sequence = sequence_row_mask.shape[0]
    row_at = lax.axis_index("row")
    col_at = lax.axis_index("col")
    number_of_rows = lax.axis_size("row")
    contract_first = (((0,), (0,)), ((), ()))
    contract_second = (((1,), (1,)), ((), ()))
    resident_features = layer_normalize(alignment_state, norm_gain_vector)
    seq_flags = sequence_row_mask.astype(jnp.float32)
    res_flags = residue_mask.astype(jnp.float32)
    my_cols = lax.dynamic_slice_in_dim(res_flags, col_at * column_count, column_count, 0)
    my_rows = lax.dynamic_slice_in_dim(res_flags, row_at * count_of_rows, count_of_rows, 0)
    panel_mask = seq_flags[:, None] * my_rows[None, :]
    column_mask = seq_flags[:, None] * my_cols[None, :]
    broadcast_features = lax.all_gather(
        resident_features.reshape(sequence_resident, column_count * alignment_channel_count),
        "col",
        axis=1,
        tiled=True,
    )
    row_portions = broadcast_features.reshape(
        sequence_resident, number_of_rows, count_of_rows * alignment_channel_count
    )
    row_feats = lax.all_to_all(
        row_portions, "row", split_axis=1, concat_axis=0, tiled=True
    ).reshape(every_sequence * count_of_rows, alignment_channel_count)
    left_panel = (
        jnp.dot(row_feats, left_matrix_weight, preferred_element_type=jnp.float32).reshape(
            every_sequence, count_of_rows, projection_width
        )
        * panel_mask[:, :, None]
    ).astype(jnp.bfloat16)
    left_matrix = left_panel.transpose(1, 2, 0).reshape(
        count_of_rows * projection_width, every_sequence
    )
    column_features = lax.all_gather(
        resident_features.reshape(sequence_resident, column_count * alignment_channel_count),
        "row",
        axis=0,
        tiled=True,
    ).reshape(every_sequence, column_count, alignment_channel_count)
    right_panel = (
        jnp.dot(
            column_features.reshape(every_sequence * column_count, alignment_channel_count),
            right_matrix_weight,
            preferred_element_type=jnp.float32,
        ).reshape(every_sequence, column_count, projection_width)
        * column_mask[:, :, None]
    ).astype(jnp.bfloat16)
    surplus_offset = jnp.zeros((alignment_channel_count, projection_width), jnp.float32)

    def absorb(extra, first_col, width_columns, right_part):
        feat_blk = (
            lax.dynamic_slice_in_dim(column_features, first_col, width_columns, 1)
            .reshape(every_sequence * width_columns, alignment_channel_count)
            .astype(jnp.float32)
        )
        mask_blk = lax.dynamic_slice_in_dim(column_mask, first_col, width_columns, 1)
        masked_part = (
            right_part.reshape(every_sequence, width_columns, projection_width)
            * mask_blk[:, :, None]
        ).reshape(every_sequence * width_columns, projection_width)
        return extra + jnp.dot(feat_blk.T, masked_part, precision=lax.Precision.HIGHEST)

    right_flat = right_panel.reshape(every_sequence, column_count * projection_width)
    row_total = jnp.sum(seq_flags)
    col_block = 128
    n_blocks = column_count // col_block

    def one_block(block_idx, carry):
        new_update, grad_out, grad_gate, left_acc, extra = carry
        first_col = block_idx * col_block
        right_blk = lax.dynamic_slice_in_dim(
            right_flat, first_col * projection_width, col_block * projection_width, 1
        )
        outer_prod = jnp.dot(left_matrix, right_blk, preferred_element_type=jnp.float32)
        outer_prod = outer_prod.reshape(
            count_of_rows, projection_width, col_block, projection_width
        ).transpose(0, 2, 1, 3)
        outer_prod = outer_prod.reshape(
            count_of_rows * col_block, projection_width * projection_width
        ).astype(jnp.bfloat16)
        linear = (
            jnp.dot(outer_prod, output_weight, preferred_element_type=jnp.float32) + output_bias
        )
        pair_blk = lax.dynamic_slice_in_dim(pair_state, first_col, col_block, 1).reshape(
            count_of_rows * col_block, pair_chans
        )
        gate_val = jax.nn.sigmoid(
            jnp.dot(pair_blk, gate_matrix, preferred_element_type=jnp.float32)
        )
        blk_flags = lax.dynamic_slice_in_dim(my_cols, first_col, col_block, 0)
        divisor = jnp.maximum(row_total * my_rows[:, None] * blk_flags[None, :], 1.0).reshape(
            count_of_rows * col_block, 1
        )
        cot_blk = (
            lax.dynamic_slice_in_dim(cotangent, first_col, col_block, 1)
            .reshape(count_of_rows * col_block, pair_chans)
            .astype(jnp.float32)
        )
        new_pair = (gate_val * linear / divisor).astype(jnp.bfloat16)
        new_update = lax.dynamic_update_slice_in_dim(
            new_update, new_pair.reshape(count_of_rows, col_block, pair_chans), first_col, 1
        )
        grad_lin = (cot_blk * gate_val / divisor).astype(jnp.bfloat16)
        grad_pre = (cot_blk * linear / divisor * gate_val * (1.0 - gate_val)).astype(jnp.bfloat16)
        grad_out = grad_out + lax.dot_general(
            outer_prod, grad_lin, contract_first, preferred_element_type=jnp.float32
        )
        grad_gate = grad_gate + lax.dot_general(
            pair_blk, grad_pre, contract_first, preferred_element_type=jnp.float32
        )
        grad_outer = lax.dot_general(
            grad_lin, output_weight, contract_second, preferred_element_type=jnp.float32
        ).astype(jnp.bfloat16)
        outer_turned = (
            grad_outer.reshape(count_of_rows, col_block, projection_width, projection_width)
            .transpose(0, 2, 1, 3)
            .reshape(count_of_rows * projection_width, col_block * projection_width)
        )
        left_acc = left_acc + lax.dot_general(
            outer_turned, right_blk, contract_second, preferred_element_type=jnp.float32
        )
        right_part = lax.dot_general(
            left_matrix, outer_turned, contract_first, preferred_element_type=jnp.float32
        )
        extra = absorb(extra, first_col, col_block, right_part)
        return (new_update, grad_out, grad_gate, left_acc, extra)

    start_carry = (
        jnp.zeros((count_of_rows, column_count, pair_chans), jnp.bfloat16),
        jnp.zeros((projection_width * projection_width, pair_chans), jnp.float32),
        jnp.zeros((pair_chans, pair_chans), jnp.float32),
        jnp.zeros((count_of_rows * projection_width, every_sequence), jnp.float32),
        surplus_offset,
    )
    new_update, grad_out, grad_gate, left_acc, extra = lax.fori_loop(
        0, n_blocks, one_block, start_carry
    )
    grad_left_act = (
        left_acc.reshape(count_of_rows, projection_width, every_sequence).transpose(2, 0, 1)
        * panel_mask[:, :, None]
    )
    grad_left = jnp.dot(
        row_feats.astype(jnp.float32).T,
        grad_left_act.reshape(every_sequence * count_of_rows, projection_width),
        precision=lax.Precision.HIGHEST,
    )
    summed_left, summed_right, summed_out, summed_gate = lax.psum(
        (grad_left, extra, grad_out, grad_gate), ("row", "col")
    )
    return (new_update, summed_left, summed_right, summed_out, summed_gate)


def per_device(*args):
    alignment_state, pair_state = args[0], args[1]
    fits = (
        lax.axis_size("col") == 1
        and lax.axis_size("row") == 16
        and alignment_state.shape == (2, 128, 64)
        and pair_state.shape == (8, 128, 128)
    )
    return one_column(*args) if fits else any_mesh(*args)


def solution(mesh):
    return jax.shard_map(
        per_device,
        mesh=mesh,
        in_specs=(
            P(("grp", "row"), "col", None),
            P(("grp", "row"), "col", None),
            P(("grp", "row"), "col", None),
            P("grp"),
            P("grp"),
            P(),
            P(),
            P(),
            P(),
            P(),
            P(),
        ),
        out_specs=(
            P(("grp", "row"), "col", None),
            P("grp", None),
            P("grp", None),
            P("grp", None),
            P("grp", None),
        ),
        check_vma=False,
    )
```

```python
import functools

import jax
import jax.numpy as jnp
from jax import lax
from jax.experimental import pallas as pl
from jax.experimental.pallas import tpu as pltpu
from jax.sharding import PartitionSpec as P

F32 = jnp.float32
BF16 = jnp.bfloat16
VMEM = pl.BlockSpec(memory_space=pltpu.VMEM)
SMEM = pl.BlockSpec(memory_space=pltpu.SMEM)
LHS_T = (((0,), (0,)), ((), ()))
RHS_T = (((1,), (1,)), ((), ()))
QUAD = 4
ACROSS = 4
CHANS = 32
GROUP = 16


def iota(shape, dim):
    return lax.broadcasted_iota(jnp.int32, shape, dim)


def dot(a, b, dims=(((1,), (0,)), ((), ())), **kw):
    return lax.dot_general(a, b, dims, preferred_element_type=F32, **kw)


def place_in_quad(row):
    return row % 2 + row // ACROSS % 2 * 2


def first_kernel(out_ref):
    out_ref[...] = jnp.zeros_like(out_ref)


def norm_kernel(seq_ref, res_ref, gain_ref, own_ref, near_ref, after_ref, out_ref):
    row = lax.axis_index("row")
    n = res_ref.shape[1]
    res = res_ref[...].astype(F32)
    gain = gain_ref[...]
    gain = jnp.concatenate([gain, gain], axis=1)
    for at, (state_ref, first) in enumerate(((own_ref, row * 2), (near_ref, (row ^ 4) * 2))):
        halves = []
        for s in range(2):
            value = state_ref[s].astype(F32)
            centred = value - jnp.mean(value, axis=0, keepdims=True)
            variance = jnp.mean(centred * centred, axis=0, keepdims=True)
            seq = seq_ref[first + s].astype(F32)
            halves.append(centred * (lax.rsqrt(variance + 1e-05) * (res * seq)))
        turned = jnp.concatenate(halves, axis=0).T
        out_ref[at * n : (at + 1) * n, :] = (turned * gain).astype(BF16)


def gate_kernel(
    res_s_ref, seq_ref, res_ref, pair_ref, cot_ref, gate_ref, gain_ref, bias_ref, after_ref,
    scale_ref, slope_ref, turned_ref, own_ref, core_ref, across_ref, gain_out_ref, bias_out_ref,
    full_ref,
):
    gain_out_ref[...] = gain_ref[...]
    bias_out_ref[...] = bias_ref[...]
    row = lax.axis_index("row")
    quad_at = place_in_quad(row)
    rows = pair_ref.shape[0]
    n = res_ref.shape[1]
    total = jnp.sum(seq_ref[...].astype(F32), axis=1, keepdims=True)
    eye = iota((n, n), 0) == iota((n, n), 1)
    res_col = jnp.sum(jnp.where(eye, res_ref[...].astype(F32), 0.0), axis=1, keepdims=True)
    wide = QUAD * n
    src = iota((wide, wide), 0)
    dst = iota((wide, wide), 1)
    slot = dst // n
    chan = (quad_at ^ slot) * CHANS + dst % CHANS
    place = jnp.where(
        (src // n == (dst % n) // CHANS) & (src % n == chan), 1.0, 0.0
    ).astype(BF16)
    outs = ((own_ref, 0), (core_ref, 0), (across_ref, 0), (across_ref, 2 * n))
    for half in range(rows // QUAD):
        for k in range(QUAD):
            i = half * QUAD + k
            gate = jax.nn.sigmoid(dot(pair_ref[i], gate_ref[...]))
            res_row = res_s_ref[row * rows + i].astype(F32)
            scale = gate / jnp.maximum(total * res_row * res_col, 1.0)
            lin = cot_ref[i].astype(F32) * scale
            scale_ref[i] = scale
            slope_ref[i] = lin * (1.0 - gate)
            full_ref[:, i * n : (i + 1) * n] = lin.astype(BF16)
            turned_ref[i * n : (i + 1) * n, :] = lin.T.astype(BF16)
        packed = dot(full_ref[:, half * wide : (half + 1) * wide], place).astype(BF16)
        for m in range(QUAD):
            out_ref, at = outs[m]
            out_ref[:, at + half * n : at + (half + 1) * n] = packed[:, m * n : (m + 1) * n]


def weight_kernel(
    right_ref, left_ref, out_w_ref, after_ref,
    kron_ref, block_ref, wide_ref, part_ref, wf_ref,
):
    quad_at = place_in_quad(lax.axis_index("row"))
    width, chans = right_ref.shape
    n = out_w_ref.shape[1]
    cols = width * GROUP
    spread = jnp.where(iota((width, cols), 0) == iota((width, cols), 1) // GROUP, 1.0, 0.0)
    repeated = dot(right_ref[...], spread.astype(BF16), LHS_T)
    lane = iota((chans, cols), 1) % GROUP
    for s in range(GROUP):
        kron_ref[s * chans : (s + 1) * chans, :] = jnp.where(lane == s, repeated, 0.0).astype(BF16)
    spread = jnp.where(iota((width, n), 0) == iota((width, n), 1) % width, 1.0, 0.0)
    repeated = dot(left_ref[...], spread.astype(BF16), LHS_T)
    lane = iota((chans, n), 1) // width
    for k in range(QUAD):
        block_ref[k * chans : (k + 1) * chans, :] = jnp.where(lane == k, repeated, 0.0).astype(BF16)
    wf_ref[...] = out_w_ref[...].astype(F32)
    for e in range(width):
        wide_ref[:, e * n : (e + 1) * n] = wf_ref[pl.ds(e, width, stride=width), :].astype(BF16)
    pick = jnp.where(
        iota((n, n), 0) == quad_at * CHANS + iota((n, n), 1) % CHANS, 1.0, 0.0
    ).astype(BF16)
    wf_ref[...] = dot(out_w_ref[...], pick)
    lane = iota((width, n), 1) // CHANS
    for h in range(width // QUAD):
        tile = None
        for k in range(QUAD):
            rows = wf_ref[pl.ds(h * QUAD + k, width, stride=width), :]
            tile = rows if tile is None else jnp.where(lane == k, rows, tile)
        part_ref[:, h * n : (h + 1) * n] = tile.astype(BF16)


def fold(tiles, lane):
    high, low = lane // 2 == 0, lane % 2 == 0
    pairs = [
        jnp.where(high, tiles[k], tiles[k + 2])
        + pltpu.roll(jnp.where(high, tiles[k + 2], tiles[k]), 2 * CHANS, 1)
        for k in range(2)
    ]
    other = jnp.where(low, pairs[1], pairs[0])
    size = lane.shape[1]
    other = jnp.where(low, pltpu.roll(other, size - CHANS, 1), pltpu.roll(other, CHANS, 1))
    return jnp.where(low, pairs[0], pairs[1]) + other


def half_of_rows(ys, turned, kron_ref, block_ref, wide_ref, right_t_ref, own_ref, scratch):
    m_ref, turn_ref, right_ref, flat_ref = scratch
    row = lax.axis_index("row")
    n = ys[0].shape[1]
    chans, width = 64, 32
    slots = [y[t * n : (t + 1) * n, :] for y in ys for t in range(4)]
    right = dot(jnp.concatenate(slots, axis=1), kron_ref[...]).astype(BF16)
    right_t_ref[...] = right.T
    at = iota((32, n), 0)
    four = at % 8
    member = four // 2
    here = (row ^ (member % 2 + member // 2 * ACROSS)) * 8 + (four % 2) * QUAD + at // 8
    pick = jnp.where(iota((32, n), 1) == here, 1.0, 0.0).astype(BF16)
    for t, slot in enumerate(slots):
        picked = dot(pick, slot)
        for s in range(2):
            at = (2 * t + s) * 8
            for half in range(2):
                turn_ref[half, at : at + 8, :] = jnp.concatenate(
                    [
                        picked[k * 8 : (k + 1) * 8, s * chans : (s + 1) * chans]
                        for k in (2 * half, 2 * half + 1)
                    ],
                    axis=1,
                )
    for f in range(8):
        for half in range(2):
            own_ref[f * GROUP : (f + 1) * GROUP, half * n : (half + 1) * n] = turn_ref[
                half, pl.ds(f, GROUP, stride=8), :
            ].astype(BF16)
    left = dot(own_ref[0 : 2 * GROUP, :], block_ref[...])
    mine = jnp.concatenate(
        [
            left[f * GROUP : (f + 1) * GROUP, k * width : (k + 1) * width]
            for f in range(2)
            for k in range(QUAD)
        ],
        axis=0,
    ).astype(BF16)
    for e4 in range(width // 4):
        part = dot(mine, wide_ref[:, e4 * 4 * n : (e4 + 1) * 4 * n]).astype(BF16)
        for el in range(4):
            e = e4 * 4 + el
            for i in range(8):
                m_ref[e * GROUP : (e + 1) * GROUP, i * n : (i + 1) * n] = part[
                    i * GROUP : (i + 1) * GROUP, el * n : (el + 1) * n
                ]
    linear = dot(right, m_ref[...])
    right_ref[...] = dot(m_ref[...], turned[...])
    for t in range(8):
        for s in range(2):
            flat_ref[s * width : (s + 1) * width, t * n : (t + 1) * n] = right_ref[
                pl.ds(2 * t + s, width, stride=GROUP), :
            ].astype(BF16)
    half = 4 * n
    act = dot(flat_ref[:, :half], ys[0][...]) + dot(flat_ref[:, half:], ys[1][...])
    return linear, act


def half_kernel(
    y0_ref, y1_ref, turned_ref, kron_ref, block_ref, wide_ref, bias_ref,
    linear_ref, act_ref, right_t_ref, own_ref, *scratch
):
    linear, act = half_of_rows(
        (y0_ref, y1_ref), turned_ref, kron_ref, block_ref, wide_ref, right_t_ref, own_ref, scratch
    )
    linear_ref[...] = linear + jnp.concatenate([bias_ref[...]] * 8, axis=1)
    act_ref[...] = act


def pair_kernel(
    y0_ref, y1_ref, turned_ref, kron_ref, block_ref, wide_ref,
    linear_ref, act_ref, slope_ref, pair_ref,
    value_ref, gate_ref, grad_right_ref, right_t_ref, own_ref, slope_s_ref, *scratch
):
    rows, n, _ = pair_ref.shape
    linear, act = half_of_rows(
        (y0_ref, y1_ref), turned_ref, kron_ref, block_ref, wide_ref, right_t_ref, own_ref, scratch
    )
    for i in range(rows):
        value = linear[:, i * n : (i + 1) * n] + linear_ref[:, i * n : (i + 1) * n]
        value_ref[i] = value
        slope_s_ref[i * n : (i + 1) * n, :] = (slope_ref[i] * value).astype(BF16)
    gate_ref[...] = dot(pair_ref[...].reshape(rows * n, n), slope_s_ref[...], LHS_T).astype(BF16)
    act = act + act_ref[...]
    grad_right_ref[...] = act[:32, :64] + act[32:, 64:]


def update_kernel(scale_ref, value_ref, after_ref, update_ref, token_ref):
    token_ref[...] = jnp.zeros_like(token_ref)
    update_ref[...] = (scale_ref[...] * value_ref[...]).astype(BF16)


def add_kernel(own_ref, other_ref, after_ref, out_ref):
    out_ref[...] = (own_ref[...].astype(F32) + other_ref[...].astype(F32)).astype(BF16)


def out_kernel(
    right0_ref, right1_ref, own0_ref, own1_ref, own_ref, core_ref, across_ref,
    part_ref, left_ref, gate_ref, grad_right_ref,
    sums_ref, n_ref
):
    n = gate_ref.shape[0]
    chans, width = 64, 32
    half = 8 * GROUP
    grads = (own_ref[...], core_ref[:, : 2 * n], across_ref[:, : 2 * n], core_ref[:, 2 * n :])
    for f2, grad in enumerate(grads):
        for g, right_ref in enumerate((right0_ref, right1_ref)):
            part = dot(right_ref[...], grad).astype(BF16)
            for fl in range(2):
                at = g * half + (f2 * 2 + fl) * GROUP
                for e in range(width):
                    n_ref[at : at + GROUP, e * n : (e + 1) * n] = part[
                        e * GROUP : (e + 1) * GROUP, fl * n : (fl + 1) * n
                    ]
    own_t = jnp.concatenate([own0_ref[...], own1_ref[...]], axis=0).T
    lane = iota((chans, n), 1) // CHANS
    packed = []
    for h in range(width // QUAD):
        whole = dot(own_t, n_ref[:, h * 4 * n : (h + 1) * 4 * n])
        tiles = []
        for el in range(QUAD):
            tile = whole[0:chans, el * n : (el + 1) * n]
            for k in range(1, QUAD):
                tile = jnp.where(
                    lane == k, whole[k * chans : (k + 1) * chans, el * n : (el + 1) * n], tile
                )
            tiles.append(tile)
        packed.append(fold(tiles, lane))
    feat = jnp.concatenate(packed, axis=1)
    coarse = feat.astype(BF16)
    fine = (feat - coarse.astype(F32)).astype(BF16)
    grad_out = dot(left_ref[...], coarse) + dot(left_ref[...], fine)
    for h in range(width // QUAD):
        sums_ref[h * width : (h + 1) * width, :] = grad_out[:, h * n : (h + 1) * n].astype(BF16)
    grad_left = dot(part_ref[...], coarse, RHS_T) + dot(part_ref[...], fine, RHS_T)
    sums_ref[256:384, :] = gate_ref[...]
    sums_ref[384:416, :] = jnp.concatenate([grad_left, grad_right_ref[...]], axis=1).astype(BF16)


def join_kernel(own_ref, beside_ref, across_ref, both_ref, out_ref):
    def pair(a_ref, b_ref, lo, hi):
        return a_ref[lo:hi, :].astype(F32) + b_ref[lo:hi, :].astype(F32)

    out_ref[0:256, :] = pair(own_ref, beside_ref, 0, 256).astype(BF16)
    out_ref[256:512, :] = pair(across_ref, both_ref, 0, 256).astype(BF16)
    out_ref[512:672, :] = (
        pair(own_ref, beside_ref, 256, 416) + pair(across_ref, both_ref, 256, 416)
    ).astype(BF16)


def last_kernel(local_ref, other_ref, out_ref, gate_ref, left_ref, right_ref):
    quad_at = place_in_quad(lax.axis_index("row"))
    n = local_ref.shape[1]
    wide = QUAD * n
    src = iota((wide, wide), 0)
    dst = iota((wide, wide), 1)
    chan = (quad_at ^ (src // n)) * CHANS + src % CHANS
    place = jnp.where(
        (dst // n == (src % n) // CHANS) & (dst % n == chan), 1.0, 0.0
    ).astype(BF16)
    packed = jnp.concatenate(
        [local_ref[0:256, :], other_ref[0:256, :], local_ref[256:512, :], other_ref[256:512, :]], axis=1
    )
    whole = dot(packed, place)
    for h in range(8):
        for el in range(4):
            out_ref[pl.ds(h * 4 + el, 32, stride=32), :] = whole[
                h * 32 : (h + 1) * 32, el * n : (el + 1) * n
            ]
    gate_ref[...] = local_ref[512:640, :].astype(F32) + other_ref[512:640, :].astype(F32)
    both = local_ref[640:672, :].astype(F32) + other_ref[640:672, :].astype(F32)
    left_ref[...] = both[:, 0:64]
    right_ref[...] = both[:, 64:128]


def tie_kernel(*refs):
    out_ref, at = refs[-1], 0
    for ref in refs:
        if at < out_ref.shape[0]:
            out_ref[at : at + ref.shape[0], :] = ref[...]
            at += ref.shape[0]


def call(kernel, shapes, scratch=(), smem=0, ins=0, flops=1 << 20, vmem=4):
    return pl.pallas_call(
        kernel,
        out_shape=[jax.ShapeDtypeStruct(s, d) for s, d in shapes],
        in_specs=[SMEM] * smem + [VMEM] * (ins - smem),
        out_specs=[VMEM] * len(shapes),
        scratch_shapes=[pltpu.VMEM(s, d) for s, d in scratch],
        compiler_params=pltpu.CompilerParams(vmem_limit_bytes=vmem << 20),
        cost_estimate=pl.CostEstimate(flops=flops, bytes_accessed=1 << 20, transcendentals=0),
    )


def swap(x, bit, size):
    return lax.ppermute(x, "row", [(i, i ^ bit) for i in range(size)])


def one_column(
    alignment_state, pair_state, cotangent, sequence_row_mask, residue_mask, norm_gain_vector,
    left_matrix_weight, right_matrix_weight, output_weight, output_bias, gate_matrix,
):
    size = lax.axis_size("row")
    rows, n, _ = pair_state.shape
    res = residue_mask.reshape(1, n)
    seq = sequence_row_mask.reshape(1, -1)
    state = alignment_state.transpose(0, 2, 1)
    near = swap(state, 4, size)
    (token,) = call(first_kernel, [((8, n), F32)], flops=20 << 30)()
    gain = norm_gain_vector.reshape(1, -1)
    bias = output_bias.reshape(1, n)
    scale, slope, turned, own, core, across, gain, bias = call(
        gate_kernel,
        [((rows, n, n), F32), ((rows, n, n), F32), ((rows * n, n), BF16)] + [((n, 2 * n), BF16)] * 2
        + [((n, 4 * n), BF16), (gain.shape, F32), (bias.shape, F32)],
        scratch=[((n, rows * n), BF16)], smem=1, ins=9, flops=1 << 30, vmem=12,
    )(residue_mask, seq, res, pair_state, cotangent, gate_matrix, gain, bias, token)
    (pair,) = call(norm_kernel, [((2 * n, n), BF16)], smem=1, ins=6)(
        sequence_row_mask, res, gain, state, near, own
    )
    far = swap(pair, 8, size)
    left_t = left_matrix_weight.T
    kron, block, wide, part = call(
        weight_kernel,
        [((1024, 512), BF16), ((256, n), BF16), ((32, 32 * n), BF16), ((32, 8 * n), BF16)],
        scratch=[((1024, n), F32)], ins=4, flops=1 << 30, vmem=12,
    )(right_matrix_weight.T, left_t, output_weight, pair)
    (y0,) = call(tie_kernel, [((4 * n, n), BF16)], ins=3)(pair, far, block)
    y1 = swap(y0, 2, size)
    y2 = swap(y0, 1, size)
    (across,) = call(tie_kernel, [((n, 4 * n), BF16)], ins=2)(across, y2)
    across = swap(across, ACROSS, size)
    core = swap(jnp.concatenate([core, across[:, 2 * n :]], axis=1), 1, size)
    scratch = [
        ((512, rows * n), BF16), ((2, n, n), F32), ((512, n), F32), ((64, 8 * n), BF16),
    ]
    shared = (turned, kron, block, wide)
    kept = [((512, n), BF16), ((n, 256), BF16)]
    linear, act, right0, own0 = call(
        half_kernel,
        [((n, rows * n), F32), ((64, n), F32), *kept],
        scratch=scratch, ins=7, flops=2 << 30, vmem=24,
    )(y0, y2, *shared, bias)
    (y1,) = call(tie_kernel, [((4 * n, n), BF16)], ins=2)(y1, act)
    y3 = swap(y1, 1, size)
    value, gate_sum, right_sum, right1, own1 = call(
        pair_kernel,
        [((rows, n, n), F32), ((n, n), BF16), ((32, 64), F32), *kept],
        scratch=[((rows * n, n), BF16), *scratch], ins=10, flops=2 << 30, vmem=24,
    )(y1, y3, *shared, linear, act, slope, pair_state)
    (sums,) = call(
        out_kernel, [((416, n), BF16)], scratch=[((256, 32 * n), BF16)], ins=11, flops=1 << 30, vmem=24,
    )(right0, right1, own0, own1, own, core, across, part, left_t, gate_sum, right_sum)
    update, token = call(update_kernel, [((rows, n, n), BF16), ((8, n), F32)], ins=3, flops=1 << 30, vmem=8)(scale, value, sums)
    (sums,) = call(add_kernel, [((416, n), BF16)], ins=3)(sums, swap(sums, 8, size), token)
    others = [swap(sums, step, size) for step in (2, ACROSS, 2 ^ ACROSS)]
    (local,) = call(join_kernel, [((672, n), BF16)], ins=4)(sums, *others)
    other = swap(local, 1, size)
    grad_out, grad_gate, left, right = call(
        last_kernel,
        [((1024, n), F32), ((n, n), F32), ((32, 64), F32), ((32, 64), F32)],
        ins=2,
    )(local, other)
    return update, left.T, right.T, grad_out, grad_gate


def layer_normalize(alignment_state, norm_gain_vector):
    value_entries = alignment_state.astype(jnp.float32)
    average = jnp.mean(value_entries, axis=-1, keepdims=True)
    centred = value_entries - average
    variance = jnp.mean(centred * centred, axis=-1, keepdims=True)
    return (centred * lax.rsqrt(variance + 1e-05) * norm_gain_vector).astype(jnp.bfloat16)


def any_mesh(
    alignment_state,
    pair_state,
    cotangent,
    sequence_row_mask,
    residue_mask,
    norm_gain_vector,
    left_matrix_weight,
    right_matrix_weight,
    output_weight,
    output_bias,
    gate_matrix,
):
    sequence_resident, column_count, alignment_channel_count = alignment_state.shape
    count_of_rows = pair_state.shape[0]
    pair_chans = pair_state.shape[2]
    projection_width = left_matrix_weight.shape[1]
    every_sequence = sequence_row_mask.shape[0]
    row_at = lax.axis_index("row")
    col_at = lax.axis_index("col")
    number_of_rows = lax.axis_size("row")
    contract_first = (((0,), (0,)), ((), ()))
    contract_second = (((1,), (1,)), ((), ()))
    resident_features = layer_normalize(alignment_state, norm_gain_vector)
    seq_flags = sequence_row_mask.astype(jnp.float32)
    res_flags = residue_mask.astype(jnp.float32)
    my_cols = lax.dynamic_slice_in_dim(res_flags, col_at * column_count, column_count, 0)
    my_rows = lax.dynamic_slice_in_dim(res_flags, row_at * count_of_rows, count_of_rows, 0)
    panel_mask = seq_flags[:, None] * my_rows[None, :]
    column_mask = seq_flags[:, None] * my_cols[None, :]
    broadcast_features = lax.all_gather(
        resident_features.reshape(sequence_resident, column_count * alignment_channel_count),
        "col",
        axis=1,
        tiled=True,
    )
    row_portions = broadcast_features.reshape(
        sequence_resident, number_of_rows, count_of_rows * alignment_channel_count
    )
    row_feats = lax.all_to_all(
        row_portions, "row", split_axis=1, concat_axis=0, tiled=True
    ).reshape(every_sequence * count_of_rows, alignment_channel_count)
    left_panel = (
        jnp.dot(row_feats, left_matrix_weight, preferred_element_type=jnp.float32).reshape(
            every_sequence, count_of_rows, projection_width
        )
        * panel_mask[:, :, None]
    ).astype(jnp.bfloat16)
    left_matrix = left_panel.transpose(1, 2, 0).reshape(
        count_of_rows * projection_width, every_sequence
    )
    column_features = lax.all_gather(
        resident_features.reshape(sequence_resident, column_count * alignment_channel_count),
        "row",
        axis=0,
        tiled=True,
    ).reshape(every_sequence, column_count, alignment_channel_count)
    right_panel = (
        jnp.dot(
            column_features.reshape(every_sequence * column_count, alignment_channel_count),
            right_matrix_weight,
            preferred_element_type=jnp.float32,
        ).reshape(every_sequence, column_count, projection_width)
        * column_mask[:, :, None]
    ).astype(jnp.bfloat16)
    surplus_offset = jnp.zeros((alignment_channel_count, projection_width), jnp.float32)

    def absorb(extra, first_col, width_columns, right_part):
        feat_blk = (
            lax.dynamic_slice_in_dim(column_features, first_col, width_columns, 1)
            .reshape(every_sequence * width_columns, alignment_channel_count)
            .astype(jnp.float32)
        )
        mask_blk = lax.dynamic_slice_in_dim(column_mask, first_col, width_columns, 1)
        masked_part = (
            right_part.reshape(every_sequence, width_columns, projection_width)
            * mask_blk[:, :, None]
        ).reshape(every_sequence * width_columns, projection_width)
        return extra + jnp.dot(feat_blk.T, masked_part, precision=lax.Precision.HIGHEST)

    right_flat = right_panel.reshape(every_sequence, column_count * projection_width)
    row_total = jnp.sum(seq_flags)
    col_block = 128
    n_blocks = column_count // col_block

    def one_block(block_idx, carry):
        new_update, grad_out, grad_gate, left_acc, extra = carry
        first_col = block_idx * col_block
        right_blk = lax.dynamic_slice_in_dim(
            right_flat, first_col * projection_width, col_block * projection_width, 1
        )
        outer_prod = jnp.dot(left_matrix, right_blk, preferred_element_type=jnp.float32)
        outer_prod = outer_prod.reshape(
            count_of_rows, projection_width, col_block, projection_width
        ).transpose(0, 2, 1, 3)
        outer_prod = outer_prod.reshape(
            count_of_rows * col_block, projection_width * projection_width
        ).astype(jnp.bfloat16)
        linear = (
            jnp.dot(outer_prod, output_weight, preferred_element_type=jnp.float32) + output_bias
        )
        pair_blk = lax.dynamic_slice_in_dim(pair_state, first_col, col_block, 1).reshape(
            count_of_rows * col_block, pair_chans
        )
        gate_val = jax.nn.sigmoid(
            jnp.dot(pair_blk, gate_matrix, preferred_element_type=jnp.float32)
        )
        blk_flags = lax.dynamic_slice_in_dim(my_cols, first_col, col_block, 0)
        divisor = jnp.maximum(row_total * my_rows[:, None] * blk_flags[None, :], 1.0).reshape(
            count_of_rows * col_block, 1
        )
        cot_blk = (
            lax.dynamic_slice_in_dim(cotangent, first_col, col_block, 1)
            .reshape(count_of_rows * col_block, pair_chans)
            .astype(jnp.float32)
        )
        new_pair = (gate_val * linear / divisor).astype(jnp.bfloat16)
        new_update = lax.dynamic_update_slice_in_dim(
            new_update, new_pair.reshape(count_of_rows, col_block, pair_chans), first_col, 1
        )
        grad_lin = (cot_blk * gate_val / divisor).astype(jnp.bfloat16)
        grad_pre = (cot_blk * linear / divisor * gate_val * (1.0 - gate_val)).astype(jnp.bfloat16)
        grad_out = grad_out + lax.dot_general(
            outer_prod, grad_lin, contract_first, preferred_element_type=jnp.float32
        )
        grad_gate = grad_gate + lax.dot_general(
            pair_blk, grad_pre, contract_first, preferred_element_type=jnp.float32
        )
        grad_outer = lax.dot_general(
            grad_lin, output_weight, contract_second, preferred_element_type=jnp.float32
        ).astype(jnp.bfloat16)
        outer_turned = (
            grad_outer.reshape(count_of_rows, col_block, projection_width, projection_width)
            .transpose(0, 2, 1, 3)
            .reshape(count_of_rows * projection_width, col_block * projection_width)
        )
        left_acc = left_acc + lax.dot_general(
            outer_turned, right_blk, contract_second, preferred_element_type=jnp.float32
        )
        right_part = lax.dot_general(
            left_matrix, outer_turned, contract_first, preferred_element_type=jnp.float32
        )
        extra = absorb(extra, first_col, col_block, right_part)
        return (new_update, grad_out, grad_gate, left_acc, extra)

    start_carry = (
        jnp.zeros((count_of_rows, column_count, pair_chans), jnp.bfloat16),
        jnp.zeros((projection_width * projection_width, pair_chans), jnp.float32),
        jnp.zeros((pair_chans, pair_chans), jnp.float32),
        jnp.zeros((count_of_rows * projection_width, every_sequence), jnp.float32),
        surplus_offset,
    )
    new_update, grad_out, grad_gate, left_acc, extra = lax.fori_loop(
        0, n_blocks, one_block, start_carry
    )
    grad_left_act = (
        left_acc.reshape(count_of_rows, projection_width, every_sequence).transpose(2, 0, 1)
        * panel_mask[:, :, None]
    )
    grad_left = jnp.dot(
        row_feats.astype(jnp.float32).T,
        grad_left_act.reshape(every_sequence * count_of_rows, projection_width),
        precision=lax.Precision.HIGHEST,
    )
    summed_left, summed_right, summed_out, summed_gate = lax.psum(
        (grad_left, extra, grad_out, grad_gate), ("row", "col")
    )
    return (new_update, summed_left, summed_right, summed_out, summed_gate)


def per_device(*args):
    alignment_state, pair_state = args[0], args[1]
    fits = (
        lax.axis_size("col") == 1
        and lax.axis_size("row") == 16
        and alignment_state.shape == (2, 128, 64)
        and pair_state.shape == (8, 128, 128)
    )
    return one_column(*args) if fits else any_mesh(*args)


def solution(mesh):
    return jax.shard_map(
        per_device,
        mesh=mesh,
        in_specs=(
            P(("grp", "row"), "col", None),
            P(("grp", "row"), "col", None),
            P(("grp", "row"), "col", None),
            P("grp"),
            P("grp"),
            P(),
            P(),
            P(),
            P(),
            P(),
            P(),
        ),
        out_specs=(
            P(("grp", "row"), "col", None),
            P("grp", None),
            P("grp", None),
            P("grp", None),
            P("grp", None),
        ),
        check_vma=False,
    )
```

```python
import functools

import jax
import jax.numpy as jnp
from jax import lax
from jax.experimental import pallas as pl
from jax.experimental.pallas import tpu as pltpu
from jax.sharding import PartitionSpec as P

F32 = jnp.float32
BF16 = jnp.bfloat16
VMEM = pl.BlockSpec(memory_space=pltpu.VMEM)
SMEM = pl.BlockSpec(memory_space=pltpu.SMEM)
LHS_T = (((0,), (0,)), ((), ()))
RHS_T = (((1,), (1,)), ((), ()))
QUAD = 4
ACROSS = 4
CHANS = 32
GROUP = 16


def iota(shape, dim):
    return lax.broadcasted_iota(jnp.int32, shape, dim)


def dot(a, b, dims=(((1,), (0,)), ((), ())), **kw):
    return lax.dot_general(a, b, dims, preferred_element_type=F32, **kw)


def place_in_quad(row):
    return row % 2 + row // ACROSS % 2 * 2


def first_kernel(out_ref):
    out_ref[...] = jnp.zeros_like(out_ref)


def norm_kernel(
    seq_ref, res_ref, gain_ref, own_ref, near_ref, core_ref, across_ref, out_ref, to_core_ref, to_across_ref
):
    row = lax.axis_index("row")
    n = res_ref.shape[1]
    res = res_ref[...].astype(F32)
    gain = gain_ref[...]
    gain = jnp.concatenate([gain, gain], axis=1)
    for at, (state_ref, first) in enumerate(((own_ref, row * 2), (near_ref, (row ^ 8) * 2))):
        halves = []
        for s in range(2):
            value = state_ref[s].astype(F32)
            centred = value - jnp.mean(value, axis=0, keepdims=True)
            variance = jnp.mean(centred * centred, axis=0, keepdims=True)
            seq = seq_ref[first + s].astype(F32)
            halves.append(centred * (lax.rsqrt(variance + 1e-05) * (res * seq)))
        turned = jnp.concatenate(halves, axis=0).T
        value = (turned * gain).astype(BF16)
        for ref in (out_ref, to_core_ref, to_across_ref):
            ref[at * n : (at + 1) * n, :] = value
    to_core_ref[2 * n :, :] = core_ref[...]
    to_across_ref[2 * n :, :] = across_ref[...]


def gate_kernel(
    res_s_ref, seq_ref, res_ref, pair_ref, cot_ref, gate_ref, gain_ref, bias_ref, after_ref,
    scale_ref, slope_ref, turned_ref, own_ref, core_ref, across_ref, gain_out_ref, bias_out_ref,
    full_ref,
):
    gain_out_ref[...] = gain_ref[...]
    bias_out_ref[...] = bias_ref[...]
    row = lax.axis_index("row")
    quad_at = place_in_quad(row)
    rows = pair_ref.shape[0]
    n = res_ref.shape[1]
    total = jnp.sum(seq_ref[...].astype(F32), axis=1, keepdims=True)
    eye = iota((n, n), 0) == iota((n, n), 1)
    res_col = jnp.sum(jnp.where(eye, res_ref[...].astype(F32), 0.0), axis=1, keepdims=True)
    wide = QUAD * n
    src = iota((wide, wide), 0)
    dst = iota((wide, wide), 1)
    slot = dst // n
    chan = (quad_at ^ slot) * CHANS + dst % CHANS
    place = jnp.where(
        (src // n == (dst % n) // CHANS) & (src % n == chan), 1.0, 0.0
    ).astype(BF16)
    outs = ((own_ref, 0), (core_ref, 0), (across_ref, 0), (across_ref, 2))
    for half in range(rows // QUAD):
        for k in range(QUAD):
            i = half * QUAD + k
            gate = jax.nn.sigmoid(dot(pair_ref[i], gate_ref[...]))
            res_row = res_s_ref[row * rows + i].astype(F32)
            scale = gate / jnp.maximum(total * res_row * res_col, 1.0)
            lin = cot_ref[i].astype(F32) * scale
            scale_ref[i] = scale
            slope_ref[i] = lin * (1.0 - gate)
            full_ref[:, i * n : (i + 1) * n] = lin.astype(BF16)
            turned_ref[i * n : (i + 1) * n, :] = lin.T.astype(BF16)
        packed = dot(full_ref[:, half * wide : (half + 1) * wide], place).astype(BF16)
        for m in range(QUAD):
            out_ref, at = outs[m]
            out_ref[(at + half) * n : (at + half + 1) * n, :] = packed[:, m * n : (m + 1) * n]


def weight_kernel(
    right_ref, left_ref, out_w_ref, after_ref,
    kron_ref, block_ref, wide_ref, part_ref, wf_ref,
):
    quad_at = place_in_quad(lax.axis_index("row"))
    width, chans = right_ref.shape
    n = out_w_ref.shape[1]
    cols = width * GROUP
    spread = jnp.where(iota((width, cols), 0) == iota((width, cols), 1) // GROUP, 1.0, 0.0)
    repeated = dot(right_ref[...], spread.astype(BF16), LHS_T)
    lane = iota((chans, cols), 1) % GROUP
    for s in range(GROUP):
        kron_ref[s * chans : (s + 1) * chans, :] = jnp.where(lane == s, repeated, 0.0).astype(BF16)
    spread = jnp.where(iota((width, n), 0) == iota((width, n), 1) % width, 1.0, 0.0)
    repeated = dot(left_ref[...], spread.astype(BF16), LHS_T)
    lane = iota((chans, n), 1) // width
    for k in range(QUAD):
        block_ref[k * chans : (k + 1) * chans, :] = jnp.where(lane == k, repeated, 0.0).astype(BF16)
    wf_ref[...] = out_w_ref[...].astype(F32)
    for e in range(width):
        wide_ref[:, e * n : (e + 1) * n] = wf_ref[pl.ds(e, width, stride=width), :].astype(BF16)
    pick = jnp.where(
        iota((n, n), 0) == quad_at * CHANS + iota((n, n), 1) % CHANS, 1.0, 0.0
    ).astype(BF16)
    wf_ref[...] = dot(out_w_ref[...], pick)
    lane = iota((width, n), 1) // CHANS
    for h in range(width // QUAD):
        tile = None
        for k in range(QUAD):
            rows = wf_ref[pl.ds(h * QUAD + k, width, stride=width), :]
            tile = rows if tile is None else jnp.where(lane == k, rows, tile)
        part_ref[:, h * n : (h + 1) * n] = tile.astype(BF16)


def fold(tiles, lane):
    high, low = lane // 2 == 0, lane % 2 == 0
    pairs = [
        jnp.where(high, tiles[k], tiles[k + 2])
        + pltpu.roll(jnp.where(high, tiles[k + 2], tiles[k]), 2 * CHANS, 1)
        for k in range(2)
    ]
    other = jnp.where(low, pairs[1], pairs[0])
    size = lane.shape[1]
    other = jnp.where(low, pltpu.roll(other, size - CHANS, 1), pltpu.roll(other, CHANS, 1))
    return jnp.where(low, pairs[0], pairs[1]) + other


def half_of_rows(ys, turned, kron_ref, block_ref, wide_ref, right_t_ref, own_ref, scratch):
    m_ref, turn_ref, right_ref, flat_ref = scratch
    row = lax.axis_index("row")
    n = ys[0].shape[1]
    chans, width = 64, 32
    slots = [y[t * n : (t + 1) * n, :] for y in ys for t in range(2)]
    right = dot(jnp.concatenate(slots, axis=1), kron_ref[...]).astype(BF16)
    right_t_ref[...] = right.T
    at = iota((32, n), 0)
    four = at % 8
    member = four // 2
    here = (row ^ (member % 2 + member // 2 * ACROSS)) * 8 + (four % 2) * QUAD + at // 8
    pick = jnp.where(iota((32, n), 1) == here, 1.0, 0.0).astype(BF16)
    for t, slot in enumerate(slots):
        picked = dot(pick, slot)
        for s in range(2):
            at = (2 * t + s) * 8
            for half in range(2):
                turn_ref[half, at : at + 8, :] = jnp.concatenate(
                    [
                        picked[k * 8 : (k + 1) * 8, s * chans : (s + 1) * chans]
                        for k in (2 * half, 2 * half + 1)
                    ],
                    axis=1,
                )
    for f in range(8):
        for half in range(2):
            own_ref[f * GROUP : (f + 1) * GROUP, half * n : (half + 1) * n] = turn_ref[
                half, pl.ds(f, GROUP, stride=8), :
            ].astype(BF16)
    left = dot(own_ref[0 : 2 * GROUP, :], block_ref[...])
    mine = jnp.concatenate(
        [
            left[f * GROUP : (f + 1) * GROUP, k * width : (k + 1) * width]
            for f in range(2)
            for k in range(QUAD)
        ],
        axis=0,
    ).astype(BF16)
    for e4 in range(width // 4):
        part = dot(mine, wide_ref[:, e4 * 4 * n : (e4 + 1) * 4 * n]).astype(BF16)
        for el in range(4):
            e = e4 * 4 + el
            for i in range(8):
                m_ref[e * GROUP : (e + 1) * GROUP, i * n : (i + 1) * n] = part[
                    i * GROUP : (i + 1) * GROUP, el * n : (el + 1) * n
                ]
    linear = dot(right, m_ref[...])
    right_ref[...] = dot(m_ref[...], turned[...])
    for t in range(8):
        for s in range(2):
            flat_ref[s * width : (s + 1) * width, t * n : (t + 1) * n] = right_ref[
                pl.ds(2 * t + s, width, stride=GROUP), :
            ].astype(BF16)
    act = sum(dot(flat_ref[:, k * 2 * n : (k + 1) * 2 * n], y[: 2 * n, :]) for k, y in enumerate(ys))
    return linear, act


def half_kernel(
    y0_ref, y1_ref, y2_ref, y3_ref, turned_ref, kron_ref, block_ref, wide_ref, bias_ref,
    linear_ref, act_ref, right_t_ref, own_ref, *scratch
):
    linear, act = half_of_rows(
        (y0_ref, y1_ref, y2_ref, y3_ref), turned_ref, kron_ref, block_ref, wide_ref, right_t_ref, own_ref, scratch
    )
    linear_ref[...] = linear + jnp.concatenate([bias_ref[...]] * 8, axis=1)
    act_ref[...] = act


def pair_kernel(
    y0_ref, y1_ref, y2_ref, y3_ref, turned_ref, kron_ref, block_ref, wide_ref,
    linear_ref, act_ref, slope_ref, pair_ref,
    value_ref, gate_ref, grad_right_ref, right_t_ref, own_ref, slope_s_ref, *scratch
):
    rows, n, _ = pair_ref.shape
    linear, act = half_of_rows(
        (y0_ref, y1_ref, y2_ref, y3_ref), turned_ref, kron_ref, block_ref, wide_ref, right_t_ref, own_ref, scratch
    )
    for i in range(rows):
        value = linear[:, i * n : (i + 1) * n] + linear_ref[:, i * n : (i + 1) * n]
        value_ref[i] = value
        slope_s_ref[i * n : (i + 1) * n, :] = (slope_ref[i] * value).astype(BF16)
    gate_ref[...] = dot(pair_ref[...].reshape(rows * n, n), slope_s_ref[...], LHS_T).astype(BF16)
    act = act + act_ref[...]
    grad_right_ref[...] = act[:32, :64] + act[32:, 64:]


def update_kernel(scale_ref, value_ref, after_ref, update_ref, token_ref):
    token_ref[...] = jnp.zeros_like(token_ref)
    update_ref[...] = (scale_ref[...] * value_ref[...]).astype(BF16)


def add_kernel(own_ref, other_ref, after_ref, out_ref):
    out_ref[...] = (own_ref[...].astype(F32) + other_ref[...].astype(F32)).astype(BF16)


def out_kernel(
    right0_ref, right1_ref, own0_ref, own1_ref, own_ref, core_ref, across_ref, both_ref,
    part_ref, left_ref, gate_ref, grad_right_ref,
    sums_ref, n_ref
):
    n = gate_ref.shape[0]
    chans, width = 64, 32
    half = 8 * GROUP
    grads = ((own_ref, 0), (core_ref, 2), (across_ref, 2), (both_ref, 4))
    for f2, (ref, at) in enumerate(grads):
        grad = jnp.concatenate([ref[(at + k) * n : (at + k + 1) * n, :] for k in range(2)], axis=1)
        for g, right_ref in enumerate((right0_ref, right1_ref)):
            part = dot(right_ref[...], grad).astype(BF16)
            for fl in range(2):
                at = g * half + (f2 * 2 + fl) * GROUP
                for e in range(width):
                    n_ref[at : at + GROUP, e * n : (e + 1) * n] = part[
                        e * GROUP : (e + 1) * GROUP, fl * n : (fl + 1) * n
                    ]
    own_t = jnp.concatenate([own0_ref[...], own1_ref[...]], axis=0).T
    lane = iota((chans, n), 1) // CHANS
    packed = []
    for h in range(width // QUAD):
        whole = dot(own_t, n_ref[:, h * 4 * n : (h + 1) * 4 * n])
        tiles = []
        for el in range(QUAD):
            tile = whole[0:chans, el * n : (el + 1) * n]
            for k in range(1, QUAD):
                tile = jnp.where(
                    lane == k, whole[k * chans : (k + 1) * chans, el * n : (el + 1) * n], tile
                )
            tiles.append(tile)
        packed.append(fold(tiles, lane))
    feat = jnp.concatenate(packed, axis=1)
    coarse = feat.astype(BF16)
    fine = (feat - coarse.astype(F32)).astype(BF16)
    grad_out = dot(left_ref[...], coarse) + dot(left_ref[...], fine)
    for h in range(width // QUAD):
        sums_ref[h * width : (h + 1) * width, :] = grad_out[:, h * n : (h + 1) * n].astype(BF16)
    grad_left = dot(part_ref[...], coarse, RHS_T) + dot(part_ref[...], fine, RHS_T)
    sums_ref[256:384, :] = gate_ref[...]
    sums_ref[384:416, :] = jnp.concatenate([grad_left, grad_right_ref[...]], axis=1).astype(BF16)


def join_kernel(own_ref, beside_ref, across_ref, both_ref, out_ref):
    def pair(a_ref, b_ref, lo, hi):
        return a_ref[lo:hi, :].astype(F32) + b_ref[lo:hi, :].astype(F32)

    out_ref[0:256, :] = pair(own_ref, beside_ref, 0, 256).astype(BF16)
    out_ref[256:512, :] = pair(across_ref, both_ref, 0, 256).astype(BF16)
    out_ref[512:672, :] = (
        pair(own_ref, beside_ref, 256, 416) + pair(across_ref, both_ref, 256, 416)
    ).astype(BF16)


def last_kernel(local_ref, other_ref, out_ref, gate_ref, left_ref, right_ref):
    quad_at = place_in_quad(lax.axis_index("row"))
    n = local_ref.shape[1]
    wide = QUAD * n
    src = iota((wide, wide), 0)
    dst = iota((wide, wide), 1)
    chan = (quad_at ^ (src // n)) * CHANS + src % CHANS
    place = jnp.where(
        (dst // n == (src % n) // CHANS) & (dst % n == chan), 1.0, 0.0
    ).astype(BF16)
    packed = jnp.concatenate(
        [local_ref[0:256, :], other_ref[0:256, :], local_ref[256:512, :], other_ref[256:512, :]], axis=1
    )
    whole = dot(packed, place)
    for h in range(8):
        for el in range(4):
            out_ref[pl.ds(h * 4 + el, 32, stride=32), :] = whole[
                h * 32 : (h + 1) * 32, el * n : (el + 1) * n
            ]
    gate_ref[...] = local_ref[512:640, :].astype(F32) + other_ref[512:640, :].astype(F32)
    both = local_ref[640:672, :].astype(F32) + other_ref[640:672, :].astype(F32)
    left_ref[...] = both[:, 0:64]
    right_ref[...] = both[:, 64:128]


def tie_kernel(*refs):
    out_ref, at = refs[-1], 0
    for ref in refs:
        if at < out_ref.shape[0]:
            out_ref[at : at + ref.shape[0], :] = ref[...]
            at += ref.shape[0]


def call(kernel, shapes, scratch=(), smem=0, ins=0, flops=1 << 20, vmem=4):
    return pl.pallas_call(
        kernel,
        out_shape=[jax.ShapeDtypeStruct(s, d) for s, d in shapes],
        in_specs=[SMEM] * smem + [VMEM] * (ins - smem),
        out_specs=[VMEM] * len(shapes),
        scratch_shapes=[pltpu.VMEM(s, d) for s, d in scratch],
        compiler_params=pltpu.CompilerParams(vmem_limit_bytes=vmem << 20),
        cost_estimate=pl.CostEstimate(flops=flops, bytes_accessed=1 << 20, transcendentals=0),
    )


def swap(x, bit, size):
    return lax.ppermute(x, "row", [(i, i ^ bit) for i in range(size)])


def one_column(
    alignment_state, pair_state, cotangent, sequence_row_mask, residue_mask, norm_gain_vector,
    left_matrix_weight, right_matrix_weight, output_weight, output_bias, gate_matrix,
):
    size = lax.axis_size("row")
    rows, n, _ = pair_state.shape
    res = residue_mask.reshape(1, n)
    seq = sequence_row_mask.reshape(1, -1)
    state = alignment_state.transpose(0, 2, 1)
    near = swap(state, 8, size)
    (token,) = call(first_kernel, [((8, n), F32)], flops=20 << 30)()
    gain = norm_gain_vector.reshape(1, -1)
    bias = output_bias.reshape(1, n)
    scale, slope, turned, own, core, across, gain, bias = call(
        gate_kernel,
        [((rows, n, n), F32), ((rows, n, n), F32), ((rows * n, n), BF16)] + [((2 * n, n), BF16)] * 2
        + [((4 * n, n), BF16), (gain.shape, F32), (bias.shape, F32)],
        scratch=[((n, rows * n), BF16)], smem=1, ins=9, flops=1 << 30, vmem=12,
    )(residue_mask, seq, res, pair_state, cotangent, gate_matrix, gain, bias, token)
    pair, to_core, to_across = call(
        norm_kernel, [((2 * n, n), BF16), ((4 * n, n), BF16), ((6 * n, n), BF16)], smem=1, ins=7
    )(sequence_row_mask, res, gain, state, near, core, across)
    beside, ahead, corner = swap(pair, 2, size), swap(to_across, ACROSS, size), swap(pair, 2 ^ ACROSS, size)
    left_t = left_matrix_weight.T
    kron, block, wide, part = call(
        weight_kernel,
        [((1024, 512), BF16), ((256, n), BF16), ((32, 32 * n), BF16), ((32, 8 * n), BF16)],
        scratch=[((1024, n), F32)], ins=4, flops=1 << 30, vmem=12,
    )(right_matrix_weight.T, left_t, output_weight, pair)
    (beside,) = call(tie_kernel, [((2 * n, n), BF16)], ins=2)(beside, block)
    pair_core, beside_core, corner_core, ahead_core = (
        swap(y, 1, size) for y in (to_core, beside, corner, ahead)
    )
    scratch = [
        ((512, rows * n), BF16), ((2, n, n), F32), ((512, n), F32), ((64, 8 * n), BF16),
    ]
    shared = (turned, kron, block, wide)
    kept = [((512, n), BF16), ((n, 256), BF16)]
    linear, act, right0, own0 = call(
        half_kernel,
        [((n, rows * n), F32), ((64, n), F32), *kept],
        scratch=scratch, ins=9, flops=2 << 30, vmem=24,
    )(pair, pair_core, beside, beside_core, *shared, bias)
    value, gate_sum, right_sum, right1, own1 = call(
        pair_kernel,
        [((rows, n, n), F32), ((n, n), BF16), ((32, 64), F32), *kept],
        scratch=[((rows * n, n), BF16), *scratch], ins=12, flops=2 << 30, vmem=24,
    )(corner, corner_core, ahead, ahead_core, *shared, linear, act, slope, pair_state)
    (sums,) = call(
        out_kernel, [((416, n), BF16)], scratch=[((256, 32 * n), BF16)], ins=12, flops=1 << 30, vmem=24,
    )(right0, right1, own0, own1, own, pair_core, ahead, ahead_core, part, left_t, gate_sum, right_sum)
    update, token = call(update_kernel, [((rows, n, n), BF16), ((8, n), F32)], ins=3, flops=1 << 30, vmem=8)(scale, value, sums)
    (sums,) = call(add_kernel, [((416, n), BF16)], ins=3)(sums, swap(sums, 8, size), token)
    others = [swap(sums, step, size) for step in (2, ACROSS, 2 ^ ACROSS)]
    (local,) = call(join_kernel, [((672, n), BF16)], ins=4)(sums, *others)
    other = swap(local, 1, size)
    grad_out, grad_gate, left, right = call(
        last_kernel,
        [((1024, n), F32), ((n, n), F32), ((32, 64), F32), ((32, 64), F32)],
        ins=2,
    )(local, other)
    return update, left.T, right.T, grad_out, grad_gate


def layer_normalize(alignment_state, norm_gain_vector):
    value_entries = alignment_state.astype(jnp.float32)
    average = jnp.mean(value_entries, axis=-1, keepdims=True)
    centred = value_entries - average
    variance = jnp.mean(centred * centred, axis=-1, keepdims=True)
    return (centred * lax.rsqrt(variance + 1e-05) * norm_gain_vector).astype(jnp.bfloat16)


def any_mesh(
    alignment_state,
    pair_state,
    cotangent,
    sequence_row_mask,
    residue_mask,
    norm_gain_vector,
    left_matrix_weight,
    right_matrix_weight,
    output_weight,
    output_bias,
    gate_matrix,
):
    sequence_resident, column_count, alignment_channel_count = alignment_state.shape
    count_of_rows = pair_state.shape[0]
    pair_chans = pair_state.shape[2]
    projection_width = left_matrix_weight.shape[1]
    every_sequence = sequence_row_mask.shape[0]
    row_at = lax.axis_index("row")
    col_at = lax.axis_index("col")
    number_of_rows = lax.axis_size("row")
    contract_first = (((0,), (0,)), ((), ()))
    contract_second = (((1,), (1,)), ((), ()))
    resident_features = layer_normalize(alignment_state, norm_gain_vector)
    seq_flags = sequence_row_mask.astype(jnp.float32)
    res_flags = residue_mask.astype(jnp.float32)
    my_cols = lax.dynamic_slice_in_dim(res_flags, col_at * column_count, column_count, 0)
    my_rows = lax.dynamic_slice_in_dim(res_flags, row_at * count_of_rows, count_of_rows, 0)
    panel_mask = seq_flags[:, None] * my_rows[None, :]
    column_mask = seq_flags[:, None] * my_cols[None, :]
    broadcast_features = lax.all_gather(
        resident_features.reshape(sequence_resident, column_count * alignment_channel_count),
        "col",
        axis=1,
        tiled=True,
    )
    row_portions = broadcast_features.reshape(
        sequence_resident, number_of_rows, count_of_rows * alignment_channel_count
    )
    row_feats = lax.all_to_all(
        row_portions, "row", split_axis=1, concat_axis=0, tiled=True
    ).reshape(every_sequence * count_of_rows, alignment_channel_count)
    left_panel = (
        jnp.dot(row_feats, left_matrix_weight, preferred_element_type=jnp.float32).reshape(
            every_sequence, count_of_rows, projection_width
        )
        * panel_mask[:, :, None]
    ).astype(jnp.bfloat16)
    left_matrix = left_panel.transpose(1, 2, 0).reshape(
        count_of_rows * projection_width, every_sequence
    )
    column_features = lax.all_gather(
        resident_features.reshape(sequence_resident, column_count * alignment_channel_count),
        "row",
        axis=0,
        tiled=True,
    ).reshape(every_sequence, column_count, alignment_channel_count)
    right_panel = (
        jnp.dot(
            column_features.reshape(every_sequence * column_count, alignment_channel_count),
            right_matrix_weight,
            preferred_element_type=jnp.float32,
        ).reshape(every_sequence, column_count, projection_width)
        * column_mask[:, :, None]
    ).astype(jnp.bfloat16)
    surplus_offset = jnp.zeros((alignment_channel_count, projection_width), jnp.float32)

    def absorb(extra, first_col, width_columns, right_part):
        feat_blk = (
            lax.dynamic_slice_in_dim(column_features, first_col, width_columns, 1)
            .reshape(every_sequence * width_columns, alignment_channel_count)
            .astype(jnp.float32)
        )
        mask_blk = lax.dynamic_slice_in_dim(column_mask, first_col, width_columns, 1)
        masked_part = (
            right_part.reshape(every_sequence, width_columns, projection_width)
            * mask_blk[:, :, None]
        ).reshape(every_sequence * width_columns, projection_width)
        return extra + jnp.dot(feat_blk.T, masked_part, precision=lax.Precision.HIGHEST)

    right_flat = right_panel.reshape(every_sequence, column_count * projection_width)
    row_total = jnp.sum(seq_flags)
    col_block = 128
    n_blocks = column_count // col_block

    def one_block(block_idx, carry):
        new_update, grad_out, grad_gate, left_acc, extra = carry
        first_col = block_idx * col_block
        right_blk = lax.dynamic_slice_in_dim(
            right_flat, first_col * projection_width, col_block * projection_width, 1
        )
        outer_prod = jnp.dot(left_matrix, right_blk, preferred_element_type=jnp.float32)
        outer_prod = outer_prod.reshape(
            count_of_rows, projection_width, col_block, projection_width
        ).transpose(0, 2, 1, 3)
        outer_prod = outer_prod.reshape(
            count_of_rows * col_block, projection_width * projection_width
        ).astype(jnp.bfloat16)
        linear = (
            jnp.dot(outer_prod, output_weight, preferred_element_type=jnp.float32) + output_bias
        )
        pair_blk = lax.dynamic_slice_in_dim(pair_state, first_col, col_block, 1).reshape(
            count_of_rows * col_block, pair_chans
        )
        gate_val = jax.nn.sigmoid(
            jnp.dot(pair_blk, gate_matrix, preferred_element_type=jnp.float32)
        )
        blk_flags = lax.dynamic_slice_in_dim(my_cols, first_col, col_block, 0)
        divisor = jnp.maximum(row_total * my_rows[:, None] * blk_flags[None, :], 1.0).reshape(
            count_of_rows * col_block, 1
        )
        cot_blk = (
            lax.dynamic_slice_in_dim(cotangent, first_col, col_block, 1)
            .reshape(count_of_rows * col_block, pair_chans)
            .astype(jnp.float32)
        )
        new_pair = (gate_val * linear / divisor).astype(jnp.bfloat16)
        new_update = lax.dynamic_update_slice_in_dim(
            new_update, new_pair.reshape(count_of_rows, col_block, pair_chans), first_col, 1
        )
        grad_lin = (cot_blk * gate_val / divisor).astype(jnp.bfloat16)
        grad_pre = (cot_blk * linear / divisor * gate_val * (1.0 - gate_val)).astype(jnp.bfloat16)
        grad_out = grad_out + lax.dot_general(
            outer_prod, grad_lin, contract_first, preferred_element_type=jnp.float32
        )
        grad_gate = grad_gate + lax.dot_general(
            pair_blk, grad_pre, contract_first, preferred_element_type=jnp.float32
        )
        grad_outer = lax.dot_general(
            grad_lin, output_weight, contract_second, preferred_element_type=jnp.float32
        ).astype(jnp.bfloat16)
        outer_turned = (
            grad_outer.reshape(count_of_rows, col_block, projection_width, projection_width)
            .transpose(0, 2, 1, 3)
            .reshape(count_of_rows * projection_width, col_block * projection_width)
        )
        left_acc = left_acc + lax.dot_general(
            outer_turned, right_blk, contract_second, preferred_element_type=jnp.float32
        )
        right_part = lax.dot_general(
            left_matrix, outer_turned, contract_first, preferred_element_type=jnp.float32
        )
        extra = absorb(extra, first_col, col_block, right_part)
        return (new_update, grad_out, grad_gate, left_acc, extra)

    start_carry = (
        jnp.zeros((count_of_rows, column_count, pair_chans), jnp.bfloat16),
        jnp.zeros((projection_width * projection_width, pair_chans), jnp.float32),
        jnp.zeros((pair_chans, pair_chans), jnp.float32),
        jnp.zeros((count_of_rows * projection_width, every_sequence), jnp.float32),
        surplus_offset,
    )
    new_update, grad_out, grad_gate, left_acc, extra = lax.fori_loop(
        0, n_blocks, one_block, start_carry
    )
    grad_left_act = (
        left_acc.reshape(count_of_rows, projection_width, every_sequence).transpose(2, 0, 1)
        * panel_mask[:, :, None]
    )
    grad_left = jnp.dot(
        row_feats.astype(jnp.float32).T,
        grad_left_act.reshape(every_sequence * count_of_rows, projection_width),
        precision=lax.Precision.HIGHEST,
    )
    summed_left, summed_right, summed_out, summed_gate = lax.psum(
        (grad_left, extra, grad_out, grad_gate), ("row", "col")
    )
    return (new_update, summed_left, summed_right, summed_out, summed_gate)


def per_device(*args):
    alignment_state, pair_state = args[0], args[1]
    fits = (
        lax.axis_size("col") == 1
        and lax.axis_size("row") == 16
        and alignment_state.shape == (2, 128, 64)
        and pair_state.shape == (8, 128, 128)
    )
    return one_column(*args) if fits else any_mesh(*args)


def solution(mesh):
    return jax.shard_map(
        per_device,
        mesh=mesh,
        in_specs=(
            P(("grp", "row"), "col", None),
            P(("grp", "row"), "col", None),
            P(("grp", "row"), "col", None),
            P("grp"),
            P("grp"),
            P(),
            P(),
            P(),
            P(),
            P(),
            P(),
        ),
        out_specs=(
            P(("grp", "row"), "col", None),
            P("grp", None),
            P("grp", None),
            P("grp", None),
            P("grp", None),
        ),
        check_vma=False,
    )
```

```python
import functools

import jax
import jax.numpy as jnp
from jax import lax
from jax.experimental import pallas as pl
from jax.experimental.pallas import tpu as pltpu
from jax.sharding import PartitionSpec as P

F32 = jnp.float32
BF16 = jnp.bfloat16
VMEM = pl.BlockSpec(memory_space=pltpu.VMEM)
SMEM = pl.BlockSpec(memory_space=pltpu.SMEM)
LHS_T = (((0,), (0,)), ((), ()))
RHS_T = (((1,), (1,)), ((), ()))
QUAD = 4
ACROSS = 4
CHANS = 32
GROUP = 16


def iota(shape, dim):
    return lax.broadcasted_iota(jnp.int32, shape, dim)


def dot(a, b, dims=(((1,), (0,)), ((), ())), **kw):
    return lax.dot_general(a, b, dims, preferred_element_type=F32, **kw)


def place_in_quad(row):
    return row % 2 + row // ACROSS % 2 * 2


def first_kernel(out_ref):
    out_ref[...] = jnp.zeros_like(out_ref)


def norm_kernel(
    seq_ref, res_ref, gain_ref, own_ref, near_ref, core_ref, across_ref, out_ref, to_core_ref, to_across_ref
):
    row = lax.axis_index("row")
    n = res_ref.shape[1]
    res = res_ref[...].astype(F32)
    gain = gain_ref[...]
    gain = jnp.concatenate([gain, gain], axis=1)
    for at, (state_ref, first) in enumerate(((own_ref, row * 2), (near_ref, (row ^ 8) * 2))):
        halves = []
        for s in range(2):
            value = state_ref[s].astype(F32)
            centred = value - jnp.mean(value, axis=0, keepdims=True)
            variance = jnp.mean(centred * centred, axis=0, keepdims=True)
            seq = seq_ref[first + s].astype(F32)
            halves.append(centred * (lax.rsqrt(variance + 1e-05) * (res * seq)))
        turned = jnp.concatenate(halves, axis=0).T
        value = (turned * gain).astype(BF16)
        for ref in (out_ref, to_core_ref, to_across_ref):
            ref[at * n : (at + 1) * n, :] = value
    to_core_ref[2 * n :, :] = core_ref[...]
    to_across_ref[2 * n :, :] = across_ref[...]


def gate_kernel(
    res_s_ref, seq_ref, res_ref, pair_ref, cot_ref, gate_ref, gain_ref, bias_ref, after_ref,
    scale_ref, slope_ref, turned_ref, own_ref, core_ref, across_ref, gain_out_ref, bias_out_ref,
    full_ref,
):
    gain_out_ref[...] = gain_ref[...]
    bias_out_ref[...] = bias_ref[...]
    row = lax.axis_index("row")
    quad_at = place_in_quad(row)
    rows = pair_ref.shape[0]
    n = res_ref.shape[1]
    total = jnp.sum(seq_ref[...].astype(F32), axis=1, keepdims=True)
    eye = iota((n, n), 0) == iota((n, n), 1)
    res_col = jnp.sum(jnp.where(eye, res_ref[...].astype(F32), 0.0), axis=1, keepdims=True)
    wide = QUAD * n
    src = iota((wide, wide), 0)
    dst = iota((wide, wide), 1)
    slot = dst // n
    chan = (quad_at ^ slot) * CHANS + dst % CHANS
    place = jnp.where(
        (src // n == (dst % n) // CHANS) & (src % n == chan), 1.0, 0.0
    ).astype(BF16)
    outs = ((own_ref, 0), (core_ref, 0), (across_ref, 0), (across_ref, 2))
    for half in range(rows // QUAD):
        for k in range(QUAD):
            i = half * QUAD + k
            gate = jax.nn.sigmoid(dot(pair_ref[i], gate_ref[...]))
            res_row = res_s_ref[row * rows + i].astype(F32)
            scale = gate / jnp.maximum(total * res_row * res_col, 1.0)
            lin = cot_ref[i].astype(F32) * scale
            scale_ref[i] = scale
            slope_ref[i] = lin * (1.0 - gate)
            full_ref[:, i * n : (i + 1) * n] = lin.astype(BF16)
            turned_ref[i * n : (i + 1) * n, :] = lin.T.astype(BF16)
        packed = dot(full_ref[:, half * wide : (half + 1) * wide], place).astype(BF16)
        for m in range(QUAD):
            out_ref, at = outs[m]
            out_ref[(at + half) * n : (at + half + 1) * n, :] = packed[:, m * n : (m + 1) * n]


def weight_kernel(
    right_ref, left_ref, out_w_ref, after_ref,
    kron_ref, block_ref, wide_ref, part_ref, wf_ref,
):
    quad_at = place_in_quad(lax.axis_index("row"))
    width, chans = right_ref.shape
    n = out_w_ref.shape[1]
    cols = width * GROUP
    spread = jnp.where(iota((width, cols), 0) == iota((width, cols), 1) // GROUP, 1.0, 0.0)
    repeated = dot(right_ref[...], spread.astype(BF16), LHS_T)
    lane = iota((chans, cols), 1) % GROUP
    for s in range(GROUP):
        kron_ref[s * chans : (s + 1) * chans, :] = jnp.where(lane == s, repeated, 0.0).astype(BF16)
    spread = jnp.where(iota((width, n), 0) == iota((width, n), 1) % width, 1.0, 0.0)
    repeated = dot(left_ref[...], spread.astype(BF16), LHS_T)
    lane = iota((chans, n), 1) // width
    for k in range(QUAD):
        block_ref[k * chans : (k + 1) * chans, :] = jnp.where(lane == k, repeated, 0.0).astype(BF16)
    wf_ref[...] = out_w_ref[...].astype(F32)
    for e in range(width):
        wide_ref[:, e * n : (e + 1) * n] = wf_ref[pl.ds(e, width, stride=width), :].astype(BF16)
    pick = jnp.where(
        iota((n, n), 0) == quad_at * CHANS + iota((n, n), 1) % CHANS, 1.0, 0.0
    ).astype(BF16)
    wf_ref[...] = dot(out_w_ref[...], pick)
    lane = iota((width, n), 1) // CHANS
    for h in range(width // QUAD):
        tile = None
        for k in range(QUAD):
            rows = wf_ref[pl.ds(h * QUAD + k, width, stride=width), :]
            tile = rows if tile is None else jnp.where(lane == k, rows, tile)
        part_ref[:, h * n : (h + 1) * n] = tile.astype(BF16)


def fold(tiles, lane):
    high, low = lane // 2 == 0, lane % 2 == 0
    pairs = [
        jnp.where(high, tiles[k], tiles[k + 2])
        + pltpu.roll(jnp.where(high, tiles[k + 2], tiles[k]), 2 * CHANS, 1)
        for k in range(2)
    ]
    other = jnp.where(low, pairs[1], pairs[0])
    size = lane.shape[1]
    other = jnp.where(low, pltpu.roll(other, size - CHANS, 1), pltpu.roll(other, CHANS, 1))
    return jnp.where(low, pairs[0], pairs[1]) + other


def half_of_rows(ys, turned, kron_ref, block_ref, wide_ref, right_t_ref, own_ref, scratch):
    m_ref, turn_ref, right_ref, flat_ref = scratch
    row = lax.axis_index("row")
    n = ys[0].shape[1]
    chans, width = 64, 32
    slots = [y[t * n : (t + 1) * n, :] for y in ys for t in range(2)]
    right = dot(jnp.concatenate(slots, axis=1), kron_ref[...]).astype(BF16)
    right_t_ref[...] = right.T
    at = iota((32, n), 0)
    four = at % 8
    member = four // 2
    here = (row ^ (member % 2 + member // 2 * ACROSS)) * 8 + (four % 2) * QUAD + at // 8
    pick = jnp.where(iota((32, n), 1) == here, 1.0, 0.0).astype(BF16)
    for t, slot in enumerate(slots):
        picked = dot(pick, slot)
        for s in range(2):
            at = (2 * t + s) * 8
            for half in range(2):
                turn_ref[half, at : at + 8, :] = jnp.concatenate(
                    [
                        picked[k * 8 : (k + 1) * 8, s * chans : (s + 1) * chans]
                        for k in (2 * half, 2 * half + 1)
                    ],
                    axis=1,
                )
    for f in range(8):
        for half in range(2):
            own_ref[f * GROUP : (f + 1) * GROUP, half * n : (half + 1) * n] = turn_ref[
                half, pl.ds(f, GROUP, stride=8), :
            ].astype(BF16)
    left = dot(own_ref[0 : 2 * GROUP, :], block_ref[...])
    mine = jnp.concatenate(
        [
            left[f * GROUP : (f + 1) * GROUP, k * width : (k + 1) * width]
            for f in range(2)
            for k in range(QUAD)
        ],
        axis=0,
    ).astype(BF16)
    for e4 in range(width // 4):
        part = dot(mine, wide_ref[:, e4 * 4 * n : (e4 + 1) * 4 * n]).astype(BF16)
        for el in range(4):
            e = e4 * 4 + el
            for i in range(8):
                m_ref[e * GROUP : (e + 1) * GROUP, i * n : (i + 1) * n] = part[
                    i * GROUP : (i + 1) * GROUP, el * n : (el + 1) * n
                ]
    linear = dot(right, m_ref[...])
    right_ref[...] = dot(m_ref[...], turned[...])
    for t in range(8):
        for s in range(2):
            flat_ref[s * width : (s + 1) * width, t * n : (t + 1) * n] = right_ref[
                pl.ds(2 * t + s, width, stride=GROUP), :
            ].astype(BF16)
    act = sum(dot(flat_ref[:, k * 2 * n : (k + 1) * 2 * n], y[: 2 * n, :]) for k, y in enumerate(ys))
    return linear, act


def half_kernel(
    y0_ref, y1_ref, y2_ref, y3_ref, turned_ref, kron_ref, block_ref, wide_ref, bias_ref,
    linear_ref, act_ref, right_t_ref, own_ref, *scratch
):
    linear, act = half_of_rows(
        (y0_ref, y1_ref, y2_ref, y3_ref), turned_ref, kron_ref, block_ref, wide_ref, right_t_ref, own_ref, scratch
    )
    linear_ref[...] = linear + jnp.concatenate([bias_ref[...]] * 8, axis=1)
    act_ref[...] = act


def pair_kernel(
    y0_ref, y1_ref, y2_ref, y3_ref, turned_ref, kron_ref, block_ref, wide_ref,
    linear_ref, act_ref, slope_ref, pair_ref,
    value_ref, keep_ref, send_ref, grad_right_ref, right_t_ref, own_ref, slope_s_ref, *scratch
):
    rows, n, _ = pair_ref.shape
    linear, act = half_of_rows(
        (y0_ref, y1_ref, y2_ref, y3_ref), turned_ref, kron_ref, block_ref, wide_ref, right_t_ref, own_ref, scratch
    )
    for i in range(rows):
        value = linear[:, i * n : (i + 1) * n] + linear_ref[:, i * n : (i + 1) * n]
        value_ref[i] = value
        slope_s_ref[i * n : (i + 1) * n, :] = (slope_ref[i] * value).astype(BF16)
    grad_gate = dot(pair_ref[...].reshape(rows * n, n), slope_s_ref[...], LHS_T)
    halves = grad_gate[: n // 2, :], grad_gate[n // 2 :, :]
    first_core = lax.axis_index("row") % 2 == 0
    keep_ref[...] = jnp.where(first_core, halves[0], halves[1]).astype(BF16)
    send_ref[...] = jnp.where(first_core, halves[1], halves[0]).astype(BF16)
    act = act + act_ref[...]
    grad_right_ref[...] = act[:32, :64] + act[32:, 64:]


def update_kernel(scale_ref, value_ref, after_ref, update_ref, token_ref):
    token_ref[...] = jnp.zeros_like(token_ref)
    update_ref[...] = (scale_ref[...] * value_ref[...]).astype(BF16)


def chip_kernel(sums_ref, keep_ref, other_ref, out_ref):
    out_ref[0:288, :] = sums_ref[...]
    out_ref[288:352, :] = (keep_ref[...].astype(F32) + other_ref[...].astype(F32)).astype(BF16)


def add_kernel(own_ref, other_ref, after_ref, out_ref):
    out_ref[...] = (own_ref[...].astype(F32) + other_ref[...].astype(F32)).astype(BF16)


def out_kernel(
    right0_ref, right1_ref, own0_ref, own1_ref, own_ref, core_ref, across_ref, both_ref,
    part_ref, left_ref, grad_right_ref,
    sums_ref, n_ref
):
    n = sums_ref.shape[1]
    chans, width = 64, 32
    half = 8 * GROUP
    grads = ((own_ref, 0), (core_ref, 2), (across_ref, 2), (both_ref, 4))
    for f2, (ref, at) in enumerate(grads):
        grad = jnp.concatenate([ref[(at + k) * n : (at + k + 1) * n, :] for k in range(2)], axis=1)
        for g, right_ref in enumerate((right0_ref, right1_ref)):
            part = dot(right_ref[...], grad).astype(BF16)
            for fl in range(2):
                at = g * half + (f2 * 2 + fl) * GROUP
                for e in range(width):
                    n_ref[at : at + GROUP, e * n : (e + 1) * n] = part[
                        e * GROUP : (e + 1) * GROUP, fl * n : (fl + 1) * n
                    ]
    own_t = jnp.concatenate([own0_ref[...], own1_ref[...]], axis=0).T
    lane = iota((chans, n), 1) // CHANS
    packed = []
    for h in range(width // QUAD):
        whole = dot(own_t, n_ref[:, h * 4 * n : (h + 1) * 4 * n])
        tiles = []
        for el in range(QUAD):
            tile = whole[0:chans, el * n : (el + 1) * n]
            for k in range(1, QUAD):
                tile = jnp.where(
                    lane == k, whole[k * chans : (k + 1) * chans, el * n : (el + 1) * n], tile
                )
            tiles.append(tile)
        packed.append(fold(tiles, lane))
    feat = jnp.concatenate(packed, axis=1)
    coarse = feat.astype(BF16)
    fine = (feat - coarse.astype(F32)).astype(BF16)
    grad_out = dot(left_ref[...], coarse) + dot(left_ref[...], fine)
    for h in range(width // QUAD):
        sums_ref[h * width : (h + 1) * width, :] = grad_out[:, h * n : (h + 1) * n].astype(BF16)
    grad_left = dot(part_ref[...], coarse, RHS_T) + dot(part_ref[...], fine, RHS_T)
    sums_ref[256:288, :] = jnp.concatenate([grad_left, grad_right_ref[...]], axis=1).astype(BF16)


def join_kernel(own_ref, beside_ref, across_ref, both_ref, out_ref):
    def pair(a_ref, b_ref, lo, hi):
        return a_ref[lo:hi, :].astype(F32) + b_ref[lo:hi, :].astype(F32)

    out_ref[0:256, :] = pair(own_ref, beside_ref, 0, 256).astype(BF16)
    out_ref[256:512, :] = pair(across_ref, both_ref, 0, 256).astype(BF16)
    out_ref[512:608, :] = (
        pair(own_ref, beside_ref, 256, 352) + pair(across_ref, both_ref, 256, 352)
    ).astype(BF16)


def last_kernel(local_ref, other_ref, out_ref, gate_ref, left_ref, right_ref):
    row = lax.axis_index("row")
    quad_at = place_in_quad(row)
    n = local_ref.shape[1]
    wide = QUAD * n
    src = iota((wide, wide), 0)
    dst = iota((wide, wide), 1)
    chan = (quad_at ^ (src // n)) * CHANS + src % CHANS
    place = jnp.where(
        (dst // n == (src % n) // CHANS) & (dst % n == chan), 1.0, 0.0
    ).astype(BF16)
    packed = jnp.concatenate(
        [local_ref[0:256, :], other_ref[0:256, :], local_ref[256:512, :], other_ref[256:512, :]], axis=1
    )
    whole = dot(packed, place)
    for h in range(8):
        for el in range(4):
            out_ref[pl.ds(h * 4 + el, 32, stride=32), :] = whole[
                h * 32 : (h + 1) * 32, el * n : (el + 1) * n
            ]
    both = local_ref[512:544, :].astype(F32) + other_ref[512:544, :].astype(F32)
    left_ref[...] = both[:, 0:64]
    right_ref[...] = both[:, 64:128]
    halves = local_ref[544:608, :].astype(F32), other_ref[544:608, :].astype(F32)
    gate_ref[: n // 2, :] = jnp.where(row % 2 == 0, halves[0], halves[1])
    gate_ref[n // 2 :, :] = jnp.where(row % 2 == 0, halves[1], halves[0])


def tie_kernel(*refs):
    out_ref, at = refs[-1], 0
    for ref in refs:
        if at < out_ref.shape[0]:
            out_ref[at : at + ref.shape[0], :] = ref[...]
            at += ref.shape[0]


def call(kernel, shapes, scratch=(), smem=0, ins=0, flops=1 << 20, vmem=4):
    return pl.pallas_call(
        kernel,
        out_shape=[jax.ShapeDtypeStruct(s, d) for s, d in shapes],
        in_specs=[SMEM] * smem + [VMEM] * (ins - smem),
        out_specs=[VMEM] * len(shapes),
        scratch_shapes=[pltpu.VMEM(s, d) for s, d in scratch],
        compiler_params=pltpu.CompilerParams(vmem_limit_bytes=vmem << 20),
        cost_estimate=pl.CostEstimate(flops=flops, bytes_accessed=1 << 20, transcendentals=0),
    )


def swap(x, bit, size):
    return lax.ppermute(x, "row", [(i, i ^ bit) for i in range(size)])


def one_column(
    alignment_state, pair_state, cotangent, sequence_row_mask, residue_mask, norm_gain_vector,
    left_matrix_weight, right_matrix_weight, output_weight, output_bias, gate_matrix,
):
    size = lax.axis_size("row")
    rows, n, _ = pair_state.shape
    res = residue_mask.reshape(1, n)
    seq = sequence_row_mask.reshape(1, -1)
    state = alignment_state.transpose(0, 2, 1)
    near = swap(state, 8, size)
    (token,) = call(first_kernel, [((8, n), F32)], flops=20 << 30)()
    gain = norm_gain_vector.reshape(1, -1)
    bias = output_bias.reshape(1, n)
    scale, slope, turned, own, core, across, gain, bias = call(
        gate_kernel,
        [((rows, n, n), F32), ((rows, n, n), F32), ((rows * n, n), BF16)] + [((2 * n, n), BF16)] * 2
        + [((4 * n, n), BF16), (gain.shape, F32), (bias.shape, F32)],
        scratch=[((n, rows * n), BF16)], smem=1, ins=9, flops=1 << 30, vmem=12,
    )(residue_mask, seq, res, pair_state, cotangent, gate_matrix, gain, bias, token)
    pair, to_core, to_across = call(
        norm_kernel, [((2 * n, n), BF16), ((4 * n, n), BF16), ((6 * n, n), BF16)], smem=1, ins=7
    )(sequence_row_mask, res, gain, state, near, core, across)
    beside, ahead, corner = swap(pair, 2, size), swap(to_across, ACROSS, size), swap(pair, 2 ^ ACROSS, size)
    left_t = left_matrix_weight.T
    kron, block, wide, part = call(
        weight_kernel,
        [((1024, 512), BF16), ((256, n), BF16), ((32, 32 * n), BF16), ((32, 8 * n), BF16)],
        scratch=[((1024, n), F32)], ins=4, flops=1 << 30, vmem=12,
    )(right_matrix_weight.T, left_t, output_weight, pair)
    (beside,) = call(tie_kernel, [((2 * n, n), BF16)], ins=2)(beside, block)
    pair_core, beside_core, corner_core, ahead_core = (
        swap(y, 1, size) for y in (to_core, beside, corner, ahead)
    )
    scratch = [
        ((512, rows * n), BF16), ((2, n, n), F32), ((512, n), F32), ((64, 8 * n), BF16),
    ]
    shared = (turned, kron, block, wide)
    kept = [((512, n), BF16), ((n, 256), BF16)]
    linear, act, right0, own0 = call(
        half_kernel,
        [((n, rows * n), F32), ((64, n), F32), *kept],
        scratch=scratch, ins=9, flops=2 << 30, vmem=24,
    )(pair, pair_core, beside, beside_core, *shared, bias)
    value, keep, send, right_sum, right1, own1 = call(
        pair_kernel,
        [((rows, n, n), F32), ((n // 2, n), BF16), ((n // 2, n), BF16), ((32, 64), F32), *kept],
        scratch=[((rows * n, n), BF16), *scratch], ins=12, flops=2 << 30, vmem=24,
    )(corner, corner_core, ahead, ahead_core, *shared, linear, act, slope, pair_state)
    (sums,) = call(
        out_kernel, [((288, n), BF16)], scratch=[((256, 32 * n), BF16)], ins=11, flops=1 << 30, vmem=24,
    )(right0, right1, own0, own1, own, pair_core, ahead, ahead_core, part, left_t, right_sum)
    (sums,) = call(chip_kernel, [((352, n), BF16)], ins=3)(sums, keep, swap(send, 1, size))
    update, token = call(update_kernel, [((rows, n, n), BF16), ((8, n), F32)], ins=3, flops=1 << 30, vmem=8)(scale, value, sums)
    (sums,) = call(add_kernel, [((352, n), BF16)], ins=3)(sums, swap(sums, 8, size), token)
    others = [swap(sums, step, size) for step in (2, ACROSS, 2 ^ ACROSS)]
    (local,) = call(join_kernel, [((608, n), BF16)], ins=4)(sums, *others)
    other = swap(local, 1, size)
    grad_out, grad_gate, left, right = call(
        last_kernel,
        [((1024, n), F32), ((n, n), F32), ((32, 64), F32), ((32, 64), F32)],
        ins=2,
    )(local, other)
    return update, left.T, right.T, grad_out, grad_gate


def layer_normalize(alignment_state, norm_gain_vector):
    value_entries = alignment_state.astype(jnp.float32)
    average = jnp.mean(value_entries, axis=-1, keepdims=True)
    centred = value_entries - average
    variance = jnp.mean(centred * centred, axis=-1, keepdims=True)
    return (centred * lax.rsqrt(variance + 1e-05) * norm_gain_vector).astype(jnp.bfloat16)


def any_mesh(
    alignment_state,
    pair_state,
    cotangent,
    sequence_row_mask,
    residue_mask,
    norm_gain_vector,
    left_matrix_weight,
    right_matrix_weight,
    output_weight,
    output_bias,
    gate_matrix,
):
    sequence_resident, column_count, alignment_channel_count = alignment_state.shape
    count_of_rows = pair_state.shape[0]
    pair_chans = pair_state.shape[2]
    projection_width = left_matrix_weight.shape[1]
    every_sequence = sequence_row_mask.shape[0]
    row_at = lax.axis_index("row")
    col_at = lax.axis_index("col")
    number_of_rows = lax.axis_size("row")
    contract_first = (((0,), (0,)), ((), ()))
    contract_second = (((1,), (1,)), ((), ()))
    resident_features = layer_normalize(alignment_state, norm_gain_vector)
    seq_flags = sequence_row_mask.astype(jnp.float32)
    res_flags = residue_mask.astype(jnp.float32)
    my_cols = lax.dynamic_slice_in_dim(res_flags, col_at * column_count, column_count, 0)
    my_rows = lax.dynamic_slice_in_dim(res_flags, row_at * count_of_rows, count_of_rows, 0)
    panel_mask = seq_flags[:, None] * my_rows[None, :]
    column_mask = seq_flags[:, None] * my_cols[None, :]
    broadcast_features = lax.all_gather(
        resident_features.reshape(sequence_resident, column_count * alignment_channel_count),
        "col",
        axis=1,
        tiled=True,
    )
    row_portions = broadcast_features.reshape(
        sequence_resident, number_of_rows, count_of_rows * alignment_channel_count
    )
    row_feats = lax.all_to_all(
        row_portions, "row", split_axis=1, concat_axis=0, tiled=True
    ).reshape(every_sequence * count_of_rows, alignment_channel_count)
    left_panel = (
        jnp.dot(row_feats, left_matrix_weight, preferred_element_type=jnp.float32).reshape(
            every_sequence, count_of_rows, projection_width
        )
        * panel_mask[:, :, None]
    ).astype(jnp.bfloat16)
    left_matrix = left_panel.transpose(1, 2, 0).reshape(
        count_of_rows * projection_width, every_sequence
    )
    column_features = lax.all_gather(
        resident_features.reshape(sequence_resident, column_count * alignment_channel_count),
        "row",
        axis=0,
        tiled=True,
    ).reshape(every_sequence, column_count, alignment_channel_count)
    right_panel = (
        jnp.dot(
            column_features.reshape(every_sequence * column_count, alignment_channel_count),
            right_matrix_weight,
            preferred_element_type=jnp.float32,
        ).reshape(every_sequence, column_count, projection_width)
        * column_mask[:, :, None]
    ).astype(jnp.bfloat16)
    surplus_offset = jnp.zeros((alignment_channel_count, projection_width), jnp.float32)

    def absorb(extra, first_col, width_columns, right_part):
        feat_blk = (
            lax.dynamic_slice_in_dim(column_features, first_col, width_columns, 1)
            .reshape(every_sequence * width_columns, alignment_channel_count)
            .astype(jnp.float32)
        )
        mask_blk = lax.dynamic_slice_in_dim(column_mask, first_col, width_columns, 1)
        masked_part = (
            right_part.reshape(every_sequence, width_columns, projection_width)
            * mask_blk[:, :, None]
        ).reshape(every_sequence * width_columns, projection_width)
        return extra + jnp.dot(feat_blk.T, masked_part, precision=lax.Precision.HIGHEST)

    right_flat = right_panel.reshape(every_sequence, column_count * projection_width)
    row_total = jnp.sum(seq_flags)
    col_block = 128
    n_blocks = column_count // col_block

    def one_block(block_idx, carry):
        new_update, grad_out, grad_gate, left_acc, extra = carry
        first_col = block_idx * col_block
        right_blk = lax.dynamic_slice_in_dim(
            right_flat, first_col * projection_width, col_block * projection_width, 1
        )
        outer_prod = jnp.dot(left_matrix, right_blk, preferred_element_type=jnp.float32)
        outer_prod = outer_prod.reshape(
            count_of_rows, projection_width, col_block, projection_width
        ).transpose(0, 2, 1, 3)
        outer_prod = outer_prod.reshape(
            count_of_rows * col_block, projection_width * projection_width
        ).astype(jnp.bfloat16)
        linear = (
            jnp.dot(outer_prod, output_weight, preferred_element_type=jnp.float32) + output_bias
        )
        pair_blk = lax.dynamic_slice_in_dim(pair_state, first_col, col_block, 1).reshape(
            count_of_rows * col_block, pair_chans
        )
        gate_val = jax.nn.sigmoid(
            jnp.dot(pair_blk, gate_matrix, preferred_element_type=jnp.float32)
        )
        blk_flags = lax.dynamic_slice_in_dim(my_cols, first_col, col_block, 0)
        divisor = jnp.maximum(row_total * my_rows[:, None] * blk_flags[None, :], 1.0).reshape(
            count_of_rows * col_block, 1
        )
        cot_blk = (
            lax.dynamic_slice_in_dim(cotangent, first_col, col_block, 1)
            .reshape(count_of_rows * col_block, pair_chans)
            .astype(jnp.float32)
        )
        new_pair = (gate_val * linear / divisor).astype(jnp.bfloat16)
        new_update = lax.dynamic_update_slice_in_dim(
            new_update, new_pair.reshape(count_of_rows, col_block, pair_chans), first_col, 1
        )
        grad_lin = (cot_blk * gate_val / divisor).astype(jnp.bfloat16)
        grad_pre = (cot_blk * linear / divisor * gate_val * (1.0 - gate_val)).astype(jnp.bfloat16)
        grad_out = grad_out + lax.dot_general(
            outer_prod, grad_lin, contract_first, preferred_element_type=jnp.float32
        )
        grad_gate = grad_gate + lax.dot_general(
            pair_blk, grad_pre, contract_first, preferred_element_type=jnp.float32
        )
        grad_outer = lax.dot_general(
            grad_lin, output_weight, contract_second, preferred_element_type=jnp.float32
        ).astype(jnp.bfloat16)
        outer_turned = (
            grad_outer.reshape(count_of_rows, col_block, projection_width, projection_width)
            .transpose(0, 2, 1, 3)
            .reshape(count_of_rows * projection_width, col_block * projection_width)
        )
        left_acc = left_acc + lax.dot_general(
            outer_turned, right_blk, contract_second, preferred_element_type=jnp.float32
        )
        right_part = lax.dot_general(
            left_matrix, outer_turned, contract_first, preferred_element_type=jnp.float32
        )
        extra = absorb(extra, first_col, col_block, right_part)
        return (new_update, grad_out, grad_gate, left_acc, extra)

    start_carry = (
        jnp.zeros((count_of_rows, column_count, pair_chans), jnp.bfloat16),
        jnp.zeros((projection_width * projection_width, pair_chans), jnp.float32),
        jnp.zeros((pair_chans, pair_chans), jnp.float32),
        jnp.zeros((count_of_rows * projection_width, every_sequence), jnp.float32),
        surplus_offset,
    )
    new_update, grad_out, grad_gate, left_acc, extra = lax.fori_loop(
        0, n_blocks, one_block, start_carry
    )
    grad_left_act = (
        left_acc.reshape(count_of_rows, projection_width, every_sequence).transpose(2, 0, 1)
        * panel_mask[:, :, None]
    )
    grad_left = jnp.dot(
        row_feats.astype(jnp.float32).T,
        grad_left_act.reshape(every_sequence * count_of_rows, projection_width),
        precision=lax.Precision.HIGHEST,
    )
    summed_left, summed_right, summed_out, summed_gate = lax.psum(
        (grad_left, extra, grad_out, grad_gate), ("row", "col")
    )
    return (new_update, summed_left, summed_right, summed_out, summed_gate)


def per_device(*args):
    alignment_state, pair_state = args[0], args[1]
    fits = (
        lax.axis_size("col") == 1
        and lax.axis_size("row") == 16
        and alignment_state.shape == (2, 128, 64)
        and pair_state.shape == (8, 128, 128)
    )
    return one_column(*args) if fits else any_mesh(*args)


def solution(mesh):
    return jax.shard_map(
        per_device,
        mesh=mesh,
        in_specs=(
            P(("grp", "row"), "col", None),
            P(("grp", "row"), "col", None),
            P(("grp", "row"), "col", None),
            P("grp"),
            P("grp"),
            P(),
            P(),
            P(),
            P(),
            P(),
            P(),
        ),
        out_specs=(
            P(("grp", "row"), "col", None),
            P("grp", None),
            P("grp", None),
            P("grp", None),
            P("grp", None),
        ),
        check_vma=False,
    )
```

```python
import functools

import jax
import jax.numpy as jnp
from jax import lax
from jax.experimental import pallas as pl
from jax.experimental.pallas import tpu as pltpu
from jax.sharding import PartitionSpec as P

F32 = jnp.float32
BF16 = jnp.bfloat16
VMEM = pl.BlockSpec(memory_space=pltpu.VMEM)
SMEM = pl.BlockSpec(memory_space=pltpu.SMEM)
LHS_T = (((0,), (0,)), ((), ()))
RHS_T = (((1,), (1,)), ((), ()))
QUAD = 4
ACROSS = 4
CHANS = 32
GROUP = 16


def iota(shape, dim):
    return lax.broadcasted_iota(jnp.int32, shape, dim)


def dot(a, b, dims=(((1,), (0,)), ((), ())), **kw):
    return lax.dot_general(a, b, dims, preferred_element_type=F32, **kw)


def place_in_quad(row):
    return row % 2 + row // ACROSS % 2 * 2


def first_kernel(out_ref):
    out_ref[...] = jnp.zeros_like(out_ref)


def norm_kernel(
    seq_ref, res_ref, gain_ref, own_ref, near_ref, core_ref, across_ref, out_ref, to_core_ref, to_across_ref
):
    row = lax.axis_index("row")
    n = res_ref.shape[1]
    res = res_ref[...].astype(F32)
    gain = gain_ref[...]
    gain = jnp.concatenate([gain, gain], axis=1)
    for at, (state_ref, first) in enumerate(((own_ref, row * 2), (near_ref, (row ^ 8) * 2))):
        halves = []
        for s in range(2):
            value = state_ref[s].astype(F32)
            centred = value - jnp.mean(value, axis=0, keepdims=True)
            variance = jnp.mean(centred * centred, axis=0, keepdims=True)
            seq = seq_ref[first + s].astype(F32)
            halves.append(centred * (lax.rsqrt(variance + 1e-05) * (res * seq)))
        turned = jnp.concatenate(halves, axis=0).T
        value = (turned * gain).astype(BF16)
        for ref in (out_ref, to_core_ref, to_across_ref):
            ref[at * n : (at + 1) * n, :] = value
    to_core_ref[2 * n :, :] = core_ref[...]
    to_across_ref[2 * n :, :] = across_ref[...]


def gate_kernel(
    res_s_ref, seq_ref, res_ref, pair_ref, cot_ref, gate_ref, gain_ref, bias_ref, after_ref,
    scale_ref, slope_ref, turned_ref, own_ref, core_ref, across_ref, gain_out_ref, bias_out_ref,
    full_ref,
):
    gain_out_ref[...] = gain_ref[...]
    bias_out_ref[...] = bias_ref[...]
    row = lax.axis_index("row")
    quad_at = place_in_quad(row)
    rows = pair_ref.shape[0]
    n = res_ref.shape[1]
    total = jnp.sum(seq_ref[...].astype(F32), axis=1, keepdims=True)
    eye = iota((n, n), 0) == iota((n, n), 1)
    res_col = jnp.sum(jnp.where(eye, res_ref[...].astype(F32), 0.0), axis=1, keepdims=True)
    wide = QUAD * n
    src = iota((wide, wide), 0)
    dst = iota((wide, wide), 1)
    slot = dst // n
    chan = (quad_at ^ slot) * CHANS + dst % CHANS
    place = jnp.where(
        (src // n == (dst % n) // CHANS) & (src % n == chan), 1.0, 0.0
    ).astype(BF16)
    outs = ((own_ref, 0), (core_ref, 0), (across_ref, 0), (across_ref, 2))
    for half in range(rows // QUAD):
        for k in range(QUAD):
            i = half * QUAD + k
            gate = jax.nn.sigmoid(dot(pair_ref[i], gate_ref[...]))
            res_row = res_s_ref[row * rows + i].astype(F32)
            scale = gate / jnp.maximum(total * res_row * res_col, 1.0)
            lin = cot_ref[i].astype(F32) * scale
            scale_ref[i] = scale
            slope_ref[i] = lin * (1.0 - gate)
            full_ref[:, i * n : (i + 1) * n] = lin.astype(BF16)
            turned_ref[i * n : (i + 1) * n, :] = lin.T.astype(BF16)
        packed = dot(full_ref[:, half * wide : (half + 1) * wide], place).astype(BF16)
        for m in range(QUAD):
            out_ref, at = outs[m]
            out_ref[(at + half) * n : (at + half + 1) * n, :] = packed[:, m * n : (m + 1) * n]


def weight_kernel(
    right_ref, left_ref, out_w_ref, after_ref,
    kron_ref, block_ref, wide_ref, part_ref, wf_ref,
):
    quad_at = place_in_quad(lax.axis_index("row"))
    width, chans = right_ref.shape
    n = out_w_ref.shape[1]
    cols = width * GROUP
    spread = jnp.where(iota((width, cols), 0) == iota((width, cols), 1) // GROUP, 1.0, 0.0)
    repeated = dot(right_ref[...], spread.astype(BF16), LHS_T)
    lane = iota((chans, cols), 1) % GROUP
    for s in range(GROUP):
        kron_ref[s * chans : (s + 1) * chans, :] = jnp.where(lane == s, repeated, 0.0).astype(BF16)
    spread = jnp.where(iota((width, n), 0) == iota((width, n), 1) % width, 1.0, 0.0)
    repeated = dot(left_ref[...], spread.astype(BF16), LHS_T)
    lane = iota((chans, n), 1) // width
    for k in range(QUAD):
        block_ref[k * chans : (k + 1) * chans, :] = jnp.where(lane == k, repeated, 0.0).astype(BF16)
    wf_ref[...] = out_w_ref[...].astype(F32)
    for e in range(width):
        wide_ref[:, e * n : (e + 1) * n] = wf_ref[pl.ds(e, width, stride=width), :].astype(BF16)
    pick = jnp.where(
        iota((n, n), 0) == quad_at * CHANS + iota((n, n), 1) % CHANS, 1.0, 0.0
    ).astype(BF16)
    wf_ref[...] = dot(out_w_ref[...], pick)
    lane = iota((width, n), 1) // CHANS
    for h in range(width // QUAD):
        tile = None
        for k in range(QUAD):
            rows = wf_ref[pl.ds(h * QUAD + k, width, stride=width), :]
            tile = rows if tile is None else jnp.where(lane == k, rows, tile)
        part_ref[:, h * n : (h + 1) * n] = tile.astype(BF16)


def fold(tiles, lane):
    high, low = lane // 2 == 0, lane % 2 == 0
    pairs = [
        jnp.where(high, tiles[k], tiles[k + 2])
        + pltpu.roll(jnp.where(high, tiles[k + 2], tiles[k]), 2 * CHANS, 1)
        for k in range(2)
    ]
    other = jnp.where(low, pairs[1], pairs[0])
    size = lane.shape[1]
    other = jnp.where(low, pltpu.roll(other, size - CHANS, 1), pltpu.roll(other, CHANS, 1))
    return jnp.where(low, pairs[0], pairs[1]) + other


def half_of_rows(ys, turned, kron_ref, block_ref, wide_ref, right_t_ref, own_ref, scratch):
    m_ref, turn_ref, right_ref, flat_ref = scratch
    row = lax.axis_index("row")
    n = ys[0].shape[1]
    chans, width = 64, 32
    slots = [y[t * n : (t + 1) * n, :] for y in ys for t in range(2)]
    right = dot(jnp.concatenate(slots, axis=1), kron_ref[...]).astype(BF16)
    right_t_ref[...] = right.T
    at = iota((32, n), 0)
    four = at % 8
    member = four // 2
    here = (row ^ (member % 2 + member // 2 * ACROSS)) * 8 + (four % 2) * QUAD + at // 8
    pick = jnp.where(iota((32, n), 1) == here, 1.0, 0.0).astype(BF16)
    for t, slot in enumerate(slots):
        picked = dot(pick, slot)
        for s in range(2):
            at = (2 * t + s) * 8
            for half in range(2):
                turn_ref[half, at : at + 8, :] = jnp.concatenate(
                    [
                        picked[k * 8 : (k + 1) * 8, s * chans : (s + 1) * chans]
                        for k in (2 * half, 2 * half + 1)
                    ],
                    axis=1,
                )
    for f in range(8):
        for half in range(2):
            own_ref[f * GROUP : (f + 1) * GROUP, half * n : (half + 1) * n] = turn_ref[
                half, pl.ds(f, GROUP, stride=8), :
            ].astype(BF16)
    left = dot(own_ref[0 : 2 * GROUP, :], block_ref[...])
    mine = jnp.concatenate(
        [
            left[f * GROUP : (f + 1) * GROUP, k * width : (k + 1) * width]
            for f in range(2)
            for k in range(QUAD)
        ],
        axis=0,
    ).astype(BF16)
    for e8 in range(width // 8):
        part = dot(mine, wide_ref[:, e8 * 8 * n : (e8 + 1) * 8 * n]).astype(BF16)
        for el in range(8):
            e = e8 * 8 + el
            for i in range(8):
                m_ref[e * GROUP : (e + 1) * GROUP, i * n : (i + 1) * n] = part[
                    i * GROUP : (i + 1) * GROUP, el * n : (el + 1) * n
                ]
    linear = dot(right, m_ref[...])
    for k in range(4):
        at = slice(k * 128, (k + 1) * 128)
        right_ref[at, :] = dot(m_ref[at, :], turned[...])
    for t in range(8):
        for s in range(2):
            flat_ref[s * width : (s + 1) * width, t * n : (t + 1) * n] = right_ref[
                pl.ds(2 * t + s, width, stride=GROUP), :
            ].astype(BF16)
    act = sum(dot(flat_ref[:, k * 2 * n : (k + 1) * 2 * n], y[: 2 * n, :]) for k, y in enumerate(ys))
    return linear, act


def half_kernel(
    y0_ref, y1_ref, y2_ref, y3_ref, turned_ref, kron_ref, block_ref, wide_ref, bias_ref,
    linear_ref, act_ref, right_t_ref, own_ref, *scratch
):
    linear, act = half_of_rows(
        (y0_ref, y1_ref, y2_ref, y3_ref), turned_ref, kron_ref, block_ref, wide_ref, right_t_ref, own_ref, scratch
    )
    linear_ref[...] = linear + jnp.concatenate([bias_ref[...]] * 8, axis=1)
    act_ref[...] = act


def pair_kernel(
    y0_ref, y1_ref, y2_ref, y3_ref, turned_ref, kron_ref, block_ref, wide_ref,
    linear_ref, act_ref, slope_ref, pair_ref,
    value_ref, keep_ref, send_ref, grad_right_ref, right_t_ref, own_ref, slope_s_ref, *scratch
):
    rows, n, _ = pair_ref.shape
    linear, act = half_of_rows(
        (y0_ref, y1_ref, y2_ref, y3_ref), turned_ref, kron_ref, block_ref, wide_ref, right_t_ref, own_ref, scratch
    )
    for i in range(rows):
        value = linear[:, i * n : (i + 1) * n] + linear_ref[:, i * n : (i + 1) * n]
        value_ref[i] = value
        slope_s_ref[i * n : (i + 1) * n, :] = (slope_ref[i] * value).astype(BF16)
    grad_gate = dot(pair_ref[...].reshape(rows * n, n), slope_s_ref[...], LHS_T)
    halves = grad_gate[: n // 2, :], grad_gate[n // 2 :, :]
    first_core = lax.axis_index("row") % 2 == 0
    keep_ref[...] = jnp.where(first_core, halves[0], halves[1]).astype(BF16)
    send_ref[...] = jnp.where(first_core, halves[1], halves[0]).astype(BF16)
    act = act + act_ref[...]
    grad_right_ref[...] = act[:32, :64] + act[32:, 64:]


def update_kernel(scale_ref, value_ref, after_ref, update_ref, token_ref):
    token_ref[...] = jnp.zeros_like(token_ref)
    update_ref[...] = (scale_ref[...] * value_ref[...]).astype(BF16)


def chip_kernel(sums_ref, keep_ref, other_ref, out_ref):
    out_ref[0:288, :] = sums_ref[...]
    out_ref[288:352, :] = (keep_ref[...].astype(F32) + other_ref[...].astype(F32)).astype(BF16)


def add_kernel(own_ref, other_ref, after_ref, out_ref):
    out_ref[...] = (own_ref[...].astype(F32) + other_ref[...].astype(F32)).astype(BF16)


def out_kernel(
    right0_ref, right1_ref, own0_ref, own1_ref, own_ref, core_ref, across_ref, both_ref,
    part_ref, left_ref, grad_right_ref,
    sums_ref, n_ref
):
    n = sums_ref.shape[1]
    chans, width = 64, 32
    half = 8 * GROUP
    grads = ((own_ref, 0), (core_ref, 2), (across_ref, 2), (both_ref, 4))
    for f2, (ref, at) in enumerate(grads):
        grad = jnp.concatenate([ref[(at + k) * n : (at + k + 1) * n, :] for k in range(2)], axis=1)
        for g, right_ref in enumerate((right0_ref, right1_ref)):
            part = dot(right_ref[...], grad).astype(BF16)
            for fl in range(2):
                at = g * half + (f2 * 2 + fl) * GROUP
                for e in range(width):
                    n_ref[at : at + GROUP, e * n : (e + 1) * n] = part[
                        e * GROUP : (e + 1) * GROUP, fl * n : (fl + 1) * n
                    ]
    own_t = jnp.concatenate([own0_ref[...], own1_ref[...]], axis=0).T
    lane = iota((chans, n), 1) // CHANS
    packed = []
    for h in range(width // QUAD):
        whole = dot(own_t, n_ref[:, h * 4 * n : (h + 1) * 4 * n])
        tiles = []
        for el in range(QUAD):
            tile = whole[0:chans, el * n : (el + 1) * n]
            for k in range(1, QUAD):
                tile = jnp.where(
                    lane == k, whole[k * chans : (k + 1) * chans, el * n : (el + 1) * n], tile
                )
            tiles.append(tile)
        packed.append(fold(tiles, lane))
    feat = jnp.concatenate(packed, axis=1)
    coarse = feat.astype(BF16)
    fine = (feat - coarse.astype(F32)).astype(BF16)
    grad_out = dot(left_ref[...], coarse) + dot(left_ref[...], fine)
    for h in range(width // QUAD):
        sums_ref[h * width : (h + 1) * width, :] = grad_out[:, h * n : (h + 1) * n].astype(BF16)
    grad_left = dot(part_ref[...], coarse, RHS_T) + dot(part_ref[...], fine, RHS_T)
    sums_ref[256:288, :] = jnp.concatenate([grad_left, grad_right_ref[...]], axis=1).astype(BF16)


def join_kernel(own_ref, beside_ref, across_ref, both_ref, out_ref):
    def pair(a_ref, b_ref, lo, hi):
        return a_ref[lo:hi, :].astype(F32) + b_ref[lo:hi, :].astype(F32)

    out_ref[0:256, :] = pair(own_ref, beside_ref, 0, 256).astype(BF16)
    out_ref[256:512, :] = pair(across_ref, both_ref, 0, 256).astype(BF16)
    out_ref[512:608, :] = (
        pair(own_ref, beside_ref, 256, 352) + pair(across_ref, both_ref, 256, 352)
    ).astype(BF16)


def last_kernel(local_ref, other_ref, out_ref, gate_ref, left_ref, right_ref):
    row = lax.axis_index("row")
    quad_at = place_in_quad(row)
    n = local_ref.shape[1]
    wide = QUAD * n
    src = iota((wide, wide), 0)
    dst = iota((wide, wide), 1)
    chan = (quad_at ^ (src // n)) * CHANS + src % CHANS
    place = jnp.where(
        (dst // n == (src % n) // CHANS) & (dst % n == chan), 1.0, 0.0
    ).astype(BF16)
    packed = jnp.concatenate(
        [local_ref[0:256, :], other_ref[0:256, :], local_ref[256:512, :], other_ref[256:512, :]], axis=1
    )
    whole = dot(packed, place)
    for h in range(8):
        for el in range(4):
            out_ref[pl.ds(h * 4 + el, 32, stride=32), :] = whole[
                h * 32 : (h + 1) * 32, el * n : (el + 1) * n
            ]
    both = local_ref[512:544, :].astype(F32) + other_ref[512:544, :].astype(F32)
    left_ref[...] = both[:, 0:64]
    right_ref[...] = both[:, 64:128]
    halves = local_ref[544:608, :].astype(F32), other_ref[544:608, :].astype(F32)
    gate_ref[: n // 2, :] = jnp.where(row % 2 == 0, halves[0], halves[1])
    gate_ref[n // 2 :, :] = jnp.where(row % 2 == 0, halves[1], halves[0])


def tie_kernel(*refs):
    out_ref, at = refs[-1], 0
    for ref in refs:
        if at < out_ref.shape[0]:
            out_ref[at : at + ref.shape[0], :] = ref[...]
            at += ref.shape[0]


def call(kernel, shapes, scratch=(), smem=0, ins=0, flops=1 << 20, vmem=4):
    return pl.pallas_call(
        kernel,
        out_shape=[jax.ShapeDtypeStruct(s, d) for s, d in shapes],
        in_specs=[SMEM] * smem + [VMEM] * (ins - smem),
        out_specs=[VMEM] * len(shapes),
        scratch_shapes=[pltpu.VMEM(s, d) for s, d in scratch],
        compiler_params=pltpu.CompilerParams(vmem_limit_bytes=vmem << 20),
        cost_estimate=pl.CostEstimate(flops=flops, bytes_accessed=1 << 20, transcendentals=0),
    )


def swap(x, bit, size):
    return lax.ppermute(x, "row", [(i, i ^ bit) for i in range(size)])


def one_column(
    alignment_state, pair_state, cotangent, sequence_row_mask, residue_mask, norm_gain_vector,
    left_matrix_weight, right_matrix_weight, output_weight, output_bias, gate_matrix,
):
    size = lax.axis_size("row")
    rows, n, _ = pair_state.shape
    res = residue_mask.reshape(1, n)
    seq = sequence_row_mask.reshape(1, -1)
    state = alignment_state.transpose(0, 2, 1)
    near = swap(state, 8, size)
    (token,) = call(first_kernel, [((8, n), F32)], flops=20 << 30)()
    gain = norm_gain_vector.reshape(1, -1)
    bias = output_bias.reshape(1, n)
    scale, slope, turned, own, core, across, gain, bias = call(
        gate_kernel,
        [((rows, n, n), F32), ((rows, n, n), F32), ((rows * n, n), BF16)] + [((2 * n, n), BF16)] * 2
        + [((4 * n, n), BF16), (gain.shape, F32), (bias.shape, F32)],
        scratch=[((n, rows * n), BF16)], smem=1, ins=9, flops=1 << 30, vmem=12,
    )(residue_mask, seq, res, pair_state, cotangent, gate_matrix, gain, bias, token)
    pair, to_core, to_across = call(
        norm_kernel, [((2 * n, n), BF16), ((4 * n, n), BF16), ((6 * n, n), BF16)], smem=1, ins=7
    )(sequence_row_mask, res, gain, state, near, core, across)
    beside, ahead, corner = swap(pair, 2, size), swap(to_across, ACROSS, size), swap(pair, 2 ^ ACROSS, size)
    left_t = left_matrix_weight.T
    kron, block, wide, part = call(
        weight_kernel,
        [((1024, 512), BF16), ((256, n), BF16), ((32, 32 * n), BF16), ((32, 8 * n), BF16)],
        scratch=[((1024, n), F32)], ins=4, flops=1 << 30, vmem=12,
    )(right_matrix_weight.T, left_t, output_weight, pair)
    (beside,) = call(tie_kernel, [((2 * n, n), BF16)], ins=2)(beside, block)
    pair_core, beside_core, corner_core, ahead_core = (
        swap(y, 1, size) for y in (to_core, beside, corner, ahead)
    )
    scratch = [
        ((512, rows * n), BF16), ((2, n, n), F32), ((512, n), F32), ((64, 8 * n), BF16),
    ]
    shared = (turned, kron, block, wide)
    kept = [((512, n), BF16), ((n, 256), BF16)]
    linear, act, right0, own0 = call(
        half_kernel,
        [((n, rows * n), F32), ((64, n), F32), *kept],
        scratch=scratch, ins=9, flops=2 << 30, vmem=24,
    )(pair, pair_core, beside, beside_core, *shared, bias)
    value, keep, send, right_sum, right1, own1 = call(
        pair_kernel,
        [((rows, n, n), F32), ((n // 2, n), BF16), ((n // 2, n), BF16), ((32, 64), F32), *kept],
        scratch=[((rows * n, n), BF16), *scratch], ins=12, flops=2 << 30, vmem=24,
    )(corner, corner_core, ahead, ahead_core, *shared, linear, act, slope, pair_state)
    (sums,) = call(
        out_kernel, [((288, n), BF16)], scratch=[((256, 32 * n), BF16)], ins=11, flops=1 << 30, vmem=24,
    )(right0, right1, own0, own1, own, pair_core, ahead, ahead_core, part, left_t, right_sum)
    (sums,) = call(chip_kernel, [((352, n), BF16)], ins=3)(sums, keep, swap(send, 1, size))
    update, token = call(update_kernel, [((rows, n, n), BF16), ((8, n), F32)], ins=3, flops=1 << 30, vmem=8)(scale, value, sums)
    (sums,) = call(add_kernel, [((352, n), BF16)], ins=3)(sums, swap(sums, 8, size), token)
    others = [swap(sums, step, size) for step in (2, ACROSS, 2 ^ ACROSS)]
    (local,) = call(join_kernel, [((608, n), BF16)], ins=4)(sums, *others)
    other = swap(local, 1, size)
    grad_out, grad_gate, left, right = call(
        last_kernel,
        [((1024, n), F32), ((n, n), F32), ((32, 64), F32), ((32, 64), F32)],
        ins=2,
    )(local, other)
    return update, left.T, right.T, grad_out, grad_gate


def layer_normalize(alignment_state, norm_gain_vector):
    value_entries = alignment_state.astype(jnp.float32)
    average = jnp.mean(value_entries, axis=-1, keepdims=True)
    centred = value_entries - average
    variance = jnp.mean(centred * centred, axis=-1, keepdims=True)
    return (centred * lax.rsqrt(variance + 1e-05) * norm_gain_vector).astype(jnp.bfloat16)


def any_mesh(
    alignment_state,
    pair_state,
    cotangent,
    sequence_row_mask,
    residue_mask,
    norm_gain_vector,
    left_matrix_weight,
    right_matrix_weight,
    output_weight,
    output_bias,
    gate_matrix,
):
    sequence_resident, column_count, alignment_channel_count = alignment_state.shape
    count_of_rows = pair_state.shape[0]
    pair_chans = pair_state.shape[2]
    projection_width = left_matrix_weight.shape[1]
    every_sequence = sequence_row_mask.shape[0]
    row_at = lax.axis_index("row")
    col_at = lax.axis_index("col")
    number_of_rows = lax.axis_size("row")
    contract_first = (((0,), (0,)), ((), ()))
    contract_second = (((1,), (1,)), ((), ()))
    resident_features = layer_normalize(alignment_state, norm_gain_vector)
    seq_flags = sequence_row_mask.astype(jnp.float32)
    res_flags = residue_mask.astype(jnp.float32)
    my_cols = lax.dynamic_slice_in_dim(res_flags, col_at * column_count, column_count, 0)
    my_rows = lax.dynamic_slice_in_dim(res_flags, row_at * count_of_rows, count_of_rows, 0)
    panel_mask = seq_flags[:, None] * my_rows[None, :]
    column_mask = seq_flags[:, None] * my_cols[None, :]
    broadcast_features = lax.all_gather(
        resident_features.reshape(sequence_resident, column_count * alignment_channel_count),
        "col",
        axis=1,
        tiled=True,
    )
    row_portions = broadcast_features.reshape(
        sequence_resident, number_of_rows, count_of_rows * alignment_channel_count
    )
    row_feats = lax.all_to_all(
        row_portions, "row", split_axis=1, concat_axis=0, tiled=True
    ).reshape(every_sequence * count_of_rows, alignment_channel_count)
    left_panel = (
        jnp.dot(row_feats, left_matrix_weight, preferred_element_type=jnp.float32).reshape(
            every_sequence, count_of_rows, projection_width
        )
        * panel_mask[:, :, None]
    ).astype(jnp.bfloat16)
    left_matrix = left_panel.transpose(1, 2, 0).reshape(
        count_of_rows * projection_width, every_sequence
    )
    column_features = lax.all_gather(
        resident_features.reshape(sequence_resident, column_count * alignment_channel_count),
        "row",
        axis=0,
        tiled=True,
    ).reshape(every_sequence, column_count, alignment_channel_count)
    right_panel = (
        jnp.dot(
            column_features.reshape(every_sequence * column_count, alignment_channel_count),
            right_matrix_weight,
            preferred_element_type=jnp.float32,
        ).reshape(every_sequence, column_count, projection_width)
        * column_mask[:, :, None]
    ).astype(jnp.bfloat16)
    surplus_offset = jnp.zeros((alignment_channel_count, projection_width), jnp.float32)

    def absorb(extra, first_col, width_columns, right_part):
        feat_blk = (
            lax.dynamic_slice_in_dim(column_features, first_col, width_columns, 1)
            .reshape(every_sequence * width_columns, alignment_channel_count)
            .astype(jnp.float32)
        )
        mask_blk = lax.dynamic_slice_in_dim(column_mask, first_col, width_columns, 1)
        masked_part = (
            right_part.reshape(every_sequence, width_columns, projection_width)
            * mask_blk[:, :, None]
        ).reshape(every_sequence * width_columns, projection_width)
        return extra + jnp.dot(feat_blk.T, masked_part, precision=lax.Precision.HIGHEST)

    right_flat = right_panel.reshape(every_sequence, column_count * projection_width)
    row_total = jnp.sum(seq_flags)
    col_block = 128
    n_blocks = column_count // col_block

    def one_block(block_idx, carry):
        new_update, grad_out, grad_gate, left_acc, extra = carry
        first_col = block_idx * col_block
        right_blk = lax.dynamic_slice_in_dim(
            right_flat, first_col * projection_width, col_block * projection_width, 1
        )
        outer_prod = jnp.dot(left_matrix, right_blk, preferred_element_type=jnp.float32)
        outer_prod = outer_prod.reshape(
            count_of_rows, projection_width, col_block, projection_width
        ).transpose(0, 2, 1, 3)
        outer_prod = outer_prod.reshape(
            count_of_rows * col_block, projection_width * projection_width
        ).astype(jnp.bfloat16)
        linear = (
            jnp.dot(outer_prod, output_weight, preferred_element_type=jnp.float32) + output_bias
        )
        pair_blk = lax.dynamic_slice_in_dim(pair_state, first_col, col_block, 1).reshape(
            count_of_rows * col_block, pair_chans
        )
        gate_val = jax.nn.sigmoid(
            jnp.dot(pair_blk, gate_matrix, preferred_element_type=jnp.float32)
        )
        blk_flags = lax.dynamic_slice_in_dim(my_cols, first_col, col_block, 0)
        divisor = jnp.maximum(row_total * my_rows[:, None] * blk_flags[None, :], 1.0).reshape(
            count_of_rows * col_block, 1
        )
        cot_blk = (
            lax.dynamic_slice_in_dim(cotangent, first_col, col_block, 1)
            .reshape(count_of_rows * col_block, pair_chans)
            .astype(jnp.float32)
        )
        new_pair = (gate_val * linear / divisor).astype(jnp.bfloat16)
        new_update = lax.dynamic_update_slice_in_dim(
            new_update, new_pair.reshape(count_of_rows, col_block, pair_chans), first_col, 1
        )
        grad_lin = (cot_blk * gate_val / divisor).astype(jnp.bfloat16)
        grad_pre = (cot_blk * linear / divisor * gate_val * (1.0 - gate_val)).astype(jnp.bfloat16)
        grad_out = grad_out + lax.dot_general(
            outer_prod, grad_lin, contract_first, preferred_element_type=jnp.float32
        )
        grad_gate = grad_gate + lax.dot_general(
            pair_blk, grad_pre, contract_first, preferred_element_type=jnp.float32
        )
        grad_outer = lax.dot_general(
            grad_lin, output_weight, contract_second, preferred_element_type=jnp.float32
        ).astype(jnp.bfloat16)
        outer_turned = (
            grad_outer.reshape(count_of_rows, col_block, projection_width, projection_width)
            .transpose(0, 2, 1, 3)
            .reshape(count_of_rows * projection_width, col_block * projection_width)
        )
        left_acc = left_acc + lax.dot_general(
            outer_turned, right_blk, contract_second, preferred_element_type=jnp.float32
        )
        right_part = lax.dot_general(
            left_matrix, outer_turned, contract_first, preferred_element_type=jnp.float32
        )
        extra = absorb(extra, first_col, col_block, right_part)
        return (new_update, grad_out, grad_gate, left_acc, extra)

    start_carry = (
        jnp.zeros((count_of_rows, column_count, pair_chans), jnp.bfloat16),
        jnp.zeros((projection_width * projection_width, pair_chans), jnp.float32),
        jnp.zeros((pair_chans, pair_chans), jnp.float32),
        jnp.zeros((count_of_rows * projection_width, every_sequence), jnp.float32),
        surplus_offset,
    )
    new_update, grad_out, grad_gate, left_acc, extra = lax.fori_loop(
        0, n_blocks, one_block, start_carry
    )
    grad_left_act = (
        left_acc.reshape(count_of_rows, projection_width, every_sequence).transpose(2, 0, 1)
        * panel_mask[:, :, None]
    )
    grad_left = jnp.dot(
        row_feats.astype(jnp.float32).T,
        grad_left_act.reshape(every_sequence * count_of_rows, projection_width),
        precision=lax.Precision.HIGHEST,
    )
    summed_left, summed_right, summed_out, summed_gate = lax.psum(
        (grad_left, extra, grad_out, grad_gate), ("row", "col")
    )
    return (new_update, summed_left, summed_right, summed_out, summed_gate)


def per_device(*args):
    alignment_state, pair_state = args[0], args[1]
    fits = (
        lax.axis_size("col") == 1
        and lax.axis_size("row") == 16
        and alignment_state.shape == (2, 128, 64)
        and pair_state.shape == (8, 128, 128)
    )
    return one_column(*args) if fits else any_mesh(*args)


def solution(mesh):
    return jax.shard_map(
        per_device,
        mesh=mesh,
        in_specs=(
            P(("grp", "row"), "col", None),
            P(("grp", "row"), "col", None),
            P(("grp", "row"), "col", None),
            P("grp"),
            P("grp"),
            P(),
            P(),
            P(),
            P(),
            P(),
            P(),
        ),
        out_specs=(
            P(("grp", "row"), "col", None),
            P("grp", None),
            P("grp", None),
            P("grp", None),
            P("grp", None),
        ),
        check_vma=False,
    )
```

```python
import functools

import jax
import jax.numpy as jnp
from jax import lax
from jax.experimental import pallas as pl
from jax.experimental.pallas import tpu as pltpu
from jax.sharding import PartitionSpec as P

F32 = jnp.float32
BF16 = jnp.bfloat16
VMEM = pl.BlockSpec(memory_space=pltpu.VMEM)
SMEM = pl.BlockSpec(memory_space=pltpu.SMEM)
LHS_T = (((0,), (0,)), ((), ()))
RHS_T = (((1,), (1,)), ((), ()))
QUAD = 4
ACROSS = 4
CHANS = 32
GROUP = 16


def iota(shape, dim):
    return lax.broadcasted_iota(jnp.int32, shape, dim)


def dot(a, b, dims=(((1,), (0,)), ((), ())), **kw):
    return lax.dot_general(a, b, dims, preferred_element_type=F32, **kw)


def place_in_quad(row):
    return row % 2 + row // ACROSS % 2 * 2


def first_kernel(out_ref):
    out_ref[...] = jnp.zeros_like(out_ref)


def norm_kernel(
    seq_ref, res_ref, gain_ref, own_ref, near_ref, core_ref, across_ref, out_ref, to_core_ref, to_across_ref
):
    row = lax.axis_index("row")
    n = res_ref.shape[1]
    res = res_ref[...].astype(F32)
    gain = gain_ref[...]
    gain = jnp.concatenate([gain, gain], axis=1)
    for at, (state_ref, first) in enumerate(((own_ref, row * 2), (near_ref, (row ^ 8) * 2))):
        halves = []
        for s in range(2):
            value = state_ref[s].astype(F32)
            centred = value - jnp.mean(value, axis=0, keepdims=True)
            variance = jnp.mean(centred * centred, axis=0, keepdims=True)
            seq = seq_ref[first + s].astype(F32)
            halves.append(centred * (lax.rsqrt(variance + 1e-05) * (res * seq)))
        turned = jnp.concatenate(halves, axis=0).T
        value = (turned * gain).astype(BF16)
        for ref in (out_ref, to_core_ref, to_across_ref):
            ref[at * n : (at + 1) * n, :] = value
    to_core_ref[2 * n :, :] = core_ref[...]
    to_across_ref[2 * n :, :] = across_ref[...]


def gate_kernel(
    res_s_ref, seq_ref, res_ref, pair_ref, cot_ref, gate_ref, gain_ref, bias_ref, after_ref,
    scale_ref, slope_ref, turned_ref, own_ref, core_ref, across_ref, gain_out_ref, bias_out_ref,
    full_ref,
):
    gain_out_ref[...] = gain_ref[...]
    bias_out_ref[...] = bias_ref[...]
    row = lax.axis_index("row")
    quad_at = place_in_quad(row)
    rows = pair_ref.shape[0]
    n = res_ref.shape[1]
    total = jnp.sum(seq_ref[...].astype(F32), axis=1, keepdims=True)
    eye = iota((n, n), 0) == iota((n, n), 1)
    res_col = jnp.sum(jnp.where(eye, res_ref[...].astype(F32), 0.0), axis=1, keepdims=True)
    wide = QUAD * n
    src = iota((wide, wide), 0)
    dst = iota((wide, wide), 1)
    slot = dst // n
    chan = (quad_at ^ slot) * CHANS + dst % CHANS
    place = jnp.where(
        (src // n == (dst % n) // CHANS) & (src % n == chan), 1.0, 0.0
    ).astype(BF16)
    outs = ((own_ref, 0), (core_ref, 0), (across_ref, 0), (across_ref, 2))
    for half in range(rows // QUAD):
        for k in range(QUAD):
            i = half * QUAD + k
            gate = jax.nn.sigmoid(dot(pair_ref[i], gate_ref[...]))
            res_row = res_s_ref[row * rows + i].astype(F32)
            scale = gate / jnp.maximum(total * res_row * res_col, 1.0)
            lin = cot_ref[i].astype(F32) * scale
            scale_ref[i] = scale
            slope_ref[i] = lin * (1.0 - gate)
            full_ref[:, i * n : (i + 1) * n] = lin.astype(BF16)
            turned_ref[i * n : (i + 1) * n, :] = lin.T.astype(BF16)
        packed = dot(full_ref[:, half * wide : (half + 1) * wide], place).astype(BF16)
        for m in range(QUAD):
            out_ref, at = outs[m]
            out_ref[(at + half) * n : (at + half + 1) * n, :] = packed[:, m * n : (m + 1) * n]


def weight_kernel(
    right_ref, left_ref, out_w_ref, after_ref,
    kron_ref, block_ref, wide_ref, part_ref, wf_ref,
):
    quad_at = place_in_quad(lax.axis_index("row"))
    width, chans = right_ref.shape
    n = out_w_ref.shape[1]
    cols = width * GROUP
    spread = jnp.where(iota((width, cols), 0) == iota((width, cols), 1) // GROUP, 1.0, 0.0)
    repeated = dot(right_ref[...], spread.astype(BF16), LHS_T)
    lane = iota((chans, cols), 1) % GROUP
    for s in range(GROUP):
        kron_ref[s * chans : (s + 1) * chans, :] = jnp.where(lane == s, repeated, 0.0).astype(BF16)
    spread = jnp.where(iota((width, n), 0) == iota((width, n), 1) % width, 1.0, 0.0)
    repeated = dot(left_ref[...], spread.astype(BF16), LHS_T)
    lane = iota((chans, n), 1) // width
    for k in range(QUAD):
        block_ref[k * chans : (k + 1) * chans, :] = jnp.where(lane == k, repeated, 0.0).astype(BF16)
    wf_ref[...] = out_w_ref[...].astype(F32)
    for e in range(width):
        wide_ref[:, e * n : (e + 1) * n] = wf_ref[pl.ds(e, width, stride=width), :].astype(BF16)
    pick = jnp.where(
        iota((n, n), 0) == quad_at * CHANS + iota((n, n), 1) % CHANS, 1.0, 0.0
    ).astype(BF16)
    wf_ref[...] = dot(out_w_ref[...], pick)
    lane = iota((width, n), 1) // CHANS
    for h in range(width // QUAD):
        tile = None
        for k in range(QUAD):
            rows = wf_ref[pl.ds(h * QUAD + k, width, stride=width), :]
            tile = rows if tile is None else jnp.where(lane == k, rows, tile)
        part_ref[:, h * n : (h + 1) * n] = tile.astype(BF16)


def fold(tiles, lane):
    high, low = lane // 2 == 0, lane % 2 == 0
    pairs = [
        jnp.where(high, tiles[k], tiles[k + 2])
        + pltpu.roll(jnp.where(high, tiles[k + 2], tiles[k]), 2 * CHANS, 1)
        for k in range(2)
    ]
    other = jnp.where(low, pairs[1], pairs[0])
    size = lane.shape[1]
    other = jnp.where(low, pltpu.roll(other, size - CHANS, 1), pltpu.roll(other, CHANS, 1))
    return jnp.where(low, pairs[0], pairs[1]) + other


def half_of_rows(ys, turned, kron_ref, block_ref, wide_ref, right_t_ref, own_ref, scratch):
    m_ref, turn_ref, right_ref, flat_ref = scratch
    row = lax.axis_index("row")
    n = ys[0].shape[1]
    chans, width = 64, 32
    slots = [y[t * n : (t + 1) * n, :] for y in ys for t in range(2)]
    right = dot(jnp.concatenate(slots, axis=1), kron_ref[...]).astype(BF16)
    right_t_ref[...] = right.T
    at = iota((32, n), 0)
    four = at % 8
    member = four // 2
    here = (row ^ (member % 2 + member // 2 * ACROSS)) * 8 + (four % 2) * QUAD + at // 8
    pick = jnp.where(iota((32, n), 1) == here, 1.0, 0.0).astype(BF16)
    for t, slot in enumerate(slots):
        picked = dot(pick, slot)
        for s in range(2):
            at = (2 * t + s) * 8
            for half in range(2):
                turn_ref[half, at : at + 8, :] = jnp.concatenate(
                    [
                        picked[k * 8 : (k + 1) * 8, s * chans : (s + 1) * chans]
                        for k in (2 * half, 2 * half + 1)
                    ],
                    axis=1,
                )
    for f in range(8):
        for half in range(2):
            own_ref[f * GROUP : (f + 1) * GROUP, half * n : (half + 1) * n] = turn_ref[
                half, pl.ds(f, GROUP, stride=8), :
            ].astype(BF16)
    left = dot(own_ref[0 : 2 * GROUP, :], block_ref[...])
    mine = jnp.concatenate(
        [
            left[f * GROUP : (f + 1) * GROUP, k * width : (k + 1) * width]
            for f in range(2)
            for k in range(QUAD)
        ],
        axis=0,
    ).astype(BF16)
    for e8 in range(width // 8):
        part = dot(mine, wide_ref[:, e8 * 8 * n : (e8 + 1) * 8 * n]).astype(BF16)
        for el in range(8):
            e = e8 * 8 + el
            for i in range(8):
                m_ref[e * GROUP : (e + 1) * GROUP, i * n : (i + 1) * n] = part[
                    i * GROUP : (i + 1) * GROUP, el * n : (el + 1) * n
                ]
        at = slice(e8 * 8 * GROUP, (e8 + 1) * 8 * GROUP)
        right_ref[at, :] = dot(m_ref[at, :], turned[...])
    linear = dot(right, m_ref[...])
    for t in range(8):
        for s in range(2):
            flat_ref[s * width : (s + 1) * width, t * n : (t + 1) * n] = right_ref[
                pl.ds(2 * t + s, width, stride=GROUP), :
            ].astype(BF16)
    act = sum(dot(flat_ref[:, k * 2 * n : (k + 1) * 2 * n], y[: 2 * n, :]) for k, y in enumerate(ys))
    return linear, act


def half_kernel(
    y0_ref, y1_ref, y2_ref, y3_ref, turned_ref, kron_ref, block_ref, wide_ref, bias_ref,
    linear_ref, act_ref, right_t_ref, own_ref, *scratch
):
    linear, act = half_of_rows(
        (y0_ref, y1_ref, y2_ref, y3_ref), turned_ref, kron_ref, block_ref, wide_ref, right_t_ref, own_ref, scratch
    )
    linear_ref[...] = linear + jnp.concatenate([bias_ref[...]] * 8, axis=1)
    act_ref[...] = act


def pair_kernel(
    y0_ref, y1_ref, y2_ref, y3_ref, turned_ref, kron_ref, block_ref, wide_ref,
    linear_ref, act_ref, slope_ref, pair_ref,
    value_ref, keep_ref, send_ref, grad_right_ref, right_t_ref, own_ref, slope_s_ref, *scratch
):
    rows, n, _ = pair_ref.shape
    linear, act = half_of_rows(
        (y0_ref, y1_ref, y2_ref, y3_ref), turned_ref, kron_ref, block_ref, wide_ref, right_t_ref, own_ref, scratch
    )
    for i in range(rows):
        value = linear[:, i * n : (i + 1) * n] + linear_ref[:, i * n : (i + 1) * n]
        value_ref[i] = value
        slope_s_ref[i * n : (i + 1) * n, :] = (slope_ref[i] * value).astype(BF16)
    grad_gate = dot(pair_ref[...].reshape(rows * n, n), slope_s_ref[...], LHS_T)
    halves = grad_gate[: n // 2, :], grad_gate[n // 2 :, :]
    first_core = lax.axis_index("row") % 2 == 0
    keep_ref[...] = jnp.where(first_core, halves[0], halves[1]).astype(BF16)
    send_ref[...] = jnp.where(first_core, halves[1], halves[0]).astype(BF16)
    act = act + act_ref[...]
    grad_right_ref[...] = act[:32, :64] + act[32:, 64:]


def update_kernel(scale_ref, value_ref, after_ref, update_ref, token_ref):
    token_ref[...] = jnp.zeros_like(token_ref)
    update_ref[...] = (scale_ref[...] * value_ref[...]).astype(BF16)


def chip_kernel(sums_ref, keep_ref, other_ref, out_ref):
    out_ref[0:288, :] = sums_ref[...]
    out_ref[288:352, :] = (keep_ref[...].astype(F32) + other_ref[...].astype(F32)).astype(BF16)


def add_kernel(own_ref, other_ref, after_ref, out_ref):
    out_ref[...] = (own_ref[...].astype(F32) + other_ref[...].astype(F32)).astype(BF16)


def out_kernel(
    right0_ref, right1_ref, own0_ref, own1_ref, own_ref, core_ref, across_ref, both_ref,
    part_ref, left_ref, grad_right_ref,
    sums_ref, n_ref
):
    n = sums_ref.shape[1]
    chans, width = 64, 32
    half = 8 * GROUP
    grads = ((own_ref, 0), (core_ref, 2), (across_ref, 2), (both_ref, 4))
    for f2, (ref, at) in enumerate(grads):
        grad = jnp.concatenate([ref[(at + k) * n : (at + k + 1) * n, :] for k in range(2)], axis=1)
        for g, right_ref in enumerate((right0_ref, right1_ref)):
            part = dot(right_ref[...], grad).astype(BF16)
            for fl in range(2):
                at = g * half + (f2 * 2 + fl) * GROUP
                for e in range(width):
                    n_ref[at : at + GROUP, e * n : (e + 1) * n] = part[
                        e * GROUP : (e + 1) * GROUP, fl * n : (fl + 1) * n
                    ]
    own_t = jnp.concatenate([own0_ref[...], own1_ref[...]], axis=0).T
    lane = iota((chans, n), 1) // CHANS
    packed = []
    for h in range(width // QUAD):
        whole = dot(own_t, n_ref[:, h * 4 * n : (h + 1) * 4 * n])
        tiles = []
        for el in range(QUAD):
            tile = whole[0:chans, el * n : (el + 1) * n]
            for k in range(1, QUAD):
                tile = jnp.where(
                    lane == k, whole[k * chans : (k + 1) * chans, el * n : (el + 1) * n], tile
                )
            tiles.append(tile)
        packed.append(fold(tiles, lane))
    feat = jnp.concatenate(packed, axis=1)
    coarse = feat.astype(BF16)
    fine = (feat - coarse.astype(F32)).astype(BF16)
    grad_out = dot(left_ref[...], coarse) + dot(left_ref[...], fine)
    for h in range(width // QUAD):
        sums_ref[h * width : (h + 1) * width, :] = grad_out[:, h * n : (h + 1) * n].astype(BF16)
    grad_left = dot(part_ref[...], coarse, RHS_T) + dot(part_ref[...], fine, RHS_T)
    sums_ref[256:288, :] = jnp.concatenate([grad_left, grad_right_ref[...]], axis=1).astype(BF16)


def join_kernel(own_ref, beside_ref, across_ref, both_ref, out_ref):
    def pair(a_ref, b_ref, lo, hi):
        return a_ref[lo:hi, :].astype(F32) + b_ref[lo:hi, :].astype(F32)

    out_ref[0:256, :] = pair(own_ref, beside_ref, 0, 256).astype(BF16)
    out_ref[256:512, :] = pair(across_ref, both_ref, 0, 256).astype(BF16)
    out_ref[512:608, :] = (
        pair(own_ref, beside_ref, 256, 352) + pair(across_ref, both_ref, 256, 352)
    ).astype(BF16)


def last_kernel(local_ref, other_ref, out_ref, gate_ref, left_ref, right_ref):
    row = lax.axis_index("row")
    quad_at = place_in_quad(row)
    n = local_ref.shape[1]
    wide = QUAD * n
    src = iota((wide, wide), 0)
    dst = iota((wide, wide), 1)
    chan = (quad_at ^ (src // n)) * CHANS + src % CHANS
    place = jnp.where(
        (dst // n == (src % n) // CHANS) & (dst % n == chan), 1.0, 0.0
    ).astype(BF16)
    packed = jnp.concatenate(
        [local_ref[0:256, :], other_ref[0:256, :], local_ref[256:512, :], other_ref[256:512, :]], axis=1
    )
    whole = dot(packed, place)
    for h in range(8):
        for el in range(4):
            out_ref[pl.ds(h * 4 + el, 32, stride=32), :] = whole[
                h * 32 : (h + 1) * 32, el * n : (el + 1) * n
            ]
    both = local_ref[512:544, :].astype(F32) + other_ref[512:544, :].astype(F32)
    left_ref[...] = both[:, 0:64]
    right_ref[...] = both[:, 64:128]
    halves = local_ref[544:608, :].astype(F32), other_ref[544:608, :].astype(F32)
    gate_ref[: n // 2, :] = jnp.where(row % 2 == 0, halves[0], halves[1])
    gate_ref[n // 2 :, :] = jnp.where(row % 2 == 0, halves[1], halves[0])


def tie_kernel(*refs):
    out_ref, at = refs[-1], 0
    for ref in refs:
        if at < out_ref.shape[0]:
            out_ref[at : at + ref.shape[0], :] = ref[...]
            at += ref.shape[0]


def call(kernel, shapes, scratch=(), smem=0, ins=0, flops=1 << 20, vmem=4):
    return pl.pallas_call(
        kernel,
        out_shape=[jax.ShapeDtypeStruct(s, d) for s, d in shapes],
        in_specs=[SMEM] * smem + [VMEM] * (ins - smem),
        out_specs=[VMEM] * len(shapes),
        scratch_shapes=[pltpu.VMEM(s, d) for s, d in scratch],
        compiler_params=pltpu.CompilerParams(vmem_limit_bytes=vmem << 20),
        cost_estimate=pl.CostEstimate(flops=flops, bytes_accessed=1 << 20, transcendentals=0),
    )


def swap(x, bit, size):
    return lax.ppermute(x, "row", [(i, i ^ bit) for i in range(size)])


def one_column(
    alignment_state, pair_state, cotangent, sequence_row_mask, residue_mask, norm_gain_vector,
    left_matrix_weight, right_matrix_weight, output_weight, output_bias, gate_matrix,
):
    size = lax.axis_size("row")
    rows, n, _ = pair_state.shape
    res = residue_mask.reshape(1, n)
    seq = sequence_row_mask.reshape(1, -1)
    state = alignment_state.transpose(0, 2, 1)
    near = swap(state, 8, size)
    (token,) = call(first_kernel, [((8, n), F32)], flops=20 << 30)()
    gain = norm_gain_vector.reshape(1, -1)
    bias = output_bias.reshape(1, n)
    scale, slope, turned, own, core, across, gain, bias = call(
        gate_kernel,
        [((rows, n, n), F32), ((rows, n, n), F32), ((rows * n, n), BF16)] + [((2 * n, n), BF16)] * 2
        + [((4 * n, n), BF16), (gain.shape, F32), (bias.shape, F32)],
        scratch=[((n, rows * n), BF16)], smem=1, ins=9, flops=1 << 30, vmem=12,
    )(residue_mask, seq, res, pair_state, cotangent, gate_matrix, gain, bias, token)
    pair, to_core, to_across = call(
        norm_kernel, [((2 * n, n), BF16), ((4 * n, n), BF16), ((6 * n, n), BF16)], smem=1, ins=7
    )(sequence_row_mask, res, gain, state, near, core, across)
    beside, ahead, corner = swap(pair, 2, size), swap(to_across, ACROSS, size), swap(pair, 2 ^ ACROSS, size)
    left_t = left_matrix_weight.T
    kron, block, wide, part = call(
        weight_kernel,
        [((1024, 512), BF16), ((256, n), BF16), ((32, 32 * n), BF16), ((32, 8 * n), BF16)],
        scratch=[((1024, n), F32)], ins=4, flops=1 << 30, vmem=12,
    )(right_matrix_weight.T, left_t, output_weight, pair)
    (beside,) = call(tie_kernel, [((2 * n, n), BF16)], ins=2)(beside, block)
    pair_core, beside_core, corner_core, ahead_core = (
        swap(y, 1, size) for y in (to_core, beside, corner, ahead)
    )
    scratch = [
        ((512, rows * n), BF16), ((2, n, n), F32), ((512, n), F32), ((64, 8 * n), BF16),
    ]
    shared = (turned, kron, block, wide)
    kept = [((512, n), BF16), ((n, 256), BF16)]
    linear, act, right0, own0 = call(
        half_kernel,
        [((n, rows * n), F32), ((64, n), F32), *kept],
        scratch=scratch, ins=9, flops=2 << 30, vmem=24,
    )(pair, pair_core, beside, beside_core, *shared, bias)
    value, keep, send, right_sum, right1, own1 = call(
        pair_kernel,
        [((rows, n, n), F32), ((n // 2, n), BF16), ((n // 2, n), BF16), ((32, 64), F32), *kept],
        scratch=[((rows * n, n), BF16), *scratch], ins=12, flops=2 << 30, vmem=24,
    )(corner, corner_core, ahead, ahead_core, *shared, linear, act, slope, pair_state)
    (sums,) = call(
        out_kernel, [((288, n), BF16)], scratch=[((256, 32 * n), BF16)], ins=11, flops=1 << 30, vmem=24,
    )(right0, right1, own0, own1, own, pair_core, ahead, ahead_core, part, left_t, right_sum)
    (sums,) = call(chip_kernel, [((352, n), BF16)], ins=3)(sums, keep, swap(send, 1, size))
    update, token = call(update_kernel, [((rows, n, n), BF16), ((8, n), F32)], ins=3, flops=1 << 30, vmem=8)(scale, value, sums)
    (sums,) = call(add_kernel, [((352, n), BF16)], ins=3)(sums, swap(sums, 8, size), token)
    others = [swap(sums, step, size) for step in (2, ACROSS, 2 ^ ACROSS)]
    (local,) = call(join_kernel, [((608, n), BF16)], ins=4)(sums, *others)
    other = swap(local, 1, size)
    grad_out, grad_gate, left, right = call(
        last_kernel,
        [((1024, n), F32), ((n, n), F32), ((32, 64), F32), ((32, 64), F32)],
        ins=2,
    )(local, other)
    return update, left.T, right.T, grad_out, grad_gate


def layer_normalize(alignment_state, norm_gain_vector):
    value_entries = alignment_state.astype(jnp.float32)
    average = jnp.mean(value_entries, axis=-1, keepdims=True)
    centred = value_entries - average
    variance = jnp.mean(centred * centred, axis=-1, keepdims=True)
    return (centred * lax.rsqrt(variance + 1e-05) * norm_gain_vector).astype(jnp.bfloat16)


def any_mesh(
    alignment_state,
    pair_state,
    cotangent,
    sequence_row_mask,
    residue_mask,
    norm_gain_vector,
    left_matrix_weight,
    right_matrix_weight,
    output_weight,
    output_bias,
    gate_matrix,
):
    sequence_resident, column_count, alignment_channel_count = alignment_state.shape
    count_of_rows = pair_state.shape[0]
    pair_chans = pair_state.shape[2]
    projection_width = left_matrix_weight.shape[1]
    every_sequence = sequence_row_mask.shape[0]
    row_at = lax.axis_index("row")
    col_at = lax.axis_index("col")
    number_of_rows = lax.axis_size("row")
    contract_first = (((0,), (0,)), ((), ()))
    contract_second = (((1,), (1,)), ((), ()))
    resident_features = layer_normalize(alignment_state, norm_gain_vector)
    seq_flags = sequence_row_mask.astype(jnp.float32)
    res_flags = residue_mask.astype(jnp.float32)
    my_cols = lax.dynamic_slice_in_dim(res_flags, col_at * column_count, column_count, 0)
    my_rows = lax.dynamic_slice_in_dim(res_flags, row_at * count_of_rows, count_of_rows, 0)
    panel_mask = seq_flags[:, None] * my_rows[None, :]
    column_mask = seq_flags[:, None] * my_cols[None, :]
    broadcast_features = lax.all_gather(
        resident_features.reshape(sequence_resident, column_count * alignment_channel_count),
        "col",
        axis=1,
        tiled=True,
    )
    row_portions = broadcast_features.reshape(
        sequence_resident, number_of_rows, count_of_rows * alignment_channel_count
    )
    row_feats = lax.all_to_all(
        row_portions, "row", split_axis=1, concat_axis=0, tiled=True
    ).reshape(every_sequence * count_of_rows, alignment_channel_count)
    left_panel = (
        jnp.dot(row_feats, left_matrix_weight, preferred_element_type=jnp.float32).reshape(
            every_sequence, count_of_rows, projection_width
        )
        * panel_mask[:, :, None]
    ).astype(jnp.bfloat16)
    left_matrix = left_panel.transpose(1, 2, 0).reshape(
        count_of_rows * projection_width, every_sequence
    )
    column_features = lax.all_gather(
        resident_features.reshape(sequence_resident, column_count * alignment_channel_count),
        "row",
        axis=0,
        tiled=True,
    ).reshape(every_sequence, column_count, alignment_channel_count)
    right_panel = (
        jnp.dot(
            column_features.reshape(every_sequence * column_count, alignment_channel_count),
            right_matrix_weight,
            preferred_element_type=jnp.float32,
        ).reshape(every_sequence, column_count, projection_width)
        * column_mask[:, :, None]
    ).astype(jnp.bfloat16)
    surplus_offset = jnp.zeros((alignment_channel_count, projection_width), jnp.float32)

    def absorb(extra, first_col, width_columns, right_part):
        feat_blk = (
            lax.dynamic_slice_in_dim(column_features, first_col, width_columns, 1)
            .reshape(every_sequence * width_columns, alignment_channel_count)
            .astype(jnp.float32)
        )
        mask_blk = lax.dynamic_slice_in_dim(column_mask, first_col, width_columns, 1)
        masked_part = (
            right_part.reshape(every_sequence, width_columns, projection_width)
            * mask_blk[:, :, None]
        ).reshape(every_sequence * width_columns, projection_width)
        return extra + jnp.dot(feat_blk.T, masked_part, precision=lax.Precision.HIGHEST)

    right_flat = right_panel.reshape(every_sequence, column_count * projection_width)
    row_total = jnp.sum(seq_flags)
    col_block = 128
    n_blocks = column_count // col_block

    def one_block(block_idx, carry):
        new_update, grad_out, grad_gate, left_acc, extra = carry
        first_col = block_idx * col_block
        right_blk = lax.dynamic_slice_in_dim(
            right_flat, first_col * projection_width, col_block * projection_width, 1
        )
        outer_prod = jnp.dot(left_matrix, right_blk, preferred_element_type=jnp.float32)
        outer_prod = outer_prod.reshape(
            count_of_rows, projection_width, col_block, projection_width
        ).transpose(0, 2, 1, 3)
        outer_prod = outer_prod.reshape(
            count_of_rows * col_block, projection_width * projection_width
        ).astype(jnp.bfloat16)
        linear = (
            jnp.dot(outer_prod, output_weight, preferred_element_type=jnp.float32) + output_bias
        )
        pair_blk = lax.dynamic_slice_in_dim(pair_state, first_col, col_block, 1).reshape(
            count_of_rows * col_block, pair_chans
        )
        gate_val = jax.nn.sigmoid(
            jnp.dot(pair_blk, gate_matrix, preferred_element_type=jnp.float32)
        )
        blk_flags = lax.dynamic_slice_in_dim(my_cols, first_col, col_block, 0)
        divisor = jnp.maximum(row_total * my_rows[:, None] * blk_flags[None, :], 1.0).reshape(
            count_of_rows * col_block, 1
        )
        cot_blk = (
            lax.dynamic_slice_in_dim(cotangent, first_col, col_block, 1)
            .reshape(count_of_rows * col_block, pair_chans)
            .astype(jnp.float32)
        )
        new_pair = (gate_val * linear / divisor).astype(jnp.bfloat16)
        new_update = lax.dynamic_update_slice_in_dim(
            new_update, new_pair.reshape(count_of_rows, col_block, pair_chans), first_col, 1
        )
        grad_lin = (cot_blk * gate_val / divisor).astype(jnp.bfloat16)
        grad_pre = (cot_blk * linear / divisor * gate_val * (1.0 - gate_val)).astype(jnp.bfloat16)
        grad_out = grad_out + lax.dot_general(
            outer_prod, grad_lin, contract_first, preferred_element_type=jnp.float32
        )
        grad_gate = grad_gate + lax.dot_general(
            pair_blk, grad_pre, contract_first, preferred_element_type=jnp.float32
        )
        grad_outer = lax.dot_general(
            grad_lin, output_weight, contract_second, preferred_element_type=jnp.float32
        ).astype(jnp.bfloat16)
        outer_turned = (
            grad_outer.reshape(count_of_rows, col_block, projection_width, projection_width)
            .transpose(0, 2, 1, 3)
            .reshape(count_of_rows * projection_width, col_block * projection_width)
        )
        left_acc = left_acc + lax.dot_general(
            outer_turned, right_blk, contract_second, preferred_element_type=jnp.float32
        )
        right_part = lax.dot_general(
            left_matrix, outer_turned, contract_first, preferred_element_type=jnp.float32
        )
        extra = absorb(extra, first_col, col_block, right_part)
        return (new_update, grad_out, grad_gate, left_acc, extra)

    start_carry = (
        jnp.zeros((count_of_rows, column_count, pair_chans), jnp.bfloat16),
        jnp.zeros((projection_width * projection_width, pair_chans), jnp.float32),
        jnp.zeros((pair_chans, pair_chans), jnp.float32),
        jnp.zeros((count_of_rows * projection_width, every_sequence), jnp.float32),
        surplus_offset,
    )
    new_update, grad_out, grad_gate, left_acc, extra = lax.fori_loop(
        0, n_blocks, one_block, start_carry
    )
    grad_left_act = (
        left_acc.reshape(count_of_rows, projection_width, every_sequence).transpose(2, 0, 1)
        * panel_mask[:, :, None]
    )
    grad_left = jnp.dot(
        row_feats.astype(jnp.float32).T,
        grad_left_act.reshape(every_sequence * count_of_rows, projection_width),
        precision=lax.Precision.HIGHEST,
    )
    summed_left, summed_right, summed_out, summed_gate = lax.psum(
        (grad_left, extra, grad_out, grad_gate), ("row", "col")
    )
    return (new_update, summed_left, summed_right, summed_out, summed_gate)


def per_device(*args):
    alignment_state, pair_state = args[0], args[1]
    fits = (
        lax.axis_size("col") == 1
        and lax.axis_size("row") == 16
        and alignment_state.shape == (2, 128, 64)
        and pair_state.shape == (8, 128, 128)
    )
    return one_column(*args) if fits else any_mesh(*args)


def solution(mesh):
    return jax.shard_map(
        per_device,
        mesh=mesh,
        in_specs=(
            P(("grp", "row"), "col", None),
            P(("grp", "row"), "col", None),
            P(("grp", "row"), "col", None),
            P("grp"),
            P("grp"),
            P(),
            P(),
            P(),
            P(),
            P(),
            P(),
        ),
        out_specs=(
            P(("grp", "row"), "col", None),
            P("grp", None),
            P("grp", None),
            P("grp", None),
            P("grp", None),
        ),
        check_vma=False,
    )
```
